128 devices in a mesh: lat: 32 (over y, x_lo, z), lon: 4 (over x_hi, core).
Axes of the slice: x: 4 (x_hi: 2, x_lo: 2; x = x_hi * 2 + x_lo), y: 4, z: 4, core: 2. Of those that a mesh axis runs over, the one named last changes fastest.
Arguments:
- obs_feat: bfloat16 [262144, 128], P(('lat', 'lon')), may hold values from -6 to 6
- obs_dest: int32 [262144, 1], P(('lat', 'lon')), may hold values from 0 to 127; in each aligned block of 2048 rows (0 to 2047, 2048 to 4095, ...) at most 32 rows name the same one
- obs_cell: int32 [262144], P(('lat', 'lon')), may hold values from 0 to 3071
- obs_sub: int32 [262144], P(('lat', 'lon')), may hold values from 0 to 255
- background: bfloat16 [768, 512, 512], P('lat', 'lon'), may hold values from -6 to 6
- w_in: bfloat16 [128, 512], replicated, may hold values from -0.5 to 0.5
- dens_vec: float32 [512], replicated, may hold values from -6 to 6
- conv_w: bfloat16 [4, 4, 512, 512], replicated, may hold values from -0.0625 to 0.0625
- conv_b: float32 [512], replicated, may hold values from -3 to 3
- norm_gain: float32 [512], replicated, may hold values from 0.1 to 1.9
- w_qkv: bfloat16 [512, 1536], replicated, may hold values from -0.25 to 0.25
- rel_bias: float32 [8, 13, 13], replicated, may hold values from -6 to 266
- w_out: bfloat16 [512, 512], replicated, may hold values from -0.25 to 0.25
Outputs:
- encoded: bfloat16 [384, 256, 512], P('lat', 'lon')
The draws below stay inside these ranges and needn't reach their ends.
Inputs may be any that keep to these rules, and one draw needn't show every extreme that they name: `obs_dest`: destination device of each observation, numbered lat index * 4 + lon index; the rows of one device name one destination at most 32 times, and 32 is reached. `obs_cell`: row-major cell inside the destination tile. `obs_sub`: 16 * sub-row + sub-column inside the cell.
All inputs are finite; a program needn't handle non-finite values.
Results may differ from the reference program's by a relative error of at most 0.012.
Values may be sent and summed in bfloat16 or wider, within the bound.
A program may use at most 128 MiB of HBM per device.

```python
import math
import jax
import jax.numpy as jnp
import numpy as np
from jax import lax

C = 512
OF = 128
HEADS = 8
SPAN = 13
LR = 24
LC = 128
OBS_DEV = 2048
CAP = 32
OBS = 262144
CR = 12
CC = 64
LATG = 768
LONG = 512
LATC = 384
LONC = 256
N_LAT = 32
N_LON = 4
DEVICES = 128


def draw_rel_bias(key, part):
    key = jax.random.fold_in(key, 7)
    base_key = jax.random.fold_in(key, 0)
    table = jnp.clip(jax.random.normal(base_key, (HEADS, SPAN * SPAN), jnp.float32), -6.0, 6.0)
    return table.reshape(HEADS, SPAN, SPAN)


def touch_ends(result, key, smallest, high):
    extent = result.shape
    spot = [jax.random.randint(jax.random.fold_in(key, axis), (), 0, extent[axis]) for axis in range(len(extent))]
    result = result.at[tuple(spot)].set(smallest)
    longest = extent.index(max(extent))
    spot[longest] = (spot[longest] + 1) % extent[longest]
    return result.at[tuple(spot)].set(high)


def level_of(own_key, dims, shards, low, top_value):
    gain = 1.0
    for position, blocks in shards:
        steps = jax.random.uniform(jax.random.fold_in(jax.random.fold_in(own_key, 6), position), (blocks,), jnp.float32, low / len(shards), top_value / len(shards))
        gain = gain * jnp.repeat(jnp.exp(steps), dims[position] // blocks).reshape((-1,) + (1,) * (len(dims) - 1 - position))
    return gain


def assign_block(own_key, own, number, rows, count, top, most, slope):
    order = jax.random.permutation(own_key, count)
    heavy_load, common = portions_of(count, rows * top, most, slope, True), portions_of(count, rows * top, most, slope, False)
    places = jnp.arange(count)

    def named(tallies, rotation):
        used = int((tallies > 0).sum())
        fixed = max(1, used // 4)
        passed = fixed + (places - fixed + rotation * (used - fixed)) % max(1, count - fixed)
        return jnp.zeros((count,), jnp.int32).at[order[jnp.where(places < fixed, places, passed)]].set(jnp.asarray(tallies, jnp.int32))

    tallies = jnp.where(number % 4 == 0, named(heavy_load, number // 4), named(common, number - number // 4 - 1))
    mixed = jax.random.permutation(jax.random.fold_in(own, 3), count)
    giver, sink = mixed[0:count // 2 * 2:2], mixed[1:count // 2 * 2:2]
    slack = jnp.minimum(tallies[giver] - 1, most - tallies[sink]) // 2
    slack = jnp.where((giver == order[0]) | (sink == order[0]) | (tallies[sink] == 0), 0, jnp.maximum(slack, 0))
    passed = jax.random.randint(jax.random.fold_in(own, 4), (count // 2,), 0, 1 << 20) % (slack + 1)
    tallies = tallies.at[giver].add(-passed).at[sink].add(passed)
    members = jnp.searchsorted(jnp.cumsum(tallies), jnp.arange(rows * top), side="right").astype(jnp.int32)
    listing = members.reshape(top, rows).T
    listing = listing[jax.random.permutation(jax.random.fold_in(own, 1), rows)]
    rotation = jax.random.randint(jax.random.fold_in(own, 2), (rows, 1), 0, top)
    return jnp.take_along_axis(listing, (jnp.arange(top)[None, :] + rotation) % top, axis=1)


def portions_of(amount, total, bound, lean, full):
    weights = [(1 << 20) // math.isqrt(grade ** lean) + 1 for grade in range(1, amount + 1)]
    largest = bound if full else min(bound, max(-(-total // amount), total * weights[0] // sum(weights)))
    least = 1 if total - largest >= amount - 1 else 0
    counts, rest = [largest] + [least] * (amount - 1), total - largest - least * (amount - 1)
    while rest > 0:
        free = [i for i in range(1, amount) if counts[i] < largest] or [i for i in range(1, amount) if counts[i] < bound]
        pool, budget = sum([weights[i] for i in free]), rest
        for i in free:
            more = min(bound - counts[i], max(1, budget * weights[i] // pool), rest)
            counts[i] = counts[i] + more
            rest = rest - more
    return np.array(counts)


def scatter_about(key, shape, deviation, most, cuts=(), kind=jnp.bfloat16):
    values = deviation * jax.random.normal(key, shape, jnp.float32)
    if cuts:
        values = values * level_of(key, shape, cuts, -0.22, 0.18)
    return jnp.clip(values, -most, most).astype(kind)


def setup_inputs(seed: int = 0) -> dict:
    seeds = jax.random.split(jax.random.key(seed), 14)
    obs_feat = scatter_about(seeds[0], (OBS, OF), 1.0, 6.0, ((0, 128),))
    obs_dest_keys = jax.random.split(jax.random.fold_in(seeds[1], 1), OBS // OBS_DEV)
    obs_dest_turns = jax.random.permutation(jax.random.fold_in(seeds[1], 3), OBS // OBS_DEV)
    obs_dest = jax.vmap(lambda own, number: assign_block(jax.random.fold_in(seeds[1], 2), own, number, OBS_DEV, DEVICES, 1, CAP, 2))(obs_dest_keys, obs_dest_turns).reshape((OBS, 1))
    obs_cell = touch_ends(jax.random.randint(seeds[2], (OBS,), 0, LR * LC), jax.random.fold_in(seeds[2], 1), 0, (LR * LC) - 1).astype(jnp.int32)
    obs_sub = touch_ends(jax.random.randint(seeds[3], (OBS,), 0, 256), jax.random.fold_in(seeds[3], 1), 0, 255).astype(jnp.int32)
    background = scatter_about(seeds[4], (LATG, LONG, C), 1.0, 6.0, ((0, 32), (1, 4)))
    w_in = scatter_about(seeds[5], (OF, C), OF ** -0.5, 0.5)
    dens_vec = scatter_about(seeds[6], (C,), 1.0, 6.0, (), jnp.float32)
    conv_w = scatter_about(seeds[7], (4, 4, C, C), (16 * C) ** -0.5, 0.0625)
    conv_b = scatter_about(seeds[8], (C,), 0.5, 3.0, (), jnp.float32)
    norm_gain = jnp.clip(1.0 + 0.18 * jax.random.normal(seeds[9], (C,), jnp.float32), 0.1, 1.9)
    w_qkv = scatter_about(seeds[10], (C, 3 * C), C ** -0.5, 0.25)
    rel_bias = draw_rel_bias(jax.random.fold_in(seeds[13], 71), 0)
    w_out = scatter_about(seeds[12], (C, C), C ** -0.5, 0.25)
    return dict(obs_feat=obs_feat, obs_dest=obs_dest, obs_cell=obs_cell, obs_sub=obs_sub, background=background, w_in=w_in, dens_vec=dens_vec, conv_w=conv_w, conv_b=conv_b, norm_gain=norm_gain, w_qkv=w_qkv, rel_bias=rel_bias, w_out=w_out)


def kernel_weight(code):
    row_off = (code // 16).astype(jnp.float32)
    col_off = (code % 16).astype(jnp.float32)
    delta_row = (row_off + 0.5) / 16.0 - 0.5
    delta_col = (col_off + 0.5) / 16.0 - 0.5
    return jnp.exp(-(delta_row * delta_row + delta_col * delta_col) / (2.0 * 0.35 * 0.35))

def strided_conv(padded, conv_w, out_rows, out_cols):
    channels = padded.shape[2]
    total = jnp.zeros((out_rows * out_cols, conv_w.shape[3]), jnp.float32)
    for row_tap in range(4):
        for col_tap in range(4):
            window = padded[row_tap:row_tap + 2 * out_rows:2, col_tap:col_tap + 2 * out_cols:2, :]
            total = total + jnp.dot(window.reshape(out_rows * out_cols, channels), conv_w[row_tap, col_tap], preferred_element_type=jnp.float32)
    return total

def attend(query_block, key_block, value_block, row_valid, rel_bias, head_count):
    query_rows, query_cols, channels = query_block.shape
    key_rows, key_cols = (key_block.shape[0], key_block.shape[1])
    window_span = rel_bias.shape[1]
    head_size = channels // head_count
    row_gap = jnp.arange(key_rows, dtype=jnp.int32)[None, :] - jnp.arange(query_rows, dtype=jnp.int32)[:, None]
    col_gap = jnp.arange(key_cols, dtype=jnp.int32)[None, :] - jnp.arange(query_cols, dtype=jnp.int32)[:, None]
    tap_index = jnp.arange(window_span, dtype=jnp.int32)
    row_pick = (row_gap[:, :, None] == tap_index).astype(jnp.float32)
    col_pick = (col_gap[:, :, None] == tap_index).astype(jnp.float32)
    partial_bias = jnp.einsum('ira,hab->hirb', row_pick, rel_bias, precision=lax.Precision.HIGHEST)
    bias_table = jnp.einsum('hirb,jcb->hijrc', partial_bias, col_pick, precision=lax.Precision.HIGHEST)
    row_inside = (row_gap >= 0) & (row_gap < window_span) & row_valid[None, :]
    col_inside = (col_gap >= 0) & (col_gap < window_span)
    in_window = row_inside[:, None, :, None] & col_inside[None, :, None, :]
    total_queries = query_rows * query_cols
    total_keys = key_rows * key_cols
    query_heads = query_block.reshape(total_queries, head_count, head_size).astype(jnp.float32)
    key_heads = key_block.reshape(total_keys, head_count, head_size).astype(jnp.float32)
    value_heads = value_block.reshape(total_keys, head_count, head_size).astype(jnp.float32)
    scores = jnp.einsum('qhd,khd->hqk', query_heads, key_heads) * head_size ** (-0.5)
    scores = scores + bias_table.reshape(head_count, total_queries, total_keys)
    scores = jnp.where(in_window.reshape(1, total_queries, total_keys), scores, -1e+30)
    row_peak = lax.optimization_barrier(jnp.max(scores, axis=2, keepdims=True))
    exponent = jnp.exp(scores - row_peak)
    weights = (exponent / lax.optimization_barrier(jnp.sum(exponent, axis=2, keepdims=True))).astype(jnp.bfloat16)
    blended = jnp.einsum('hqk,khd->qhd', weights.astype(jnp.float32), value_heads)
    return blended.astype(jnp.bfloat16).reshape(total_queries, channels)

def reference(obs_feat, obs_dest, obs_cell, obs_sub, background, w_in, dens_vec, conv_w, conv_b, norm_gain, w_qkv, rel_bias, w_out):
    target = obs_dest[:, 0]
    grid_row = target // N_LON * LR + obs_cell // LC
    grid_col = target % N_LON * LC + obs_cell % LC
    flat_cell = (grid_row * LONG + grid_col).astype(jnp.int32)
    kernel = kernel_weight(obs_sub)
    summed = jax.ops.segment_sum(obs_feat.astype(jnp.float32) * kernel[:, None], flat_cell, num_segments=LATG * LONG)
    density = jax.ops.segment_sum(kernel, flat_cell, num_segments=LATG * LONG)
    normed_obs = (summed / (density[:, None] + 1.0)).astype(jnp.bfloat16)
    lifted = jnp.dot(normed_obs, w_in, preferred_element_type=jnp.float32)
    gridded = background.reshape(LATG * LONG, C).astype(jnp.float32) + lifted + density[:, None] * dens_vec[None, :]
    gridded = gridded.astype(jnp.bfloat16).reshape(LATG, LONG, C)
    wrapped = jnp.concatenate([gridded[:, -1:], gridded, gridded[:, :1]], axis=1)
    padded = jnp.pad(wrapped, ((1, 1), (0, 0), (0, 0)))
    conv_sum = strided_conv(padded, conv_w, LATC, LONC) + conv_b[None, :]
    coarse = jax.nn.gelu(conv_sum, approximate=True).astype(jnp.bfloat16)
    coarse_f = coarse.astype(jnp.float32)
    inv_scale = lax.rsqrt(lax.optimization_barrier(jnp.mean(coarse_f * coarse_f, axis=1, keepdims=True)) + 1e-05)
    normed = (coarse_f * inv_scale * norm_gain[None, :]).astype(jnp.bfloat16)
    projected = jnp.dot(normed, w_qkv, preferred_element_type=jnp.float32).astype(jnp.bfloat16)
    query_grid = projected[:, :C].reshape(LATC, LONC, C)
    key_value = projected[:, C:].reshape(LATC, LONC, 2 * C)
    reach = SPAN // 2
    key_value = jnp.concatenate([key_value[:, -reach:], key_value, key_value[:, :reach]], axis=1)
    key_value = jnp.pad(key_value, ((reach, reach), (0, 0), (0, 0)))

    def one_tile(index):
        lat_at = (index // N_LON).astype(jnp.int32)
        lon_at = (index % N_LON).astype(jnp.int32)
        zero = jnp.zeros((), jnp.int32)
        query_block = lax.dynamic_slice(query_grid, ((lat_at * CR).astype(jnp.int32), (lon_at * CC).astype(jnp.int32), zero), (CR, CC, C))
        pair_block = lax.dynamic_slice(key_value, ((lat_at * CR).astype(jnp.int32), (lon_at * CC).astype(jnp.int32), zero), (CR + 2 * reach, CC + 2 * reach, 2 * C))
        global_rows = lat_at * CR + jnp.arange(CR + 2 * reach, dtype=jnp.int32) - reach
        row_valid = (global_rows >= 0) & (global_rows < LATC)
        return attend(query_block, pair_block[:, :, :C], pair_block[:, :, C:], row_valid, rel_bias, HEADS).reshape(CR, CC, C)
    tiles = lax.map(one_tile, jnp.arange(N_LAT * N_LON, dtype=jnp.int32))
    attended = tiles.reshape(N_LAT, N_LON, CR, CC, C).transpose(0, 2, 1, 3, 4).reshape(LATC * LONC, C)
    encoded = coarse_f + jnp.dot(attended, w_out, preferred_element_type=jnp.float32)
    return encoded.astype(jnp.bfloat16).reshape(LATC, LONC, C)
```

```python
import functools

import jax
import jax.numpy as jnp
from jax import lax
from jax.experimental import pallas as pl
from jax.experimental.pallas import tpu as pltpu
from jax.sharding import PartitionSpec as P

HEADS = 8
F32 = jnp.float32
BF16 = jnp.bfloat16
I32 = jnp.int32
NEG = -1e30


def iota(shape, dim):
    return lax.broadcasted_iota(I32, shape, dim)


def pack_kernel(dest_ref, cell_ref, sub_ref, feat_ref, sendf_ref, sendm_ref, pos_ref, wide_ref):
    obs, width = feat_ref.shape
    owners = sendf_ref.shape[0] // 32
    step = 256
    upper = (iota((step, step), 0) < iota((step, step), 1)).astype(F32).astype(BF16)
    running = jnp.zeros((owners, 1), F32)
    for at in range(0, obs, step):
        dest = dest_ref[:, at : at + step]
        member = (iota((owners, step), 0) == dest).astype(F32)
        earlier = jnp.dot(member.astype(BF16), upper, preferred_element_type=F32) + running
        rank = jnp.sum(member * earlier, axis=0, keepdims=True)
        running = running + jnp.sum(member, axis=1, keepdims=True)
        pos_ref[:, at : at + step] = dest * 32 + rank.astype(I32)
        cell = cell_ref[:, at : at + step]
        sub = sub_ref[:, at : at + step]
        line = iota((width, step), 0)
        meta = jnp.where(
            line == 0,
            ((cell >> 7) + 1).astype(F32),
            jnp.where(
                line == 1,
                (cell & 127).astype(F32),
                jnp.where(line == 2, sub.astype(F32), 0.0),
            ),
        )
        wide_ref[at : at + step, width:] = meta.T.astype(BF16)
        wide_ref[at : at + step, :width] = feat_ref[at : at + step, :]

    @pl.loop(0, owners * 32 // step)
    def _(tile):
        local = pos_ref[...] - tile * step
        local = jnp.where((local >= 0) & (local < step), local, -1).astype(F32).astype(BF16)
        slot = iota((step, obs), 0).astype(F32).astype(BF16)
        pick = jnp.where(slot == local, jnp.ones((), BF16), jnp.zeros((), BF16))
        packed = jnp.dot(pick, wide_ref[...], preferred_element_type=F32)
        at = pl.multiple_of(tile * step, step)
        sendf_ref[pl.ds(at, step), :] = packed[:, :width].astype(BF16)
        meta = packed[:, width:].T
        code = (meta[0:1] * 128.0 + meta[1:2]).astype(I32) * 256 + meta[2:3].astype(I32)
        sendm_ref[:, pl.ds(at, step)] = code


def pack_call(dest, cell, sub, feat, owners):
    obs, width = feat.shape
    return pl.pallas_call(
        pack_kernel,
        name="pack",
        out_shape=(
            jax.ShapeDtypeStruct((owners * 32, width), BF16),
            jax.ShapeDtypeStruct((1, owners * 32), I32),
        ),
        scratch_shapes=[pltpu.VMEM((1, obs), I32), pltpu.VMEM((obs, 2 * width), BF16)],
        compiler_params=pltpu.CompilerParams(vmem_limit_bytes=48 << 20),
    )(dest, cell, sub, feat)


def grid_kernel(
    feat_ref, code_ref, back_ref, win_ref, dens_ref, grid_ref, wide_ref, cell_ref, kern_ref
):
    slots, width = feat_ref.shape
    cells = back_ref.shape[0]
    step = 256
    code = code_ref[...]
    sub = code & 255
    cell_ref[...] = (code >> 8) - 128
    row = ((sub >> 4).astype(F32) + 0.5) / 16.0 - 0.5
    col = ((sub & 15).astype(F32) + 0.5) / 16.0 - 0.5
    kern_ref[...] = jnp.exp(-(row * row + col * col) / (2.0 * 0.35 * 0.35))
    wide_ref[:, :width] = feat_ref[...]
    wide_ref[:, width:] = jnp.ones((slots, width), BF16)

    @pl.loop(0, cells // step)
    def _(tile):
        local = cell_ref[...] - tile * step
        local = jnp.where((local >= 0) & (local < step), local, -1).astype(F32).astype(BF16)
        kern = kern_ref[...].astype(BF16)
        line = iota((step, slots), 0).astype(F32).astype(BF16)
        pick = jnp.where(line == local, kern, jnp.zeros((), BF16))
        total = jnp.dot(pick, wide_ref[...], preferred_element_type=F32)
        density = total[:, width : width + 1]
        normed = (total[:, :width] / (density + 1.0)).astype(BF16)
        at = pl.multiple_of(tile * step, step)
        lifted = jnp.dot(normed, win_ref[...], preferred_element_type=F32)
        value = back_ref[pl.ds(at, step), :].astype(F32) + lifted + density * dens_ref[...]
        grid_ref[pl.ds(at, step), :] = value.astype(BF16)


def grid_call(feat, code, back, w_in, dens_vec):
    slots, width = feat.shape
    return pl.pallas_call(
        grid_kernel,
        name="grid",
        out_shape=jax.ShapeDtypeStruct(back.shape, BF16),
        scratch_shapes=[
            pltpu.VMEM((slots, 2 * width), BF16),
            pltpu.VMEM((1, slots), I32),
            pltpu.VMEM((1, slots), F32),
        ],
        compiler_params=pltpu.CompilerParams(vmem_limit_bytes=48 << 20),
    )(feat, code, back, w_in, dens_vec)


def conv_kernel(
    grid_ref, left_ref, right_ref, top_ref, bottom_ref, w_ref, b_ref, gain_ref,
    coarse_ref, normed_ref, line_ref, taps_ref, side_ref,
):
    rows, cols, channels = grid_ref.shape
    side_ref[0] = left_ref[...].astype(F32)
    side_ref[1] = right_ref[...].astype(F32)
    half = cols // 2

    def lay(at, line, left, right):
        for c in range(channels // 128):
            lanes = slice(c * 128, (c + 1) * 128)
            line_ref[c, 8 : 8 + cols, :] = line[:, lanes].astype(F32)
            line_ref[c, 7:8, :] = left[:, lanes].astype(F32)
            line_ref[c, 8 + cols : 9 + cols, :] = right[:, lanes].astype(F32)
            for tap in range(4):
                part = line_ref[c, pl.ds(7 + tap, half, stride=2), :]
                base = tap * channels + c * 128
                taps_ref[at, :, base : base + 128] = part.astype(BF16)

    lay(0, top_ref[:cols, :], top_ref[cols : cols + 1, :], top_ref[cols + 1 : cols + 2, :])
    lay(
        rows + 1,
        bottom_ref[:cols, :],
        bottom_ref[cols : cols + 1, :],
        bottom_ref[cols + 1 : cols + 2, :],
    )

    @pl.loop(0, rows)
    def _(row):
        lay(row + 1, grid_ref[row], side_ref[0, pl.ds(row, 1), :], side_ref[1, pl.ds(row, 1), :])

    @pl.loop(0, rows // 8)
    def _(part):
        total = jnp.zeros((4 * half, channels), F32)
        for tap in range(4):
            window = jnp.concatenate(
                [taps_ref[part * 8 + 2 * i + tap] for i in range(4)], axis=0
            )
            total = total + jnp.dot(window, w_ref[tap], preferred_element_type=F32)
        total = total + b_ref[...]
        inner = 0.7978845608028654 * (total + 0.044715 * total * total * total)
        coarse = (0.5 * total * (1.0 + jnp.tanh(inner))).astype(BF16)
        at = pl.multiple_of(part * 4 * half, 4 * half)
        coarse_ref[pl.ds(at, 4 * half), :] = coarse
        value = coarse.astype(F32)
        scale = lax.rsqrt(jnp.mean(value * value, axis=1, keepdims=True) + 1e-05)
        normed_ref[pl.ds(at, 4 * half), :] = (value * scale * gain_ref[...]).astype(BF16)


def conv_call(grid, left, right, top, bottom, conv_w, conv_b, norm_gain):
    rows, cols, channels = grid.shape
    out = jax.ShapeDtypeStruct((rows // 2 * cols // 2, channels), BF16)
    return pl.pallas_call(
        conv_kernel,
        name="conv",
        out_shape=(out, out),
        scratch_shapes=[
            pltpu.VMEM((channels // 128, cols + 16, 128), F32),
            pltpu.VMEM((rows + 2, cols // 2, 4 * channels), BF16),
            pltpu.VMEM((2, rows, channels), F32),
        ],
        compiler_params=pltpu.CompilerParams(vmem_limit_bytes=56 << 20),
    )(grid, left, right, top, bottom, conv_w, conv_b, norm_gain)


def attend_kernel(
    normed_ref, ext_ref, wqkv_ref, strip_ref, wout_ref, coarse_ref, out_ref,
    query_ref, key_ref, value_ref, bias_ref,
):
    key_rows, key_cols, channels = ext_ref.shape
    rows, cols = key_rows - 12, key_cols - 16
    half = channels // 2
    head = channels // HEADS
    lat, lat_count = lax.axis_index("lat"), lax.axis_size("lat")
    query_ref[...] = (
        jnp.dot(normed_ref[...], wqkv_ref[:, :channels], preferred_element_type=F32)
        .astype(BF16)
        .reshape(rows, cols, channels)
    )

    @pl.loop(0, key_rows // 4)
    def _(part):
        ext = ext_ref[pl.ds(part * 4, 4)].reshape(4 * key_cols, channels)
        both = jnp.dot(ext, wqkv_ref[:, channels:], preferred_element_type=F32).astype(BF16)
        key_ref[pl.ds(part * 4, 4)] = both[:, :channels].reshape(4, key_cols, channels)
        value_ref[pl.ds(part * 4, 4)] = both[:, channels:].reshape(4, key_cols, channels)

    for h in range(HEADS):
        strip = jnp.broadcast_to(strip_ref[h : h + 1, :], (16, 512))
        for r in range(4):
            at = h * 64 + r * 16
            bias_ref[at : at + 16, :] = pltpu.roll(
                strip, 2 + 32 * r, 1, stride=1, stride_axis=0
            )

    lane_head = iota((64, half), 1) // head

    @pl.loop(0, rows // 4)
    def _(down):
        first = lat * rows - 6 + down * 4
        key_row = first + iota((1, 512), 1) // 32
        edge = jnp.where((key_row >= 0) & (key_row < lat_count * rows), 0.0, NEG)

        @pl.loop(0, cols // 16)
        def _(across):
            c0 = pl.multiple_of(across * 16, 16)
            query = query_ref[pl.ds(down * 4, 4), pl.ds(c0, 16), :].reshape(64, channels)
            query = query * 0.125
            parts = []
            for g in range(2):
                lanes = slice(g * half, (g + 1) * half)
                keys = key_ref[pl.ds(down * 4, 16), pl.ds(c0, 32), lanes].reshape(512, half)
                values = value_ref[pl.ds(down * 4, 16), pl.ds(c0, 32), lanes].reshape(512, half)
                wide = query[:, lanes]
                masked = jnp.concatenate(
                    [jnp.where(lane_head == h, wide, jnp.zeros((), BF16)) for h in range(4)],
                    axis=0,
                )
                scores = lax.dot_general(
                    masked, keys, (((1,), (1,)), ((), ())), preferred_element_type=F32
                )
                scores = scores + bias_ref[g * 256 : (g + 1) * 256, :] + edge
                peak = jnp.max(scores, axis=1, keepdims=True)
                weight = jnp.exp(scores - peak)
                norm = jnp.sum(weight, axis=1, keepdims=True)
                mixed = jnp.dot(weight.astype(BF16), values, preferred_element_type=F32) / norm
                total = jnp.zeros((64, half), F32)
                for h in range(4):
                    total = jnp.where(lane_head == h, mixed[h * 64 : (h + 1) * 64], total)
                parts.append(total.astype(BF16))
            attended = jnp.concatenate(parts, axis=1)
            lifted = jnp.dot(attended, wout_ref[...], preferred_element_type=F32)
            base = coarse_ref[pl.ds(down * 4, 4), pl.ds(c0, 16), :].astype(F32)
            result = base + lifted.reshape(4, 16, channels)
            out_ref[pl.ds(down * 4, 4), pl.ds(c0, 16), :] = result.astype(BF16)


def attend_call(normed, ext, w_qkv, strip, w_out, coarse):
    key_rows, key_cols, channels = ext.shape
    rows, cols = key_rows - 12, key_cols - 16
    return pl.pallas_call(
        attend_kernel,
        name="attend",
        out_shape=jax.ShapeDtypeStruct((rows, cols, channels), BF16),
        scratch_shapes=[
            pltpu.VMEM((rows, cols, channels), BF16),
            pltpu.VMEM((key_rows, key_cols, channels), BF16),
            pltpu.VMEM((key_rows, key_cols, channels), BF16),
            pltpu.VMEM((512, 512), F32),
        ],
        compiler_params=pltpu.CompilerParams(vmem_limit_bytes=48 << 20),
    )(normed, ext, w_qkv, strip, w_out, coarse)


def moved(x, axis, step, wrap):
    size = lax.axis_size(axis)
    pairs = [(i, i + step) for i in range(size) if 0 <= i + step < size]
    if wrap:
        pairs = [(i, (i + step) % size) for i in range(size)]
    return lax.ppermute(x, axis, pairs)


def body(
    obs_feat, obs_dest, obs_cell, obs_sub, background, w_in, dens_vec,
    conv_w, conv_b, norm_gain, w_qkv, rel_bias, w_out,
):
    owners = lax.axis_size("lat") * lax.axis_size("lon")
    rows, cols, channels = background.shape
    obs, width = obs_feat.shape
    sendf, sendm = pack_call(
        obs_dest.reshape(1, obs), obs_cell.reshape(1, obs), obs_sub.reshape(1, obs), obs_feat, owners
    )
    both = ("lat", "lon")
    recvf = lax.all_to_all(sendf.reshape(owners, 32, width), both, 0, 0, tiled=True)
    recvm = lax.all_to_all(sendm.reshape(owners, 32), both, 0, 0, tiled=True)
    grid = grid_call(
        recvf.reshape(owners * 32, width),
        recvm.reshape(1, owners * 32),
        background.reshape(rows * cols, channels),
        w_in,
        dens_vec.reshape(1, channels),
    ).reshape(rows, cols, channels)
    left = moved(grid[:, cols - 1, :], "lon", 1, True)
    right = moved(grid[:, 0, :], "lon", -1, True)
    pad = jnp.zeros((14, channels), BF16)
    top = moved(jnp.concatenate([grid[-1], left[-1:], right[-1:], pad]), "lat", 1, False)
    bottom = moved(jnp.concatenate([grid[0], left[:1], right[:1], pad]), "lat", -1, False)
    coarse, normed = conv_call(
        grid, left, right, top, bottom,
        conv_w.reshape(4, 4 * channels, channels),
        conv_b.reshape(1, channels),
        norm_gain.reshape(1, channels),
    )
    normed3 = normed.reshape(rows // 2, cols // 2, channels)
    before = moved(normed3[:, -8:], "lon", 1, True)
    after = moved(normed3[:, :8], "lon", -1, True)
    ext = jnp.concatenate([before, normed3, after], axis=1)
    over = moved(ext[-6:], "lat", 1, False)
    under = moved(ext[:6], "lat", -1, False)
    ext = jnp.concatenate([over, ext, under], axis=0)
    strip = jnp.pad(rel_bias, ((0, 0), (0, 3), (0, 19)), constant_values=NEG).reshape(HEADS, 512)
    return attend_call(
        normed, ext, w_qkv, strip, w_out, coarse.reshape(rows // 2, cols // 2, channels)
    )


def solution(mesh):
    split = P(("lat", "lon"))
    wide = P(("lat", "lon"), None)
    tile = P("lat", "lon", None)
    in_specs = (wide, wide, split, split, tile) + (P(),) * 8
    return jax.shard_map(body, mesh=mesh, in_specs=in_specs, out_specs=tile, check_vma=False)
```

```python
import functools

import jax
import jax.numpy as jnp
from jax import lax
from jax.experimental import pallas as pl
from jax.experimental.pallas import tpu as pltpu
from jax.sharding import PartitionSpec as P

HEADS = 8
F32 = jnp.float32
BF16 = jnp.bfloat16
I32 = jnp.int32
NEG = -1e30
MESH = pl.DeviceIdType.MESH


def iota(shape, dim):
    return lax.broadcasted_iota(I32, shape, dim)


def route_kernel(
    dest_ref, cell_ref, sub_ref, feat_ref, recvf_ref, recvm_ref,
    pos_ref, wide_ref, sendf_ref, sendm_ref, send_sem, recv_sem, own_sem,
):
    obs, width = feat_ref.shape
    owners = sendf_ref.shape[0]
    step = 256
    lon_count = lax.axis_size("lon")
    lon = lax.axis_index("lon")
    me = lax.axis_index("lat") * lon_count + lon

    barrier = pltpu.get_barrier_semaphore()

    @pl.loop(1, owners)
    def _(k):
        peer = lax.rem(me + k, owners)
        pl.semaphore_signal(
            barrier, inc=1, device_id=(peer // lon_count, lax.rem(peer, lon_count)), device_id_type=MESH
        )

    upper = (iota((step, step), 0) < iota((step, step), 1)).astype(F32).astype(BF16)
    running = jnp.zeros((owners, 1), F32)
    for at in range(0, obs, step):
        dest = dest_ref[:, at : at + step]
        member = (iota((owners, step), 0) == dest).astype(F32)
        earlier = jnp.dot(member.astype(BF16), upper, preferred_element_type=F32) + running
        rank = jnp.sum(member * earlier, axis=0, keepdims=True)
        running = running + jnp.sum(member, axis=1, keepdims=True)
        pos_ref[:, at : at + step] = dest * 32 + rank.astype(I32)
        cell = cell_ref[:, at : at + step]
        sub = sub_ref[:, at : at + step]
        line = iota((width, step), 0)
        meta = jnp.where(
            line == 0,
            ((cell >> 7) + 1).astype(F32),
            jnp.where(
                line == 1,
                (cell & 127).astype(F32),
                jnp.where(line == 2, sub.astype(F32), 0.0),
            ),
        )
        wide_ref[at : at + step, width:] = meta.T.astype(BF16)
        wide_ref[at : at + step, :width] = feat_ref[at : at + step, :]

    pl.semaphore_wait(barrier, owners - 1)
    tiles = owners * 32 // step
    peers = step // 32
    near = (lon - iota((peers, 128), 0)) & 3
    mine = iota((peers, 128), 1) // 32 == lon

    @pl.loop(0, tiles)
    def _(turn):
        tile = lax.rem(turn + me // peers, tiles)
        local = pos_ref[...] - tile * step
        local = jnp.where((local >= 0) & (local < step), local, -1).astype(F32).astype(BF16)
        slot = iota((step, obs), 0).astype(F32).astype(BF16)
        pick = jnp.where(slot == local, jnp.ones((), BF16), jnp.zeros((), BF16))
        packed = jnp.dot(pick, wide_ref[...], preferred_element_type=F32)
        first = tile * peers
        sendf_ref[pl.ds(first, peers)] = packed[:, :width].astype(BF16).reshape(peers, 32, width)
        meta = packed[:, width:].T
        code = (meta[0:1] * 128.0 + meta[1:2]).astype(I32) * 256 + meta[2:3].astype(I32)
        lines = jnp.concatenate(
            [jnp.broadcast_to(code[:, :128], (4, 128)), jnp.broadcast_to(code[:, 128:], (4, 128))], axis=0
        )
        placed = jnp.zeros((peers, 128), I32)
        for k in range(4):
            placed = jnp.where(near == k, pltpu.roll(lines, 32 * k, 1) if k else lines, placed)
        placed = jnp.where(mine, placed, 0)
        for j in range(peers):
            sendm_ref[first + j] = placed[j : j + 1]
        for j in range(peers):
            peer = first + j

            @pl.when(peer != me)
            def _():
                there = (peer // lon_count, lax.rem(peer, lon_count))
                pltpu.make_async_remote_copy(
                    src_ref=sendf_ref.at[peer],
                    dst_ref=recvf_ref.at[me],
                    send_sem=send_sem.at[0],
                    recv_sem=recv_sem.at[0],
                    device_id=there,
                    device_id_type=MESH,
                ).start()
                pltpu.make_async_remote_copy(
                    src_ref=sendm_ref.at[peer],
                    dst_ref=recvm_ref.at[me],
                    send_sem=send_sem.at[1],
                    recv_sem=recv_sem.at[1],
                    device_id=there,
                    device_id_type=MESH,
                ).start()

    own = [
        pltpu.make_async_copy(sendf_ref.at[me], recvf_ref.at[me], own_sem.at[0]),
        pltpu.make_async_copy(sendm_ref.at[me], recvm_ref.at[me], own_sem.at[1]),
    ]
    for copy in own:
        copy.start()
    for copy in own:
        copy.wait()
    for sem in (send_sem, recv_sem):
        for i, (src, dst) in enumerate(((sendf_ref, recvf_ref), (sendm_ref, recvm_ref))):
            rest = pl.ds(0, owners - 1)
            pltpu.make_async_copy(src.at[rest], dst.at[rest], sem.at[i]).wait()


def route_call(dest, cell, sub, feat, owners):
    obs, width = feat.shape
    return pl.pallas_call(
        route_kernel,
        name="route",
        out_shape=(
            jax.ShapeDtypeStruct((owners, 32, width), BF16),
            jax.ShapeDtypeStruct((owners, 1, 128), I32),
        ),
        in_specs=[pl.BlockSpec(memory_space=pltpu.VMEM)] * 4,
        out_specs=[pl.BlockSpec(memory_space=pltpu.VMEM)] * 2,
        scratch_shapes=[
            pltpu.VMEM((1, obs), I32),
            pltpu.VMEM((obs, 2 * width), BF16),
            pltpu.VMEM((owners, 32, width), BF16),
            pltpu.VMEM((owners, 1, 128), I32),
            pltpu.SemaphoreType.DMA((2,)),
            pltpu.SemaphoreType.DMA((2,)),
            pltpu.SemaphoreType.DMA((2,)),
        ],
        compiler_params=pltpu.CompilerParams(
            collective_id=0, has_side_effects=True, vmem_limit_bytes=40 << 20
        ),
    )(dest, cell, sub, feat)


def grid_kernel(
    feat_ref, code_ref, back_ref, win_ref, dens_ref, grid_ref, wide_ref, cell_ref, kern_ref, codes_ref
):
    slots, width = feat_ref.shape
    cells = back_ref.shape[0]
    step = 256
    for group in range(code_ref.shape[0] // 4):
        code = code_ref[group * 4]
        for other in range(1, 4):
            code = code + code_ref[group * 4 + other]
        codes_ref[:, group * 128 : group * 128 + 128] = code
    code = codes_ref[...]
    sub = code & 255
    cell_ref[...] = (code >> 8) - 128
    row = ((sub >> 4).astype(F32) + 0.5) / 16.0 - 0.5
    col = ((sub & 15).astype(F32) + 0.5) / 16.0 - 0.5
    kern_ref[...] = jnp.exp(-(row * row + col * col) / (2.0 * 0.35 * 0.35))
    wide_ref[:, :width] = feat_ref[...]
    wide_ref[:, width:] = jnp.ones((slots, width), BF16)

    @pl.loop(0, cells // step)
    def _(tile):
        local = cell_ref[...] - tile * step
        local = jnp.where((local >= 0) & (local < step), local, -1).astype(F32).astype(BF16)
        kern = kern_ref[...].astype(BF16)
        line = iota((step, slots), 0).astype(F32).astype(BF16)
        pick = jnp.where(line == local, kern, jnp.zeros((), BF16))
        total = jnp.dot(pick, wide_ref[...], preferred_element_type=F32)
        density = total[:, width : width + 1]
        normed = (total[:, :width] / (density + 1.0)).astype(BF16)
        at = pl.multiple_of(tile * step, step)
        lifted = jnp.dot(normed, win_ref[...], preferred_element_type=F32)
        value = back_ref[pl.ds(at, step), :].astype(F32) + lifted + density * dens_ref[...]
        grid_ref[pl.ds(at, step), :] = value.astype(BF16)


def grid_call(feat, code, back, w_in, dens_vec):
    slots, width = feat.shape
    return pl.pallas_call(
        grid_kernel,
        name="grid",
        out_shape=jax.ShapeDtypeStruct(back.shape, BF16),
        scratch_shapes=[
            pltpu.VMEM((slots, 2 * width), BF16),
            pltpu.VMEM((1, slots), I32),
            pltpu.VMEM((1, slots), F32),
            pltpu.VMEM((1, slots), I32),
        ],
        compiler_params=pltpu.CompilerParams(vmem_limit_bytes=48 << 20),
    )(feat, code, back, w_in, dens_vec)


def conv_kernel(
    grid_ref, left_ref, right_ref, top_ref, bottom_ref, w_ref, b_ref, gain_ref,
    coarse_ref, normed_ref, line_ref, taps_ref, side_ref,
):
    rows, cols, channels = grid_ref.shape
    side_ref[0] = left_ref[...].astype(F32)
    side_ref[1] = right_ref[...].astype(F32)
    half = cols // 2

    def lay(at, line, left, right):
        for c in range(channels // 128):
            lanes = slice(c * 128, (c + 1) * 128)
            line_ref[c, 8 : 8 + cols, :] = line[:, lanes].astype(F32)
            line_ref[c, 7:8, :] = left[:, lanes].astype(F32)
            line_ref[c, 8 + cols : 9 + cols, :] = right[:, lanes].astype(F32)
            for tap in range(4):
                part = line_ref[c, pl.ds(7 + tap, half, stride=2), :]
                base = tap * channels + c * 128
                taps_ref[at, :, base : base + 128] = part.astype(BF16)

    lay(0, top_ref[:cols, :], top_ref[cols : cols + 1, :], top_ref[cols + 1 : cols + 2, :])
    lay(
        rows + 1,
        bottom_ref[:cols, :],
        bottom_ref[cols : cols + 1, :],
        bottom_ref[cols + 1 : cols + 2, :],
    )

    @pl.loop(0, rows)
    def _(row):
        lay(row + 1, grid_ref[row], side_ref[0, pl.ds(row, 1), :], side_ref[1, pl.ds(row, 1), :])

    @pl.loop(0, rows // 8)
    def _(part):
        total = jnp.zeros((4 * half, channels), F32)
        for tap in range(4):
            window = jnp.concatenate(
                [taps_ref[part * 8 + 2 * i + tap] for i in range(4)], axis=0
            )
            total = total + jnp.dot(window, w_ref[tap], preferred_element_type=F32)
        total = total + b_ref[...]
        inner = 0.7978845608028654 * (total + 0.044715 * total * total * total)
        coarse = (0.5 * total * (1.0 + jnp.tanh(inner))).astype(BF16)
        at = pl.multiple_of(part * 4 * half, 4 * half)
        coarse_ref[pl.ds(at, 4 * half), :] = coarse
        value = coarse.astype(F32)
        scale = lax.rsqrt(jnp.mean(value * value, axis=1, keepdims=True) + 1e-05)
        normed_ref[pl.ds(at, 4 * half), :] = (value * scale * gain_ref[...]).astype(BF16)


def conv_call(grid, left, right, top, bottom, conv_w, conv_b, norm_gain):
    rows, cols, channels = grid.shape
    out = jax.ShapeDtypeStruct((rows // 2 * cols // 2, channels), BF16)
    return pl.pallas_call(
        conv_kernel,
        name="conv",
        out_shape=(out, out),
        scratch_shapes=[
            pltpu.VMEM((channels // 128, cols + 16, 128), F32),
            pltpu.VMEM((rows + 2, cols // 2, 4 * channels), BF16),
            pltpu.VMEM((2, rows, channels), F32),
        ],
        compiler_params=pltpu.CompilerParams(vmem_limit_bytes=56 << 20),
    )(grid, left, right, top, bottom, conv_w, conv_b, norm_gain)


def attend_kernel(
    normed_ref, ext_ref, wqkv_ref, strip_ref, wout_ref, coarse_ref, out_ref,
    query_ref, key_ref, value_ref, bias_ref,
):
    key_rows, key_cols, channels = ext_ref.shape
    rows, cols = key_rows - 12, key_cols - 16
    half = channels // 2
    head = channels // HEADS
    lat, lat_count = lax.axis_index("lat"), lax.axis_size("lat")
    query_ref[...] = (
        jnp.dot(normed_ref[...], wqkv_ref[:, :channels], preferred_element_type=F32)
        .astype(BF16)
        .reshape(rows, cols, channels)
    )

    @pl.loop(0, key_rows // 4)
    def _(part):
        ext = ext_ref[pl.ds(part * 4, 4)].reshape(4 * key_cols, channels)
        both = jnp.dot(ext, wqkv_ref[:, channels:], preferred_element_type=F32).astype(BF16)
        key_ref[pl.ds(part * 4, 4)] = both[:, :channels].reshape(4, key_cols, channels)
        value_ref[pl.ds(part * 4, 4)] = both[:, channels:].reshape(4, key_cols, channels)

    for h in range(HEADS):
        strip = jnp.broadcast_to(strip_ref[h : h + 1, :], (16, 512))
        for r in range(4):
            at = h * 64 + r * 16
            bias_ref[at : at + 16, :] = pltpu.roll(
                strip, 2 + 32 * r, 1, stride=1, stride_axis=0
            )

    lane_head = iota((64, half), 1) // head

    @pl.loop(0, rows // 4)
    def _(down):
        first = lat * rows - 6 + down * 4
        key_row = first + iota((1, 512), 1) // 32
        edge = jnp.where((key_row >= 0) & (key_row < lat_count * rows), 0.0, NEG)

        @pl.loop(0, cols // 16)
        def _(across):
            c0 = pl.multiple_of(across * 16, 16)
            query = query_ref[pl.ds(down * 4, 4), pl.ds(c0, 16), :].reshape(64, channels)
            query = query * 0.125
            parts = []
            for g in range(2):
                lanes = slice(g * half, (g + 1) * half)
                keys = key_ref[pl.ds(down * 4, 16), pl.ds(c0, 32), lanes].reshape(512, half)
                values = value_ref[pl.ds(down * 4, 16), pl.ds(c0, 32), lanes].reshape(512, half)
                wide = query[:, lanes]
                masked = jnp.concatenate(
                    [jnp.where(lane_head == h, wide, jnp.zeros((), BF16)) for h in range(4)],
                    axis=0,
                )
                scores = lax.dot_general(
                    masked, keys, (((1,), (1,)), ((), ())), preferred_element_type=F32
                )
                scores = scores + bias_ref[g * 256 : (g + 1) * 256, :] + edge
                peak = jnp.max(scores, axis=1, keepdims=True)
                weight = jnp.exp(scores - peak)
                norm = jnp.sum(weight, axis=1, keepdims=True)
                mixed = jnp.dot(weight.astype(BF16), values, preferred_element_type=F32) / norm
                total = jnp.zeros((64, half), F32)
                for h in range(4):
                    total = jnp.where(lane_head == h, mixed[h * 64 : (h + 1) * 64], total)
                parts.append(total.astype(BF16))
            attended = jnp.concatenate(parts, axis=1)
            lifted = jnp.dot(attended, wout_ref[...], preferred_element_type=F32)
            base = coarse_ref[pl.ds(down * 4, 4), pl.ds(c0, 16), :].astype(F32)
            result = base + lifted.reshape(4, 16, channels)
            out_ref[pl.ds(down * 4, 4), pl.ds(c0, 16), :] = result.astype(BF16)


def attend_call(normed, ext, w_qkv, strip, w_out, coarse):
    key_rows, key_cols, channels = ext.shape
    rows, cols = key_rows - 12, key_cols - 16
    return pl.pallas_call(
        attend_kernel,
        name="attend",
        out_shape=jax.ShapeDtypeStruct((rows, cols, channels), BF16),
        scratch_shapes=[
            pltpu.VMEM((rows, cols, channels), BF16),
            pltpu.VMEM((key_rows, key_cols, channels), BF16),
            pltpu.VMEM((key_rows, key_cols, channels), BF16),
            pltpu.VMEM((512, 512), F32),
        ],
        compiler_params=pltpu.CompilerParams(vmem_limit_bytes=48 << 20),
    )(normed, ext, w_qkv, strip, w_out, coarse)


def moved(x, axis, step, wrap):
    size = lax.axis_size(axis)
    pairs = [(i, i + step) for i in range(size) if 0 <= i + step < size]
    if wrap:
        pairs = [(i, (i + step) % size) for i in range(size)]
    return lax.ppermute(x, axis, pairs)


def body(
    obs_feat, obs_dest, obs_cell, obs_sub, background, w_in, dens_vec,
    conv_w, conv_b, norm_gain, w_qkv, rel_bias, w_out,
):
    owners = lax.axis_size("lat") * lax.axis_size("lon")
    rows, cols, channels = background.shape
    obs, width = obs_feat.shape
    recvf, recvm = route_call(
        obs_dest.reshape(1, obs), obs_cell.reshape(1, obs), obs_sub.reshape(1, obs), obs_feat, owners
    )
    grid = grid_call(
        recvf.reshape(owners * 32, width),
        recvm,
        background.reshape(rows * cols, channels),
        w_in,
        dens_vec.reshape(1, channels),
    ).reshape(rows, cols, channels)
    left = moved(grid[:, cols - 1, :], "lon", 1, True)
    right = moved(grid[:, 0, :], "lon", -1, True)
    pad = jnp.zeros((14, channels), BF16)
    top = moved(jnp.concatenate([grid[-1], left[-1:], right[-1:], pad]), "lat", 1, False)
    bottom = moved(jnp.concatenate([grid[0], left[:1], right[:1], pad]), "lat", -1, False)
    coarse, normed = conv_call(
        grid, left, right, top, bottom,
        conv_w.reshape(4, 4 * channels, channels),
        conv_b.reshape(1, channels),
        norm_gain.reshape(1, channels),
    )
    normed3 = normed.reshape(rows // 2, cols // 2, channels)
    before = moved(normed3[:, -8:], "lon", 1, True)
    after = moved(normed3[:, :8], "lon", -1, True)
    ext = jnp.concatenate([before, normed3, after], axis=1)
    over = moved(ext[-6:], "lat", 1, False)
    under = moved(ext[:6], "lat", -1, False)
    ext = jnp.concatenate([over, ext, under], axis=0)
    strip = jnp.pad(rel_bias, ((0, 0), (0, 3), (0, 19)), constant_values=NEG).reshape(HEADS, 512)
    return attend_call(
        normed, ext, w_qkv, strip, w_out, coarse.reshape(rows // 2, cols // 2, channels)
    )


def solution(mesh):
    split = P(("lat", "lon"))
    wide = P(("lat", "lon"), None)
    tile = P("lat", "lon", None)
    in_specs = (wide, wide, split, split, tile) + (P(),) * 8
    return jax.shard_map(body, mesh=mesh, in_specs=in_specs, out_specs=tile, check_vma=False)
```

```python
import jax
import jax.numpy as jnp
from jax import lax
from jax.experimental import pallas as pl
from jax.experimental.pallas import tpu as pltpu
from jax.sharding import PartitionSpec as P

HEADS = 8
F32 = jnp.float32
BF16 = jnp.bfloat16
I32 = jnp.int32
NEG = -1e30
MESH = pl.DeviceIdType.MESH
WAYS = ((-1, 0), (1, 0), (0, -1), (0, 1), (-1, -1), (-1, 1), (1, -1), (1, 1))


def iota(shape, dim):
    return lax.broadcasted_iota(I32, shape, dim)


def narrow(x):
    return x.astype(F32).astype(BF16)


def dot(x, y):
    return jnp.dot(x, y, preferred_element_type=F32)


def dot_t(x, y):
    return lax.dot_general(x, y, (((1,), (1,)), ((), ())), preferred_element_type=F32)


def column(row):
    return jnp.broadcast_to(row.astype(F32), (128, 128)).T.astype(BF16)


def one_hot(place_ref, index, value):
    for part in range(place_ref.shape[0] // 256):
        local = index - part * 256
        local = narrow(jnp.where((local >= 0) & (local < 256), local, -1))
        line = narrow(iota((256, index.shape[1]), 0))
        place_ref[part * 256 : part * 256 + 256, :] = jnp.where(
            line == local, value, jnp.zeros((), BF16)
        )


def main_kernel(
    dest_ref, cell_ref, sub_ref, feat_ref, back_hbm, win_ref, dens_ref, conv_hbm, bias_in_ref,
    gain_ref, wqkv_hbm, strip_ref, wout_hbm,
    out_ref,
    back_ref, conv_ref, wqkv_ref, wout_ref,
    sendf_ref, sendm_ref, recvf_ref, recvm_ref, pick_ref, group_ref, local_ref,
    edge_ref, brow_ref, bside_ref, line_ref, taps_ref, acc_ref, comp_ref,
    codes_ref, spread_ref, sums_ref, oedge_ref, oline_ref, orow_ref, oside_ref, otaps_ref,
    own_ref, coarse_ref, vert_ref, side_ref, query_ref, key_ref, value_ref, bias_ref,
    load_sem, route_sem, own_sem, halo_send, halo_recv,
):
    obs, width = feat_ref.shape
    owners = sendf_ref.shape[0]
    slots = owners * 32
    rows, cols, channels = back_ref.shape
    half = cols // 2
    out_rows = rows // 2
    both = 2 * width
    lat_count, lon_count = lax.axis_size("lat"), lax.axis_size("lon")
    lat, lon = lax.axis_index("lat"), lax.axis_index("lon")
    me = lat * lon_count + lon

    loads = [
        pltpu.make_async_copy(src, dst, load_sem.at[i])
        for i, (src, dst) in enumerate(
            ((back_hbm, back_ref), (conv_hbm, conv_ref), (wqkv_hbm, wqkv_ref), (wout_hbm, wout_ref))
        )
    ]
    for load in loads:
        load.start()

    barrier = pltpu.get_barrier_semaphore()

    @pl.loop(1, owners)
    def _(k):
        peer = lax.rem(me + k, owners)
        pl.semaphore_signal(
            barrier, inc=1, device_id=(peer // lon_count, lax.rem(peer, lon_count)), device_id_type=MESH
        )

    def inside(da):
        return (lat + da >= 0) & (lat + da < lat_count)

    def halo(base, parts):
        copies = []
        for i, ((da, db), (src, dst)) in enumerate(zip(WAYS, parts)):
            copies.append(
                (
                    da,
                    pltpu.make_async_remote_copy(
                        src_ref=src,
                        dst_ref=dst,
                        send_sem=halo_send.at[base + i],
                        recv_sem=halo_recv.at[base + i],
                        device_id=(lat + da, lax.rem(lon + db + lon_count, lon_count)),
                        device_id_type=MESH,
                    ),
                )
            )
        return copies

    def halo_start(copies):
        for da, copy in copies:
            pl.when(inside(da))(copy.start)

    def halo_arrive(copies):
        for da, copy in copies:
            pl.when(inside(-da))(copy.wait_recv)

    def halo_sent(copies):
        for da, copy in copies:
            pl.when(inside(da))(copy.wait_send)

    step = 256
    upper = (iota((step, step), 0) < iota((step, step), 1)).astype(F32).astype(BF16)
    running = jnp.zeros((owners, 1), F32)
    for at in range(0, obs, step):
        dest = dest_ref[:, at : at + step]
        member = (iota((owners, step), 0) == dest).astype(F32)
        earlier = dot(member.astype(BF16), upper) + running
        rank = jnp.sum(member * earlier, axis=0, keepdims=True)
        running = running + jnp.sum(member, axis=1, keepdims=True)
        local_ref[:, at : at + step] = (dest & 15) * 32 + rank.astype(I32)
        for more in range(0, step, 128):
            group_ref[at + more : at + more + 128, :] = column(dest[:, more : more + 128] >> 4)
    one_hot(pick_ref, local_ref[...], jnp.ones((), BF16))

    dest, cell, sub = dest_ref[...], cell_ref[...], sub_ref[...]
    same = iota((8, obs), 0) == (dest >> 4)
    meta = jnp.concatenate(
        [jnp.where(same, value, 0) for value in ((cell >> 7) + 1, cell & 127, sub, dest * 0)], axis=0
    )
    meta = dot_t(narrow(meta), pick_ref[...])
    code = (meta[0:8] * 128.0 + meta[8:16]).astype(I32) * 256 + meta[16:24].astype(I32)
    mine = iota((8, 128), 1) // 32 == lon
    for c in range(4):
        chunk = code[:, c * 128 : c * 128 + 128]
        turned = [chunk] + [pltpu.roll(chunk, 32 * k, 1) for k in range(1, 4)]
        for j in range(4):
            near = (lon - j) & 3
            placed = jnp.where(
                near < 2,
                jnp.where(near == 0, turned[0], turned[1]),
                jnp.where(near == 2, turned[2], turned[3]),
            )
            placed = jnp.where(mine, placed, 0)
            for g in range(8):
                sendm_ref[g * 16 + c * 4 + j] = placed[g : g + 1]

    loads[0].wait()
    for row in range(rows):
        tile = back_ref[row, 0:16, :].astype(F32)
        edge_ref[0, row : row + 1, :] = tile[0:1]
        tile = back_ref[row, cols - 16 : cols, :].astype(F32)
        edge_ref[1, row : row + 1, :] = tile[15:16]

    pl.semaphore_wait(barrier, owners - 1)

    def fine_parts(first, last, edge, row, side):
        top, bottom = pl.ds(0, 8), pl.ds(rows - 8, 8)
        return (
            (first, row.at[1]),
            (last, row.at[0]),
            (edge.at[0], side.at[1, pl.ds(8, rows)]),
            (edge.at[1], side.at[0, pl.ds(8, rows)]),
            (edge.at[0, top], side.at[1, pl.ds(8 + rows, 8)]),
            (edge.at[1, top], side.at[0, pl.ds(8 + rows, 8)]),
            (edge.at[0, bottom], side.at[1, pl.ds(0, 8)]),
            (edge.at[1, bottom], side.at[0, pl.ds(0, 8)]),
        )

    halo_back = halo(0, fine_parts(back_ref.at[0], back_ref.at[rows - 1], edge_ref, brow_ref, bside_ref))
    halo_start(halo_back)

    @pl.loop(0, owners // 32)
    def _(turn):
        part = lax.rem(turn + me // 32, owners // 32)
        group = group_ref[...]
        feat = feat_ref[...]
        wide = jnp.concatenate(
            [
                jnp.where(
                    group == jnp.full((1, 1), 2 * part + i, I32).astype(F32).astype(BF16),
                    feat,
                    jnp.zeros((), BF16),
                )
                for i in range(2)
            ],
            axis=1,
        )
        packed = dot(pick_ref[...], wide).astype(BF16)
        for i in range(2):
            sendf_ref[pl.ds(part * 32 + i * 16, 16)] = packed[:, i * width : (i + 1) * width].reshape(
                16, 32, width
            )

        @pl.loop(0, 32)
        def _(k):
            peer = part * 32 + k

            @pl.when(peer != me)
            def _():
                there = (peer // lon_count, lax.rem(peer, lon_count))
                for i, (src, dst) in enumerate(((sendf_ref, recvf_ref), (sendm_ref, recvm_ref))):
                    pltpu.make_async_remote_copy(
                        src_ref=src.at[peer],
                        dst_ref=dst.at[me],
                        send_sem=route_sem.at[i],
                        recv_sem=route_sem.at[2 + i],
                        device_id=there,
                        device_id_type=MESH,
                    ).start()

    own_copies = [
        pltpu.make_async_copy(src.at[me], dst.at[me], own_sem.at[i])
        for i, (src, dst) in enumerate(((sendf_ref, recvf_ref), (sendm_ref, recvm_ref)))
    ]
    for copy in own_copies:
        copy.start()

    @pl.when(lat == 0)
    def _():
        brow_ref[0] = jnp.zeros((cols, channels), BF16)
        bside_ref[:, 0:8, :] = jnp.zeros((2, 8, channels), F32)
        orow_ref[0] = jnp.zeros((cols, both), BF16)
        oside_ref[:, 0:8, :] = jnp.zeros((2, 8, both), F32)
        vert_ref[0] = jnp.zeros((6, half, channels), BF16)
        side_ref[:, 0:6] = jnp.zeros((2, 6, 16, channels), BF16)

    @pl.when(lat == lat_count - 1)
    def _():
        brow_ref[1] = jnp.zeros((cols, channels), BF16)
        bside_ref[:, 8 + rows :, :] = jnp.zeros((2, 8, channels), F32)
        orow_ref[1] = jnp.zeros((cols, both), BF16)
        oside_ref[:, 8 + rows :, :] = jnp.zeros((2, 8, both), F32)
        vert_ref[1] = jnp.zeros((6, half, channels), BF16)
        side_ref[:, 18:24] = jnp.zeros((2, 6, 16, channels), BF16)

    halo_arrive(halo_back)

    def lay(taps, buffer, slot, at, line, left, right):
        size = line.shape[1]
        for c in range(size // 128):
            lanes = slice(c * 128, (c + 1) * 128)
            spot = slot * (size // 128) + c
            buffer[spot, 8 : 8 + cols, :] = line[:, lanes].astype(F32)
            if left is not None:
                buffer[spot, 7:8, :] = left[:, lanes]
                buffer[spot, 8 + cols : 9 + cols, :] = right[:, lanes]
            for tap in range(4):
                part = buffer[spot, pl.ds(7 + tap, half, stride=2), :]
                base = tap * size + c * 128
                taps[at, :, base : base + 128] = part.astype(BF16)

    for i, at in ((0, 0), (1, rows + 1)):
        lay(
            taps_ref, line_ref, i, at, brow_ref[i],
            bside_ref[0, at + 7 : at + 8, :], bside_ref[1, at + 7 : at + 8, :],
        )

    @pl.loop(0, rows // 2)
    def _(pair):
        for i in range(2):
            row = pair * 2 + i
            lay(
                taps_ref, line_ref, i, row + 1, back_ref[row],
                bside_ref[0, pl.ds(row + 8, 1), :], bside_ref[1, pl.ds(row + 8, 1), :],
            )

    loads[1].wait()
    block = 4 * half

    def window(taps, part, tap):
        return taps[pl.ds(part * 4 + tap // 2, 4), tap % 2].reshape(block, taps.shape[3])

    taps4 = taps_ref.reshape(rows // 2 + 1, 2, half, 4 * channels)
    otaps4 = otaps_ref.reshape(rows // 2 + 1, 2, half, 4 * both)

    @pl.loop(0, out_rows // 4)
    def _(part):
        total = jnp.broadcast_to(bias_in_ref[...], (block, channels))
        for tap in range(4):
            total = total + dot(window(taps4, part, tap), conv_ref[tap])
        acc_ref[pl.ds(pl.multiple_of(part * block, block), block), :] = total

    dens = jnp.broadcast_to(dens_ref[...], (16, channels))
    dens_hi = dens.astype(BF16)
    dens_lo = (dens - dens_hi.astype(F32)).astype(BF16)
    line16 = iota((16, channels), 0)
    tail = jnp.where(
        line16 == 0, dens_hi.astype(F32), jnp.where(line16 == 1, dens_lo.astype(F32), 0.0)
    ).astype(BF16)
    lift = jnp.concatenate([win_ref[...], tail], axis=0)

    @pl.loop(0, 4)
    def _(tap):
        for s in range(4):
            made = dot(lift, conv_ref[tap, s * channels : (s + 1) * channels, :])
            base = s * both
            comp_ref[tap, base : base + width, :] = made[:width].astype(BF16)
            whole = made[width : width + 1] + made[width + 1 : width + 2]
            upper_part = whole.astype(BF16).astype(F32)
            rest = jnp.where(
                line16 < 2, upper_part, jnp.where(line16 == 2, whole - upper_part, 0.0)
            ).astype(BF16)
            comp_ref[tap, base + width : base + width + 16, :] = rest
            comp_ref[tap, base + width + 16 : base + both, :] = jnp.zeros(
                (width - 16, channels), BF16
            )

    for h in range(HEADS):
        strip = jnp.broadcast_to(strip_ref[h : h + 1, :], (16, 512))
        for r in range(4):
            at = h * 64 + r * 16
            bias_ref[at : at + 16, :] = pltpu.roll(strip, 2 + 32 * r, 1, stride=1, stride_axis=0)

    for copy in own_copies:
        copy.wait()
    rest = pl.ds(0, owners - 1)
    for i, (src, dst) in enumerate(((sendf_ref, recvf_ref), (sendm_ref, recvm_ref))):
        pltpu.make_async_copy(src.at[rest], dst.at[rest], route_sem.at[i]).wait()
        pltpu.make_async_copy(src.at[rest], dst.at[rest], route_sem.at[2 + i]).wait()
    for group in range(owners // 4):
        code = recvm_ref[group * 4]
        for other in range(1, 4):
            code = code + recvm_ref[group * 4 + other]
        codes_ref[:, group * 128 : group * 128 + 128] = code

    chunk = spread_ref.shape[0]
    lane = narrow(iota((128, 128), 1))
    for c in range(slots // chunk):
        code = codes_ref[:, c * chunk : (c + 1) * chunk]
        sub = code & 255
        cell = (code >> 8) - 128
        row_off = ((sub >> 4).astype(F32) + 0.5) / 16.0 - 0.5
        col_off = ((sub & 15).astype(F32) + 0.5) / 16.0 - 0.5
        kern = jnp.exp(-(row_off * row_off + col_off * col_off) / (2.0 * 0.35 * 0.35))
        one_hot(pick_ref, cell & 511, kern.astype(BF16))
        band = cell >> 9
        for b in range(chunk // 128):
            spot = column(band[:, b * 128 : b * 128 + 128])
            first = (c * chunk + b * 128) // 32
            feat = recvf_ref[first : first + 4].reshape(128, width)
            lines = slice(b * 128, b * 128 + 128)
            for g in range(rows // 4):
                here = jnp.full((1, 1), g, F32).astype(BF16)
                spread_ref[lines, g * width : (g + 1) * width] = jnp.where(
                    spot == here, feat, jnp.zeros((), BF16)
                )
            spread_ref[lines, rows // 4 * width :] = jnp.where(
                spot == lane, jnp.ones((), BF16), jnp.zeros((), BF16)
            )
        part = dot(pick_ref[...], spread_ref[...])
        sums_ref[...] = part if c == 0 else sums_ref[...] + part

    lane_f = iota((cols, width), 1)
    for g in range(rows // 4):
        for r in range(4):
            row = g * 4 + r
            lines = slice(r * cols, (r + 1) * cols)
            density = sums_ref[lines, rows // 4 * width + g : rows // 4 * width + g + 1]
            normed = sums_ref[lines, g * width : (g + 1) * width] / (density + 1.0)
            high = density.astype(BF16).astype(F32)
            marks = jnp.where(
                (lane_f == 0) | (lane_f == 2), high, jnp.where(lane_f == 1, density - high, 0.0)
            )
            line = jnp.concatenate([normed, marks], axis=1)
            oedge_ref[0, row : row + 1, :] = line[0:1]
            oedge_ref[1, row : row + 1, :] = line[cols - 1 : cols]
            if row == 0:
                orow_ref[2] = line.astype(BF16)
            if row == rows - 1:
                orow_ref[3] = line.astype(BF16)
            lay(otaps_ref, oline_ref, row % 2, row + 1, line, None, None)

    halo_obs = halo(8, fine_parts(orow_ref.at[2], orow_ref.at[3], oedge_ref, orow_ref, oside_ref))
    halo_start(halo_obs)
    halo_arrive(halo_obs)
    for i, at in ((0, 0), (1, rows + 1)):
        lay(otaps_ref, oline_ref, i, at, orow_ref[i], None, None)
    first_line = iota((16, both), 0) == 0
    last_line = iota((16, both), 0) == 15
    for at in range(rows + 2):
        old = otaps_ref[at, 0:16, 0:both].astype(F32)
        otaps_ref[at, 0:16, 0:both] = jnp.where(
            first_line, oside_ref[0, at + 7 : at + 8, :], old
        ).astype(BF16)
        old = otaps_ref[at, half - 16 : half, 3 * both :].astype(F32)
        otaps_ref[at, half - 16 : half, 3 * both :] = jnp.where(
            last_line, oside_ref[1, at + 7 : at + 8, :], old
        ).astype(BF16)

    loads[2].wait()
    loads[3].wait()

    @pl.loop(0, out_rows // 4)
    def _(part):
        at = pl.multiple_of(part * block, block)
        total = acc_ref[pl.ds(at, block), :]
        for tap in range(4):
            total = total + dot(window(otaps4, part, tap), comp_ref[tap])
        inner = 0.7978845608028654 * (total + 0.044715 * total * total * total)
        coarse = (0.5 * total * (1.0 + jnp.tanh(inner))).astype(BF16)
        coarse_ref[pl.ds(part * 4, 4)] = coarse.reshape(4, half, channels)
        value = coarse.astype(F32)
        scale = lax.rsqrt(jnp.mean(value * value, axis=1, keepdims=True) + 1e-05)
        normed = (value * scale * gain_ref[...]).astype(BF16)
        own_ref[pl.ds(part * 4, 4)] = normed.reshape(4, half, channels)

    upside, downside = pl.ds(0, 6), pl.ds(out_rows - 6, 6)
    lower, higher = pl.ds(0, 16), pl.ds(half - 16, 16)
    middle, before, after = pl.ds(6, out_rows), pl.ds(0, 6), pl.ds(6 + out_rows, 6)
    halo_norm = halo(
        16,
        (
            (own_ref.at[upside], vert_ref.at[1]),
            (own_ref.at[downside], vert_ref.at[0]),
            (own_ref.at[:, lower], side_ref.at[1, middle]),
            (own_ref.at[:, higher], side_ref.at[0, middle]),
            (own_ref.at[upside, lower], side_ref.at[1, after]),
            (own_ref.at[upside, higher], side_ref.at[0, after]),
            (own_ref.at[downside, lower], side_ref.at[1, before]),
            (own_ref.at[downside, higher], side_ref.at[0, before]),
        ),
    )
    halo_start(halo_norm)

    def keys_values(x, lead):
        made = dot(x.reshape(lead * x.shape[1], channels), wqkv_ref[:, channels:])
        made = made.reshape(lead, x.shape[1], 2 * channels)
        return made[:, :, :channels], made[:, :, channels:]

    @pl.loop(0, out_rows // 4)
    def _(part):
        own = own_ref[pl.ds(part * 4, 4)]
        query = dot(own.reshape(block, channels), wqkv_ref[:, :channels]).astype(BF16) * 0.125
        query_ref[pl.ds(part * 4, 4)] = query.astype(BF16).reshape(4, half, channels)
        key, value = keys_values(own, 4)
        key_ref[pl.ds(part * 4 + 6, 4), 8 : 8 + half, :] = key.astype(BF16)
        value_ref[pl.ds(part * 4 + 6, 4), 8 : 8 + half, :] = value.astype(BF16)

    halo_arrive(halo_norm)
    for i, at in ((0, 0), (1, 6 + out_rows)):
        key, value = keys_values(vert_ref[i], 6)
        key_ref[at : at + 6, 8 : 8 + half, :] = key.astype(BF16)
        value_ref[at : at + 6, 8 : 8 + half, :] = value.astype(BF16)
    for i, at, cut in ((0, 0, slice(8, 16)), (1, 8 + half, slice(0, 8))):
        key, value = keys_values(side_ref[i], out_rows + 12)
        key_ref[:, at : at + 8, :] = key[:, cut].astype(BF16)
        value_ref[:, at : at + 8, :] = value[:, cut].astype(BF16)

    half_ch = channels // 2
    lane_head = iota((64, half_ch), 1) // (channels // HEADS)

    @pl.loop(0, out_rows // 4)
    def _(down):
        first = lat * out_rows - 6 + down * 4
        key_row = first + iota((1, 512), 1) // 32
        beyond = jnp.where((key_row >= 0) & (key_row < lat_count * out_rows), 0.0, NEG)

        @pl.loop(0, half // 16)
        def _(across):
            c0 = pl.multiple_of(across * 16, 16)
            query = query_ref[pl.ds(down * 4, 4), pl.ds(c0, 16), :].reshape(64, channels)
            parts = []
            for g in range(2):
                lanes = slice(g * half_ch, (g + 1) * half_ch)
                keys = key_ref[pl.ds(down * 4, 16), pl.ds(c0, 32), lanes].reshape(512, half_ch)
                values = value_ref[pl.ds(down * 4, 16), pl.ds(c0, 32), lanes].reshape(512, half_ch)
                wide = query[:, lanes]
                masked = jnp.concatenate(
                    [jnp.where(lane_head == h, wide, jnp.zeros((), BF16)) for h in range(4)], axis=0
                )
                scores = dot_t(masked, keys)
                scores = scores + bias_ref[g * 256 : (g + 1) * 256, :] + beyond
                peak = jnp.max(scores, axis=1, keepdims=True)
                weight = jnp.exp(scores - peak)
                norm = jnp.sum(weight, axis=1, keepdims=True)
                mixed = dot(weight.astype(BF16), values) / norm
                total = jnp.zeros((64, half_ch), F32)
                for h in range(4):
                    total = jnp.where(lane_head == h, mixed[h * 64 : (h + 1) * 64], total)
                parts.append(total.astype(BF16))
            attended = jnp.concatenate(parts, axis=1)
            lifted = dot(attended, wout_ref[...])
            base = coarse_ref[pl.ds(down * 4, 4), pl.ds(c0, 16), :].astype(F32)
            result = base + lifted.reshape(4, 16, channels)
            out_ref[pl.ds(down * 4, 4), pl.ds(c0, 16), :] = result.astype(BF16)

    for copies in (halo_back, halo_obs, halo_norm):
        halo_sent(copies)


def body(
    obs_feat, obs_dest, obs_cell, obs_sub, background, w_in, dens_vec,
    conv_w, conv_b, norm_gain, w_qkv, rel_bias, w_out,
):
    owners = lax.axis_size("lat") * lax.axis_size("lon")
    rows, cols, channels = background.shape
    obs, width = obs_feat.shape
    half, out_rows, both = cols // 2, rows // 2, 2 * width
    strip = jnp.pad(rel_bias, ((0, 0), (0, 3), (0, 19)), constant_values=NEG).reshape(HEADS, 512)
    vmem = pl.BlockSpec(memory_space=pltpu.VMEM)
    hbm = pl.BlockSpec(memory_space=pl.ANY)
    scratch = [
        ((rows, cols, channels), BF16),
        ((4, 4 * channels, channels), BF16),
        ((channels, 3 * channels), BF16),
        ((channels, channels), BF16),
        ((owners, 32, width), BF16),
        ((owners, 1, 128), I32),
        ((owners, 32, width), BF16),
        ((owners, 1, 128), I32),
        ((512, obs), BF16),
        ((obs, width), BF16),
        ((1, obs), I32),
        ((2, rows, channels), F32),
        ((2, cols, channels), BF16),
        ((2, rows + 16, channels), F32),
        ((2 * channels // 128, cols + 16, 128), F32),
        ((rows + 2, half, 4 * channels), BF16),
        ((half * out_rows, channels), F32),
        ((4, 4 * both, channels), BF16),
        ((1, owners * 32), I32),
        ((obs, rows // 4 * width + 128), BF16),
        ((512, rows // 4 * width + 128), F32),
        ((2, rows, both), F32),
        ((2 * both // 128, cols + 16, 128), F32),
        ((4, cols, both), BF16),
        ((2, rows + 16, both), F32),
        ((rows + 2, half, 4 * both), BF16),
        ((out_rows, half, channels), BF16),
        ((out_rows, half, channels), BF16),
        ((2, 6, half, channels), BF16),
        ((2, out_rows + 12, 16, channels), BF16),
        ((out_rows, half, channels), BF16),
        ((out_rows + 12, half + 16, channels), BF16),
        ((out_rows + 12, half + 16, channels), BF16),
        ((HEADS * 64, 512), F32),
    ]
    sems = [pltpu.SemaphoreType.DMA((n,)) for n in (4, 4, 2, 24, 24)]
    return pl.pallas_call(
        main_kernel,
        name="main",
        out_shape=jax.ShapeDtypeStruct((out_rows, half, channels), BF16),
        in_specs=[vmem, vmem, vmem, vmem, hbm, vmem, vmem, hbm, vmem, vmem, hbm, vmem, hbm],
        out_specs=vmem,
        scratch_shapes=[pltpu.VMEM(shape, dtype) for shape, dtype in scratch] + sems,
        compiler_params=pltpu.CompilerParams(
            collective_id=0, has_side_effects=True, vmem_limit_bytes=62 << 20
        ),
    )(
        obs_dest.reshape(1, obs),
        obs_cell.reshape(1, obs),
        obs_sub.reshape(1, obs),
        obs_feat,
        background,
        w_in,
        dens_vec.reshape(1, channels),
        conv_w.reshape(4, 4 * channels, channels),
        conv_b.reshape(1, channels),
        norm_gain.reshape(1, channels),
        w_qkv,
        strip,
        w_out,
    )


def solution(mesh):
    split = P(("lat", "lon"))
    wide = P(("lat", "lon"), None)
    tile = P("lat", "lon", None)
    in_specs = (wide, wide, split, split, tile) + (P(),) * 8
    return jax.shard_map(body, mesh=mesh, in_specs=in_specs, out_specs=tile, check_vma=False)
```

```python
import jax
import jax.numpy as jnp
from jax import lax
from jax.experimental import pallas as pl
from jax.experimental.pallas import tpu as pltpu
from jax.sharding import PartitionSpec as P

HEADS = 8
F32 = jnp.float32
BF16 = jnp.bfloat16
I32 = jnp.int32
NEG = -1e30
MESH = pl.DeviceIdType.MESH
WAYS = ((-1, 0), (1, 0), (0, -1), (0, 1), (-1, -1), (-1, 1), (1, -1), (1, 1))


def iota(shape, dim):
    return lax.broadcasted_iota(I32, shape, dim)


def narrow(x):
    return x.astype(F32).astype(BF16)


def dot(x, y):
    return jnp.dot(x, y, preferred_element_type=F32)


def dot_t(x, y):
    return lax.dot_general(x, y, (((1,), (1,)), ((), ())), preferred_element_type=F32)


def column(row):
    return jnp.broadcast_to(row.astype(F32), (128, 128)).T.astype(BF16)


def one_hot(place_ref, index, value):
    for part in range(place_ref.shape[0] // 256):
        local = index - part * 256
        local = narrow(jnp.where((local >= 0) & (local < 256), local, -1))
        line = narrow(iota((256, index.shape[1]), 0))
        place_ref[part * 256 : part * 256 + 256, :] = jnp.where(
            line == local, value, jnp.zeros((), BF16)
        )


def main_kernel(
    dest_ref, cell_ref, sub_ref, feat_ref, back_hbm, win_ref, dens_ref, conv_hbm, bias_in_ref,
    gain_ref, wqkv_hbm, strip_ref, wout_hbm,
    out_ref,
    back_ref, conv_ref, wqkv_ref, wout_ref,
    sendf_ref, sendm_ref, recvf_ref, recvm_ref, pick_ref, group_ref, local_ref,
    edge_ref, brow_ref, bside_ref, line_ref, taps_ref, acc_ref, comp_ref,
    codes_ref, spread_ref, sums_ref, oedge_ref, oline_ref, orow_ref, oside_ref, otaps_ref,
    own_ref, coarse_ref, vert_ref, side_ref, sside_ref, query_ref, key_ref, value_ref, bias_ref,
    load_sem, route_sem, own_sem, halo_send, halo_recv, meet_sem,
):
    obs, width = feat_ref.shape
    owners = sendf_ref.shape[0]
    slots = owners * 32
    rows, cols, channels = back_ref.shape
    half = cols // 2
    out_rows = rows // 2
    both = 2 * width
    lat_count, lon_count = lax.axis_size("lat"), lax.axis_size("lon")
    lat, lon = lax.axis_index("lat"), lax.axis_index("lon")
    me = lat * lon_count + lon

    loads = [
        pltpu.make_async_copy(src, dst, load_sem.at[i])
        for i, (src, dst) in enumerate(
            ((back_hbm, back_ref), (conv_hbm, conv_ref), (wqkv_hbm, wqkv_ref), (wout_hbm, wout_ref))
        )
    ]
    for load in loads:
        load.start()

    def inside(da):
        return (lat + da >= 0) & (lat + da < lat_count)

    def place(device):
        return device // lon_count, lax.rem(device, lon_count)

    barrier = pltpu.get_barrier_semaphore()
    rounds = owners.bit_length() - 1

    def greet(where):
        pl.semaphore_signal(barrier, inc=1, device_id=where, device_id_type=MESH)

    for da, db in WAYS:
        there = (lat + da, lax.rem(lon + db + lon_count, lon_count))
        if da == 0:
            greet(there)
        else:
            pl.when(inside(da))(lambda: greet(there))
    for k in range(rounds):
        greet(place(me ^ (1 << k)))

    def meet(k):
        pl.semaphore_signal(meet_sem.at[k], inc=1, device_id=place(me ^ (1 << k)), device_id_type=MESH)
        pl.semaphore_wait(meet_sem.at[k], 1)

    def halo(base, parts):
        copies = []
        for i, ((da, db), src, dst) in enumerate(parts):
            copies.append(
                (
                    da,
                    pltpu.make_async_remote_copy(
                        src_ref=src,
                        dst_ref=dst,
                        send_sem=halo_send.at[base + i],
                        recv_sem=halo_recv.at[base + i],
                        device_id=(lat + da, lax.rem(lon + db + lon_count, lon_count)),
                        device_id_type=MESH,
                    ),
                )
            )
        return copies

    def halo_start(copies):
        for da, copy in copies:
            pl.when(inside(da))(copy.start)

    def halo_arrive(copies):
        for da, copy in copies:
            pl.when(inside(-da))(copy.wait_recv)

    def halo_sent(copies):
        for da, copy in copies:
            pl.when(inside(da))(copy.wait_send)

    loads[0].wait()
    for row in range(rows):
        tile = back_ref[row, 0:16, :].astype(F32)
        edge_ref[0, row : row + 1, :] = tile[0:1]
        tile = back_ref[row, cols - 16 : cols, :].astype(F32)
        edge_ref[1, row : row + 1, :] = tile[15:16]

    neighbours = 2 + 3 * (inside(-1).astype(I32) + inside(1).astype(I32))
    pl.semaphore_wait(barrier, rounds + neighbours)

    def fine_parts(first, last, edge, row, side):
        top, bottom = pl.ds(0, 8), pl.ds(rows - 8, 8)
        return (
            ((-1, 0), first, row.at[1]),
            ((1, 0), last, row.at[0]),
            ((0, -1), edge.at[0], side.at[1, pl.ds(8, rows)]),
            ((0, 1), edge.at[1], side.at[0, pl.ds(8, rows)]),
            ((-1, -1), edge.at[0, top], side.at[1, pl.ds(8 + rows, 8)]),
            ((-1, 1), edge.at[1, top], side.at[0, pl.ds(8 + rows, 8)]),
            ((1, -1), edge.at[0, bottom], side.at[1, pl.ds(0, 8)]),
            ((1, 1), edge.at[1, bottom], side.at[0, pl.ds(0, 8)]),
        )

    halo_back = halo(0, fine_parts(back_ref.at[0], back_ref.at[rows - 1], edge_ref, brow_ref, bside_ref))
    halo_start(halo_back)

    step = 256
    upper = (iota((step, step), 0) < iota((step, step), 1)).astype(F32).astype(BF16)
    running = jnp.zeros((owners, 1), F32)
    for at in range(0, obs, step):
        dest = dest_ref[:, at : at + step]
        member = (iota((owners, step), 0) == dest).astype(F32)
        earlier = dot(member.astype(BF16), upper) + running
        rank = jnp.sum(member * earlier, axis=0, keepdims=True)
        running = running + jnp.sum(member, axis=1, keepdims=True)
        local_ref[:, at : at + step] = (dest & 15) * 32 + rank.astype(I32)
        for more in range(0, step, 128):
            group_ref[at + more : at + more + 128, :] = column(dest[:, more : more + 128] >> 4)
        if at // step < rounds:
            meet(at // step)
    one_hot(pick_ref, local_ref[...], jnp.ones((), BF16))

    dest, cell, sub = dest_ref[...], cell_ref[...], sub_ref[...]
    same = iota((8, obs), 0) == (dest >> 4)
    meta = jnp.concatenate(
        [jnp.where(same, value, 0) for value in ((cell >> 7) + 1, cell & 127, sub, dest * 0)], axis=0
    )
    meta = dot_t(narrow(meta), pick_ref[...])
    code = (meta[0:8] * 128.0 + meta[8:16]).astype(I32) * 256 + meta[16:24].astype(I32)
    mine = iota((8, 128), 1) // 32 == lon
    for c in range(4):
        chunk = code[:, c * 128 : c * 128 + 128]
        turned = [chunk] + [pltpu.roll(chunk, 32 * k, 1) for k in range(1, 4)]
        for j in range(4):
            near = (lon - j) & 3
            placed = jnp.where(
                near < 2,
                jnp.where(near == 0, turned[0], turned[1]),
                jnp.where(near == 2, turned[2], turned[3]),
            )
            placed = jnp.where(mine, placed, 0)
            for g in range(8):
                sendm_ref[g * 16 + c * 4 + j] = placed[g : g + 1]

    for k in range(obs // step, rounds):
        meet(k)

    @pl.loop(0, owners // 32)
    def _(turn):
        part = lax.rem(turn + me // 32, owners // 32)
        group = group_ref[...]
        feat = feat_ref[...]
        wide = jnp.concatenate(
            [
                jnp.where(
                    group == jnp.full((1, 1), 2 * part + i, I32).astype(F32).astype(BF16),
                    feat,
                    jnp.zeros((), BF16),
                )
                for i in range(2)
            ],
            axis=1,
        )
        packed = dot(pick_ref[...], wide).astype(BF16)
        for i in range(2):
            sendf_ref[pl.ds(part * 32 + i * 16, 16)] = packed[:, i * width : (i + 1) * width].reshape(
                16, 32, width
            )

        @pl.loop(0, 32)
        def _(k):
            peer = part * 32 + k

            @pl.when(peer != me)
            def _():
                there = (peer // lon_count, lax.rem(peer, lon_count))
                for i, (src, dst) in enumerate(((sendf_ref, recvf_ref), (sendm_ref, recvm_ref))):
                    pltpu.make_async_remote_copy(
                        src_ref=src.at[peer],
                        dst_ref=dst.at[me],
                        send_sem=route_sem.at[i],
                        recv_sem=route_sem.at[2 + i],
                        device_id=there,
                        device_id_type=MESH,
                    ).start()

    own_copies = [
        pltpu.make_async_copy(src.at[me], dst.at[me], own_sem.at[i])
        for i, (src, dst) in enumerate(((sendf_ref, recvf_ref), (sendm_ref, recvm_ref)))
    ]
    for copy in own_copies:
        copy.start()

    @pl.when(lat == 0)
    def _():
        brow_ref[0] = jnp.zeros((cols, channels), BF16)
        bside_ref[:, 0:8, :] = jnp.zeros((2, 8, channels), F32)
        orow_ref[0] = jnp.zeros((cols, both), BF16)
        oside_ref[:, 0:8, :] = jnp.zeros((2, 8, both), F32)
        vert_ref[0] = jnp.zeros((6, half, channels), BF16)
        side_ref[:, 0:3] = jnp.zeros((2, 3, 16, channels), BF16)

    @pl.when(lat == lat_count - 1)
    def _():
        brow_ref[1] = jnp.zeros((cols, channels), BF16)
        bside_ref[:, 8 + rows :, :] = jnp.zeros((2, 8, channels), F32)
        orow_ref[1] = jnp.zeros((cols, both), BF16)
        oside_ref[:, 8 + rows :, :] = jnp.zeros((2, 8, both), F32)
        vert_ref[1] = jnp.zeros((6, half, channels), BF16)
        side_ref[:, 9:12] = jnp.zeros((2, 3, 16, channels), BF16)

    halo_arrive(halo_back)

    def lay(taps, buffer, slot, at, line, left, right):
        size = line.shape[1]
        for c in range(size // 128):
            lanes = slice(c * 128, (c + 1) * 128)
            spot = slot * (size // 128) + c
            buffer[spot, 8 : 8 + cols, :] = line[:, lanes].astype(F32)
            if left is not None:
                buffer[spot, 7:8, :] = left[:, lanes]
                buffer[spot, 8 + cols : 9 + cols, :] = right[:, lanes]
            for tap in range(4):
                part = buffer[spot, pl.ds(7 + tap, half, stride=2), :]
                base = tap * size + c * 128
                taps[at, :, base : base + 128] = part.astype(BF16)

    for i, at in ((0, 0), (1, rows + 1)):
        lay(
            taps_ref, line_ref, i, at, brow_ref[i],
            bside_ref[0, at + 7 : at + 8, :], bside_ref[1, at + 7 : at + 8, :],
        )

    @pl.loop(0, rows // 2)
    def _(pair):
        for i in range(2):
            row = pair * 2 + i
            lay(
                taps_ref, line_ref, i, row + 1, back_ref[row],
                bside_ref[0, pl.ds(row + 8, 1), :], bside_ref[1, pl.ds(row + 8, 1), :],
            )

    loads[1].wait()
    block = 4 * half

    def window(taps, part, tap):
        return taps[pl.ds(part * 4 + tap // 2, 4), tap % 2].reshape(block, taps.shape[3])

    taps4 = taps_ref.reshape(rows // 2 + 1, 2, half, 4 * channels)
    otaps4 = otaps_ref.reshape(rows // 2 + 1, 2, half, 4 * both)

    @pl.loop(0, out_rows // 4)
    def _(part):
        total = jnp.broadcast_to(bias_in_ref[...], (block, channels))
        for tap in range(4):
            total = total + dot(window(taps4, part, tap), conv_ref[tap])
        acc_ref[pl.ds(pl.multiple_of(part * block, block), block), :] = total

    dens = jnp.broadcast_to(dens_ref[...], (16, channels))
    dens_hi = dens.astype(BF16)
    dens_lo = (dens - dens_hi.astype(F32)).astype(BF16)
    line16 = iota((16, channels), 0)
    tail = jnp.where(
        line16 == 0, dens_hi.astype(F32), jnp.where(line16 == 1, dens_lo.astype(F32), 0.0)
    ).astype(BF16)
    lift = jnp.concatenate([win_ref[...], tail], axis=0)

    @pl.loop(0, 4)
    def _(tap):
        for s in range(4):
            made = dot(lift, conv_ref[tap, s * channels : (s + 1) * channels, :])
            base = s * both
            comp_ref[tap, base : base + width, :] = made[:width].astype(BF16)
            whole = made[width : width + 1] + made[width + 1 : width + 2]
            upper_part = whole.astype(BF16).astype(F32)
            rest = jnp.where(
                line16 < 2, upper_part, jnp.where(line16 == 2, whole - upper_part, 0.0)
            ).astype(BF16)
            comp_ref[tap, base + width : base + width + 16, :] = rest
            comp_ref[tap, base + width + 16 : base + both, :] = jnp.zeros(
                (width - 16, channels), BF16
            )

    for copy in own_copies:
        copy.wait()
    rest = pl.ds(0, owners - 1)
    for i, (src, dst) in enumerate(((sendf_ref, recvf_ref), (sendm_ref, recvm_ref))):
        pltpu.make_async_copy(src.at[rest], dst.at[rest], route_sem.at[i]).wait()
        pltpu.make_async_copy(src.at[rest], dst.at[rest], route_sem.at[2 + i]).wait()
    for group in range(owners // 4):
        code = recvm_ref[group * 4]
        for other in range(1, 4):
            code = code + recvm_ref[group * 4 + other]
        codes_ref[:, group * 128 : group * 128 + 128] = code

    chunk = spread_ref.shape[0]
    lane = narrow(iota((128, 128), 1))
    for c in range(slots // chunk):
        code = codes_ref[:, c * chunk : (c + 1) * chunk]
        sub = code & 255
        cell = (code >> 8) - 128
        row_off = ((sub >> 4).astype(F32) + 0.5) / 16.0 - 0.5
        col_off = ((sub & 15).astype(F32) + 0.5) / 16.0 - 0.5
        kern = jnp.exp(-(row_off * row_off + col_off * col_off) / (2.0 * 0.35 * 0.35))
        one_hot(pick_ref, cell & 511, kern.astype(BF16))
        band = cell >> 9
        for b in range(chunk // 128):
            spot = column(band[:, b * 128 : b * 128 + 128])
            first = (c * chunk + b * 128) // 32
            feat = recvf_ref[first : first + 4].reshape(128, width)
            lines = slice(b * 128, b * 128 + 128)
            for g in range(rows // 4):
                here = jnp.full((1, 1), g, F32).astype(BF16)
                spread_ref[lines, g * width : (g + 1) * width] = jnp.where(
                    spot == here, feat, jnp.zeros((), BF16)
                )
            spread_ref[lines, rows // 4 * width :] = jnp.where(
                spot == lane, jnp.ones((), BF16), jnp.zeros((), BF16)
            )
        part = dot(pick_ref[...], spread_ref[...])
        sums_ref[...] = part if c == 0 else sums_ref[...] + part

    lane_f = iota((cols, width), 1)
    for g in range(rows // 4):
        for r in range(4):
            row = g * 4 + r
            lines = slice(r * cols, (r + 1) * cols)
            density = sums_ref[lines, rows // 4 * width + g : rows // 4 * width + g + 1]
            normed = sums_ref[lines, g * width : (g + 1) * width] / (density + 1.0)
            high = density.astype(BF16).astype(F32)
            marks = jnp.where(
                (lane_f == 0) | (lane_f == 2), high, jnp.where(lane_f == 1, density - high, 0.0)
            )
            line = jnp.concatenate([normed, marks], axis=1)
            oedge_ref[0, row : row + 1, :] = line[0:1]
            oedge_ref[1, row : row + 1, :] = line[cols - 1 : cols]
            if row == 0:
                orow_ref[2] = line.astype(BF16)
            if row == rows - 1:
                orow_ref[3] = line.astype(BF16)
            lay(otaps_ref, oline_ref, row % 2, row + 1, line, None, None)

    halo_obs = halo(8, fine_parts(orow_ref.at[2], orow_ref.at[3], oedge_ref, orow_ref, oside_ref))
    halo_start(halo_obs)

    middle = slice(both, 3 * both)
    for part in (1, 0, 2):
        lines = slice(part * block, (part + 1) * block)
        total = acc_ref[lines, :]
        for tap in range(4):
            if (part, tap) not in ((0, 0), (out_rows // 4 - 1, 3)):
                total = total + dot(window(otaps4, part, tap)[:, middle], comp_ref[tap, middle, :])
        acc_ref[lines, :] = total

    for down in range(out_rows // 4):
        key_row = lat * out_rows - 6 + down * 4 + iota((1, 512), 1) // 32
        beyond = jnp.where((key_row >= 0) & (key_row < lat_count * out_rows), 0.0, NEG)
        for h in range(HEADS):
            strip = jnp.broadcast_to(strip_ref[h : h + 1, :], (16, 512))
            for r in range(4):
                at = h * 64 + r * 16
                bias_ref[down, at : at + 16, :] = (
                    pltpu.roll(strip, 2 + 32 * r, 1, stride=1, stride_axis=0) + beyond
                )

    halo_arrive(halo_obs)
    for i, at in ((0, 0), (1, rows + 1)):
        lay(otaps_ref, oline_ref, i, at, orow_ref[i], None, None)
    first_line = iota((16, both), 0) == 0
    last_line = iota((16, both), 0) == 15
    for at in range(rows + 2):
        old = otaps_ref[at, 0:16, 0:both].astype(F32)
        otaps_ref[at, 0:16, 0:both] = jnp.where(
            first_line, oside_ref[0, at + 7 : at + 8, :], old
        ).astype(BF16)
        old = otaps_ref[at, half - 16 : half, 3 * both :].astype(F32)
        otaps_ref[at, half - 16 : half, 3 * both :] = jnp.where(
            last_line, oside_ref[1, at + 7 : at + 8, :], old
        ).astype(BF16)

    loads[2].wait()
    loads[3].wait()

    outer = (slice(0, both), slice(3 * both, 4 * both))

    def finish(part):
        lines = slice(part * block, (part + 1) * block)
        total = acc_ref[lines, :]
        for tap in range(4):
            view = window(otaps4, part, tap)
            if (part, tap) in ((0, 0), (out_rows // 4 - 1, 3)):
                total = total + dot(view, comp_ref[tap])
            else:
                for lanes in outer:
                    total = total + dot(view[:, lanes], comp_ref[tap, lanes, :])
        inner = 0.7978845608028654 * (total + 0.044715 * total * total * total)
        coarse = (0.5 * total * (1.0 + jnp.tanh(inner))).astype(BF16)
        coarse_ref[part * 4 : part * 4 + 4] = coarse.reshape(4, half, channels)
        value = coarse.astype(F32)
        scale = lax.rsqrt(jnp.mean(value * value, axis=1, keepdims=True) + 1e-05)
        normed = value * scale * gain_ref[...]
        own_ref[part * 4 : part * 4 + 4] = normed.astype(BF16).reshape(4, half, channels)
        for side, at in ((0, 0), (1, half - 8)):
            for pair in range(2):
                first = pair * 2 * half + at
                both_rows = jnp.concatenate(
                    [normed[first : first + 8], normed[first + half : first + half + 8]], axis=0
                )
                sside_ref[side, part * 2 + pair] = both_rows.astype(BF16)

    def rim(first, count, side):
        return sside_ref.at[side, pl.ds(first, count)]

    def gap(first, count, side):
        return side_ref.at[side, pl.ds(first, count)]

    finish(0)
    halo_first = halo(
        16,
        (
            ((-1, 0), own_ref.at[pl.ds(0, 4)], vert_ref.at[1, pl.ds(0, 4)]),
            ((0, -1), rim(0, 2, 0), gap(3, 2, 1)),
            ((0, 1), rim(0, 2, 1), gap(3, 2, 0)),
            ((-1, -1), rim(0, 2, 0), gap(9, 2, 1)),
            ((-1, 1), rim(0, 2, 1), gap(9, 2, 0)),
        ),
    )
    halo_start(halo_first)
    finish(2)
    halo_second = halo(
        21,
        (
            ((1, 0), own_ref.at[pl.ds(8, 4)], vert_ref.at[0, pl.ds(2, 4)]),
            ((0, -1), rim(4, 2, 0), gap(7, 2, 1)),
            ((0, 1), rim(4, 2, 1), gap(7, 2, 0)),
            ((1, -1), rim(4, 2, 0), gap(1, 2, 1)),
            ((1, 1), rim(4, 2, 1), gap(1, 2, 0)),
        ),
    )
    halo_start(halo_second)
    finish(1)
    halo_third = halo(
        26,
        (
            ((-1, 0), own_ref.at[pl.ds(4, 2)], vert_ref.at[1, pl.ds(4, 2)]),
            ((1, 0), own_ref.at[pl.ds(6, 2)], vert_ref.at[0, pl.ds(0, 2)]),
            ((0, -1), rim(2, 2, 0), gap(5, 2, 1)),
            ((0, 1), rim(2, 2, 1), gap(5, 2, 0)),
            ((-1, -1), rim(2, 1, 0), gap(11, 1, 1)),
            ((-1, 1), rim(2, 1, 1), gap(11, 1, 0)),
            ((1, -1), rim(3, 1, 0), gap(0, 1, 1)),
            ((1, 1), rim(3, 1, 1), gap(0, 1, 0)),
        ),
    )
    halo_start(halo_third)
    halo_norm = halo_first + halo_second + halo_third

    def keys_values(x, lead):
        made = dot(x.reshape(lead * x.shape[1], channels), wqkv_ref[:, channels:])
        made = made.reshape(lead, x.shape[1], 2 * channels)
        return made[:, :, :channels], made[:, :, channels:]

    @pl.loop(0, out_rows // 4)
    def _(part):
        own = own_ref[pl.ds(part * 4, 4)]
        query = dot(own.reshape(block, channels), wqkv_ref[:, :channels]).astype(BF16) * 0.125
        query_ref[pl.ds(part * 4, 4)] = query.astype(BF16).reshape(4, half, channels)
        key, value = keys_values(own, 4)
        key_ref[pl.ds(part * 4 + 6, 4), 8 : 8 + half, :] = key.astype(BF16)
        value_ref[pl.ds(part * 4 + 6, 4), 8 : 8 + half, :] = value.astype(BF16)

    halo_arrive(halo_norm)
    for i, at in ((0, 0), (1, 6 + out_rows)):
        key, value = keys_values(vert_ref[i], 6)
        key_ref[at : at + 6, 8 : 8 + half, :] = key.astype(BF16)
        value_ref[at : at + 6, 8 : 8 + half, :] = value.astype(BF16)
    for i, at in ((0, 0), (1, 8 + half)):
        key, value = keys_values(side_ref[i], out_rows // 2 + 6)
        shape = (out_rows + 12, 8, channels)
        key_ref[:, at : at + 8, :] = key.reshape(shape).astype(BF16)
        value_ref[:, at : at + 8, :] = value.reshape(shape).astype(BF16)

    half_ch = channels // 2
    lane_head = iota((64, half_ch), 1) // (channels // HEADS)

    @pl.loop(0, out_rows // 4)
    def _(down):
        @pl.loop(0, half // 16)
        def _(across):
            c0 = pl.multiple_of(across * 16, 16)
            query = query_ref[pl.ds(down * 4, 4), pl.ds(c0, 16), :].reshape(64, channels)
            parts = []
            for g in range(2):
                lanes = slice(g * half_ch, (g + 1) * half_ch)
                keys = key_ref[pl.ds(down * 4, 16), pl.ds(c0, 32), lanes].reshape(512, half_ch)
                values = value_ref[pl.ds(down * 4, 16), pl.ds(c0, 32), lanes].reshape(512, half_ch)
                wide = query[:, lanes]
                masked = jnp.concatenate(
                    [jnp.where(lane_head == h, wide, jnp.zeros((), BF16)) for h in range(4)], axis=0
                )
                scores = dot_t(masked, keys)
                scores = scores + bias_ref[down, g * 256 : (g + 1) * 256, :]
                peak = jnp.max(scores, axis=1, keepdims=True)
                weight = jnp.exp(scores - peak)
                norm = jnp.sum(weight, axis=1, keepdims=True)
                mixed = dot(weight.astype(BF16), values) * (1.0 / norm)
                total = jnp.zeros((64, half_ch), F32)
                for h in range(4):
                    total = jnp.where(lane_head == h, mixed[h * 64 : (h + 1) * 64], total)
                parts.append(total.astype(BF16))
            attended = jnp.concatenate(parts, axis=1)
            lifted = dot(attended, wout_ref[...])
            base = coarse_ref[pl.ds(down * 4, 4), pl.ds(c0, 16), :].astype(F32)
            result = base + lifted.reshape(4, 16, channels)
            out_ref[pl.ds(down * 4, 4), pl.ds(c0, 16), :] = result.astype(BF16)

    for copies in (halo_back, halo_obs, halo_norm):
        halo_sent(copies)


def body(
    obs_feat, obs_dest, obs_cell, obs_sub, background, w_in, dens_vec,
    conv_w, conv_b, norm_gain, w_qkv, rel_bias, w_out,
):
    owners = lax.axis_size("lat") * lax.axis_size("lon")
    rows, cols, channels = background.shape
    obs, width = obs_feat.shape
    half, out_rows, both = cols // 2, rows // 2, 2 * width
    strip = jnp.pad(rel_bias, ((0, 0), (0, 3), (0, 19)), constant_values=NEG).reshape(HEADS, 512)
    vmem = pl.BlockSpec(memory_space=pltpu.VMEM)
    hbm = pl.BlockSpec(memory_space=pl.ANY)
    scratch = [
        ((rows, cols, channels), BF16),
        ((4, 4 * channels, channels), BF16),
        ((channels, 3 * channels), BF16),
        ((channels, channels), BF16),
        ((owners, 32, width), BF16),
        ((owners, 1, 128), I32),
        ((owners, 32, width), BF16),
        ((owners, 1, 128), I32),
        ((512, obs), BF16),
        ((obs, width), BF16),
        ((1, obs), I32),
        ((2, rows, channels), F32),
        ((2, cols, channels), BF16),
        ((2, rows + 16, channels), F32),
        ((2 * channels // 128, cols + 16, 128), F32),
        ((rows + 2, half, 4 * channels), BF16),
        ((half * out_rows, channels), F32),
        ((4, 4 * both, channels), BF16),
        ((1, owners * 32), I32),
        ((obs, rows // 4 * width + 128), BF16),
        ((512, rows // 4 * width + 128), F32),
        ((2, rows, both), F32),
        ((2 * both // 128, cols + 16, 128), F32),
        ((4, cols, both), BF16),
        ((2, rows + 16, both), F32),
        ((rows + 2, half, 4 * both), BF16),
        ((out_rows, half, channels), BF16),
        ((out_rows, half, channels), BF16),
        ((2, 6, half, channels), BF16),
        ((2, out_rows // 2 + 6, 16, channels), BF16),
        ((2, out_rows // 2, 16, channels), BF16),
        ((out_rows, half, channels), BF16),
        ((out_rows + 12, half + 16, channels), BF16),
        ((out_rows + 12, half + 16, channels), BF16),
        ((out_rows // 4, HEADS * 64, 512), F32),
    ]
    sems = [pltpu.SemaphoreType.DMA((n,)) for n in (4, 4, 2, 34, 34)]
    sems.append(pltpu.SemaphoreType.REGULAR((owners.bit_length() - 1,)))
    return pl.pallas_call(
        main_kernel,
        name="main",
        out_shape=jax.ShapeDtypeStruct((out_rows, half, channels), BF16),
        in_specs=[vmem, vmem, vmem, vmem, hbm, vmem, vmem, hbm, vmem, vmem, hbm, vmem, hbm],
        out_specs=vmem,
        scratch_shapes=[pltpu.VMEM(shape, dtype) for shape, dtype in scratch] + sems,
        compiler_params=pltpu.CompilerParams(
            collective_id=0, has_side_effects=True, vmem_limit_bytes=62 << 20
        ),
    )(
        obs_dest.reshape(1, obs),
        obs_cell.reshape(1, obs),
        obs_sub.reshape(1, obs),
        obs_feat,
        background,
        w_in,
        dens_vec.reshape(1, channels),
        conv_w.reshape(4, 4 * channels, channels),
        conv_b.reshape(1, channels),
        norm_gain.reshape(1, channels),
        w_qkv,
        strip,
        w_out,
    )


def solution(mesh):
    split = P(("lat", "lon"))
    wide = P(("lat", "lon"), None)
    tile = P("lat", "lon", None)
    in_specs = (wide, wide, split, split, tile) + (P(),) * 8
    return jax.shard_map(body, mesh=mesh, in_specs=in_specs, out_specs=tile, check_vma=False)
```

```python
import jax
import jax.numpy as jnp
from jax import lax
from jax.experimental import pallas as pl
from jax.experimental.pallas import tpu as pltpu
from jax.sharding import PartitionSpec as P

HEADS = 8
F32 = jnp.float32
BF16 = jnp.bfloat16
I32 = jnp.int32
NEG = -1e30
MESH = pl.DeviceIdType.MESH
WAYS = ((-1, 0), (1, 0), (0, -1), (0, 1), (-1, -1), (-1, 1), (1, -1), (1, 1))


def iota(shape, dim):
    return lax.broadcasted_iota(I32, shape, dim)


def narrow(x):
    return x.astype(F32).astype(BF16)


def dot(x, y):
    return jnp.dot(x, y, preferred_element_type=F32)


def dot_t(x, y):
    return lax.dot_general(x, y, (((1,), (1,)), ((), ())), preferred_element_type=F32)


def column(row):
    return jnp.broadcast_to(row.astype(F32), (128, 128)).T.astype(BF16)


def one_hot(place_ref, index, value):
    for part in range(place_ref.shape[0] // 256):
        local = index - part * 256
        local = narrow(jnp.where((local >= 0) & (local < 256), local, -1))
        line = narrow(iota((256, index.shape[1]), 0))
        place_ref[part * 256 : part * 256 + 256, :] = jnp.where(
            line == local, value, jnp.zeros((), BF16)
        )


def main_kernel(
    dest_ref, cell_ref, sub_ref, feat_ref, back_hbm, win_ref, dens_ref, conv_hbm, bias_in_ref,
    gain_ref, wqkv_hbm, strip_ref, wout_hbm,
    out_ref,
    back_ref, conv_ref, wqkv_ref, wout_ref,
    sendf_ref, sendm_ref, recvf_ref, recvm_ref, pick_ref, group_ref, local_ref,
    edge_ref, brow_ref, bside_ref, line_ref, taps_ref, acc_ref, comp_ref,
    codes_ref, spread_ref, sums_ref, oedge_ref, oline_ref, orow_ref, oside_ref, otaps_ref,
    own_ref, coarse_ref, vert_ref, side_ref, sside_ref, query_ref, ext_ref, bias_ref, rim_ref,
    far_ref, turned_ref, held_ref, stat_ref,
    load_sem, route_sem, own_sem, halo_send, halo_recv, meet_sem,
):
    obs, width = feat_ref.shape
    owners = sendf_ref.shape[0]
    slots = owners * 32
    rows, cols, channels = back_ref.shape
    half = cols // 2
    out_rows = rows // 2
    both = 2 * width
    lat_count, lon_count = lax.axis_size("lat"), lax.axis_size("lon")
    lat, lon = lax.axis_index("lat"), lax.axis_index("lon")
    me = lat * lon_count + lon

    loads = [
        pltpu.make_async_copy(src, dst, load_sem.at[i])
        for i, (src, dst) in enumerate(
            ((back_hbm, back_ref), (conv_hbm, conv_ref), (wqkv_hbm, wqkv_ref), (wout_hbm, wout_ref))
        )
    ]
    for load in loads:
        load.start()

    def inside(da):
        return (lat + da >= 0) & (lat + da < lat_count)

    def place(device):
        return device // lon_count, lax.rem(device, lon_count)

    barrier = pltpu.get_barrier_semaphore()
    near = [me ^ j for j in range(1, 16)]
    far = [me ^ (16 * j) for j in range(1, owners // 16)]

    def greet(where):
        pl.semaphore_signal(barrier, inc=1, device_id=where, device_id_type=MESH)

    for da, db in WAYS:
        there = (lat + da, lax.rem(lon + db + lon_count, lon_count))
        if da == 0:
            greet(there)
        else:
            pl.when(inside(da))(lambda: greet(there))
    for device in near + far:
        greet(place(device))

    def halo(base, parts):
        copies = []
        for i, ((da, db), src, dst) in enumerate(parts):
            copies.append(
                (
                    da,
                    pltpu.make_async_remote_copy(
                        src_ref=src,
                        dst_ref=dst,
                        send_sem=halo_send.at[base + i],
                        recv_sem=halo_recv.at[base + i],
                        device_id=(lat + da, lax.rem(lon + db + lon_count, lon_count)),
                        device_id_type=MESH,
                    ),
                )
            )
        return copies

    def halo_start(copies):
        for da, copy in copies:
            pl.when(inside(da))(copy.start)

    def halo_arrive(copies):
        for da, copy in copies:
            pl.when(inside(-da))(copy.wait_recv)

    def halo_sent(copies):
        for da, copy in copies:
            pl.when(inside(da))(copy.wait_send)

    loads[0].wait()
    for row in range(rows):
        tile = back_ref[row, 0:16, :].astype(F32)
        edge_ref[0, row : row + 1, :] = tile[0:1]
        tile = back_ref[row, cols - 16 : cols, :].astype(F32)
        edge_ref[1, row : row + 1, :] = tile[15:16]

    neighbours = 2 + 3 * (inside(-1).astype(I32) + inside(1).astype(I32))
    pl.semaphore_wait(barrier, len(near) + len(far) + neighbours)
    for device in far:
        pl.semaphore_signal(meet_sem, inc=1, device_id=place(device), device_id_type=MESH)

    def fine_parts(first, last, edge, row, side):
        top, bottom = pl.ds(0, 8), pl.ds(rows - 8, 8)
        return (
            ((-1, 0), first, row.at[1]),
            ((1, 0), last, row.at[0]),
            ((0, -1), edge.at[0], side.at[1, pl.ds(8, rows)]),
            ((0, 1), edge.at[1], side.at[0, pl.ds(8, rows)]),
            ((-1, -1), edge.at[0, top], side.at[1, pl.ds(8 + rows, 8)]),
            ((-1, 1), edge.at[1, top], side.at[0, pl.ds(8 + rows, 8)]),
            ((1, -1), edge.at[0, bottom], side.at[1, pl.ds(0, 8)]),
            ((1, 1), edge.at[1, bottom], side.at[0, pl.ds(0, 8)]),
        )

    halo_back = halo(0, fine_parts(back_ref.at[0], back_ref.at[rows - 1], edge_ref, brow_ref, bside_ref))
    halo_start(halo_back)

    step = 256
    upper = (iota((step, step), 0) < iota((step, step), 1)).astype(F32).astype(BF16)
    running = jnp.zeros((owners, 1), F32)
    for at in range(0, obs, step):
        dest = dest_ref[:, at : at + step]
        member = (iota((owners, step), 0) == dest).astype(F32)
        earlier = dot(member.astype(BF16), upper) + running
        rank = jnp.sum(member * earlier, axis=0, keepdims=True)
        running = running + jnp.sum(member, axis=1, keepdims=True)
        local_ref[:, at : at + step] = (dest >> 3) * 32 + rank.astype(I32)
        for more in range(0, step, 128):
            group_ref[at + more : at + more + 128, :] = column(dest[:, more : more + 128] & 7)
    one_hot(pick_ref, local_ref[...], jnp.ones((), BF16))

    dest, cell, sub = dest_ref[...], cell_ref[...], sub_ref[...]
    same = iota((8, obs), 0) == (dest & 7)
    meta = jnp.concatenate(
        [jnp.where(same, value, 0) for value in ((cell >> 7) + 1, cell & 127, sub, dest * 0)], axis=0
    )
    meta = dot_t(narrow(meta), pick_ref[...])
    code = (meta[0:8] * 128.0 + meta[8:16]).astype(I32) * 256 + meta[16:24].astype(I32)
    mine = iota((8, 128), 1) // 32 == lon
    for c in range(4):
        chunk = code[:, c * 128 : c * 128 + 128]
        turned = [chunk] + [pltpu.roll(chunk, 32 * k, 1) for k in range(1, 4)]
        for j in range(4):
            near = (lon - j) & 3
            placed = jnp.where(
                near < 2,
                jnp.where(near == 0, turned[0], turned[1]),
                jnp.where(near == 2, turned[2], turned[3]),
            )
            placed = jnp.where(mine, placed, 0)
            for g in range(8):
                sendm_ref[g * 16 + c * 4 + j] = placed[g : g + 1]

    pl.semaphore_wait(meet_sem, len(far))

    @pl.loop(0, owners // 32)
    def _(turn):
        part = lax.rem(turn + me + me // 4, owners // 32)
        group = group_ref[...]
        feat = feat_ref[...]
        wide = jnp.concatenate(
            [
                jnp.where(
                    group == jnp.full((1, 1), 2 * part + i, I32).astype(F32).astype(BF16),
                    feat,
                    jnp.zeros((), BF16),
                )
                for i in range(2)
            ],
            axis=1,
        )
        packed = dot(pick_ref[...], wide).astype(BF16)
        for i in range(2):
            sendf_ref[pl.ds((part * 2 + i) * 16, 16)] = packed[:, i * width : (i + 1) * width].reshape(
                16, 32, width
            )

        @pl.loop(0, 32)
        def _(k):
            turned = lax.rem(k * 5 + me, 32)
            group = part * 2 + lax.rem(turned, 2)
            peer = (turned // 2) * 8 + group

            @pl.when(peer != me)
            def _():
                there = place(peer)
                slot = group * 16 + turned // 2
                for i, (src, dst) in enumerate(((sendf_ref, recvf_ref), (sendm_ref, recvm_ref))):
                    pltpu.make_async_remote_copy(
                        src_ref=src.at[slot],
                        dst_ref=dst.at[me],
                        send_sem=route_sem.at[i],
                        recv_sem=route_sem.at[2 + i],
                        device_id=there,
                        device_id_type=MESH,
                    ).start()

    own_copies = [
        pltpu.make_async_copy(src.at[lax.rem(me, 8) * 16 + me // 8], dst.at[me], own_sem.at[i])
        for i, (src, dst) in enumerate(((sendf_ref, recvf_ref), (sendm_ref, recvm_ref)))
    ]
    for copy in own_copies:
        copy.start()

    @pl.when(lat == 0)
    def _():
        brow_ref[0] = jnp.zeros((cols, channels), BF16)
        bside_ref[:, 0:8, :] = jnp.zeros((2, 8, channels), F32)
        orow_ref[0] = jnp.zeros((cols, both), BF16)
        oside_ref[:, 0:8, :] = jnp.zeros((2, 8, both), F32)
        vert_ref[0] = jnp.zeros((6, half, channels), BF16)
        side_ref[:, 0:3] = jnp.zeros((2, 3, 16, channels), BF16)

    @pl.when(lat == lat_count - 1)
    def _():
        brow_ref[1] = jnp.zeros((cols, channels), BF16)
        bside_ref[:, 8 + rows :, :] = jnp.zeros((2, 8, channels), F32)
        orow_ref[1] = jnp.zeros((cols, both), BF16)
        oside_ref[:, 8 + rows :, :] = jnp.zeros((2, 8, both), F32)
        vert_ref[1] = jnp.zeros((6, half, channels), BF16)
        side_ref[:, 9:12] = jnp.zeros((2, 3, 16, channels), BF16)

    halo_arrive(halo_back)

    def lay(taps, buffer, slot, at, line, left, right):
        size = line.shape[1]
        for c in range(size // 128):
            lanes = slice(c * 128, (c + 1) * 128)
            spot = slot * (size // 128) + c
            buffer[spot, 8 : 8 + cols, :] = line[:, lanes].astype(F32)
            if left is not None:
                buffer[spot, 7:8, :] = left[:, lanes]
                buffer[spot, 8 + cols : 9 + cols, :] = right[:, lanes]
            for tap in range(4):
                part = buffer[spot, pl.ds(7 + tap, half, stride=2), :]
                base = tap * size + c * 128
                taps[at, :, base : base + 128] = part.astype(BF16)

    for i, at in ((0, 0), (1, rows + 1)):
        lay(
            taps_ref, line_ref, i, at, brow_ref[i],
            bside_ref[0, at + 7 : at + 8, :], bside_ref[1, at + 7 : at + 8, :],
        )

    @pl.loop(0, rows // 2)
    def _(pair):
        for i in range(2):
            row = pair * 2 + i
            lay(
                taps_ref, line_ref, i, row + 1, back_ref[row],
                bside_ref[0, pl.ds(row + 8, 1), :], bside_ref[1, pl.ds(row + 8, 1), :],
            )

    loads[1].wait()
    block = 4 * half

    def window(taps, part, tap):
        return taps[pl.ds(part * 4 + tap // 2, 4), tap % 2].reshape(block, taps.shape[3])

    taps4 = taps_ref.reshape(rows // 2 + 1, 2, half, 4 * channels)
    otaps4 = otaps_ref.reshape(rows // 2 + 1, 2, half, 4 * both)

    @pl.loop(0, out_rows // 4)
    def _(part):
        total = jnp.broadcast_to(bias_in_ref[...], (block, channels))
        for tap in range(4):
            total = total + dot(window(taps4, part, tap), conv_ref[tap])
        acc_ref[pl.ds(pl.multiple_of(part * block, block), block), :] = total

    dens = jnp.broadcast_to(dens_ref[...], (16, channels))
    dens_hi = dens.astype(BF16)
    dens_lo = (dens - dens_hi.astype(F32)).astype(BF16)
    line16 = iota((16, channels), 0)
    tail = jnp.where(
        line16 == 0, dens_hi.astype(F32), jnp.where(line16 == 1, dens_lo.astype(F32), 0.0)
    ).astype(BF16)
    lift = jnp.concatenate([win_ref[...], tail], axis=0)

    @pl.loop(0, 4)
    def _(tap):
        for s in range(4):
            made = dot(lift, conv_ref[tap, s * channels : (s + 1) * channels, :])
            base = s * both
            comp_ref[tap, base : base + width, :] = made[:width].astype(BF16)
            whole = made[width : width + 1] + made[width + 1 : width + 2]
            upper_part = whole.astype(BF16).astype(F32)
            rest = jnp.where(
                line16 < 2, upper_part, jnp.where(line16 == 2, whole - upper_part, 0.0)
            ).astype(BF16)
            comp_ref[tap, base + width : base + width + 16, :] = rest
            comp_ref[tap, base + width + 16 : base + both, :] = jnp.zeros(
                (width - 16, channels), BF16
            )

    loads[2].wait()
    loads[3].wait()
    turned_ref[...] = wqkv_ref[:, 2 * channels :].astype(F32).T.astype(BF16)

    no_up = jnp.where(lat == 0, NEG, 0.0)
    no_down = jnp.where(lat == lat_count - 1, NEG, 0.0)
    lane256 = iota((16, 256), 1)
    for pair in range(HEADS // 2):
        places = slice(pair * 128, pair * 128 + 128)
        for down in range(out_rows // 4):
            inner_part, outer_part = [], []
            for h in (2 * pair, 2 * pair + 1):
                strip = jnp.broadcast_to(strip_ref[h : h + 1, :], (16, 640))
                for r in range(4):

                    def shifted(first_row, lead, size):
                        amount = (2 + 32 * (r + 4 * down - first_row) + lead) % 640
                        return pltpu.roll(strip, amount, 1, stride=1, stride_axis=0)[:, :size]

                    inner_part.append(shifted(6, 0, 384))
                    if down == 0:
                        outer_part.append(shifted(0, 0, 256) + no_up)
                    elif down == 1:
                        outer_part.append(
                            jnp.where(
                                lane256 < 64, shifted(4, 0, 256) + no_up, shifted(18, 64, 256) + no_down
                            )
                        )
                    else:
                        outer_part.append(jnp.where(lane256 < 64, NEG, shifted(18, 64, 256) + no_down))
            bias_ref[down, :, places] = jnp.concatenate(inner_part, axis=0).T
            rim_ref[down, :, places] = jnp.concatenate(outer_part, axis=0).T

    for copy in own_copies:
        copy.wait()
    rest = pl.ds(0, owners - 1)
    for i, (src, dst) in enumerate(((sendf_ref, recvf_ref), (sendm_ref, recvm_ref))):
        pltpu.make_async_copy(src.at[rest], dst.at[rest], route_sem.at[i]).wait()
        pltpu.make_async_copy(src.at[rest], dst.at[rest], route_sem.at[2 + i]).wait()
    for group in range(owners // 4):
        code = recvm_ref[group * 4]
        for other in range(1, 4):
            code = code + recvm_ref[group * 4 + other]
        codes_ref[:, group * 128 : group * 128 + 128] = code

    chunk = spread_ref.shape[0]
    lane = narrow(iota((128, 128), 1))
    for c in range(slots // chunk):
        code = codes_ref[:, c * chunk : (c + 1) * chunk]
        sub = code & 255
        cell = (code >> 8) - 128
        row_off = ((sub >> 4).astype(F32) + 0.5) / 16.0 - 0.5
        col_off = ((sub & 15).astype(F32) + 0.5) / 16.0 - 0.5
        kern = jnp.exp(-(row_off * row_off + col_off * col_off) / (2.0 * 0.35 * 0.35))
        one_hot(pick_ref, cell & 511, kern.astype(BF16))
        band = cell >> 9
        for b in range(chunk // 128):
            spot = column(band[:, b * 128 : b * 128 + 128])
            first = (c * chunk + b * 128) // 32
            feat = recvf_ref[first : first + 4].reshape(128, width)
            lines = slice(b * 128, b * 128 + 128)
            for g in range(rows // 4):
                here = jnp.full((1, 1), g, F32).astype(BF16)
                spread_ref[lines, g * width : (g + 1) * width] = jnp.where(
                    spot == here, feat, jnp.zeros((), BF16)
                )
            spread_ref[lines, rows // 4 * width :] = jnp.where(
                spot == lane, jnp.ones((), BF16), jnp.zeros((), BF16)
            )
        part = dot(pick_ref[...], spread_ref[...])
        sums_ref[...] = part if c == 0 else sums_ref[...] + part

    lane_f = iota((cols, width), 1)
    for g in range(rows // 4):
        for r in range(4):
            row = g * 4 + r
            lines = slice(r * cols, (r + 1) * cols)
            density = sums_ref[lines, rows // 4 * width + g : rows // 4 * width + g + 1]
            normed = sums_ref[lines, g * width : (g + 1) * width] / (density + 1.0)
            high = density.astype(BF16).astype(F32)
            marks = jnp.where(
                (lane_f == 0) | (lane_f == 2), high, jnp.where(lane_f == 1, density - high, 0.0)
            )
            line = jnp.concatenate([normed, marks], axis=1)
            oedge_ref[0, row : row + 1, :] = line[0:1]
            oedge_ref[1, row : row + 1, :] = line[cols - 1 : cols]
            if row == 0:
                orow_ref[2] = line.astype(BF16)
            if row == rows - 1:
                orow_ref[3] = line.astype(BF16)
            lay(otaps_ref, oline_ref, row % 2, row + 1, line, None, None)

    halo_obs = halo(8, fine_parts(orow_ref.at[2], orow_ref.at[3], oedge_ref, orow_ref, oside_ref))
    halo_start(halo_obs)

    middle = slice(both, 3 * both)
    for part in (1, 0, 2):
        lines = slice(part * block, (part + 1) * block)
        total = acc_ref[lines, :]
        for tap in range(4):
            if (part, tap) not in ((0, 0), (out_rows // 4 - 1, 3)):
                total = total + dot(window(otaps4, part, tap)[:, middle], comp_ref[tap, middle, :])
        acc_ref[lines, :] = total

    halo_arrive(halo_obs)
    for i, at in ((0, 0), (1, rows + 1)):
        lay(otaps_ref, oline_ref, i, at, orow_ref[i], None, None)
    first_line = iota((16, both), 0) == 0
    last_line = iota((16, both), 0) == 15
    for at in range(rows + 2):
        old = otaps_ref[at, 0:16, 0:both].astype(F32)
        otaps_ref[at, 0:16, 0:both] = jnp.where(
            first_line, oside_ref[0, at + 7 : at + 8, :], old
        ).astype(BF16)
        old = otaps_ref[at, half - 16 : half, 3 * both :].astype(F32)
        otaps_ref[at, half - 16 : half, 3 * both :] = jnp.where(
            last_line, oside_ref[1, at + 7 : at + 8, :], old
        ).astype(BF16)


    outer = (slice(0, both), slice(3 * both, 4 * both))

    def finish(part):
        lines = slice(part * block, (part + 1) * block)
        total = acc_ref[lines, :]
        for tap in range(4):
            view = window(otaps4, part, tap)
            if (part, tap) in ((0, 0), (out_rows // 4 - 1, 3)):
                total = total + dot(view, comp_ref[tap])
            else:
                for lanes in outer:
                    total = total + dot(view[:, lanes], comp_ref[tap, lanes, :])
        inner = 0.7978845608028654 * (total + 0.044715 * total * total * total)
        coarse = (0.5 * total * (1.0 + jnp.tanh(inner))).astype(BF16)
        coarse_ref[part * 4 : part * 4 + 4] = coarse.reshape(4, half, channels)
        value = coarse.astype(F32)
        scale = lax.rsqrt(jnp.mean(value * value, axis=1, keepdims=True) + 1e-05)
        normed = value * scale * gain_ref[...]
        own_ref[part * 4 : part * 4 + 4] = normed.astype(BF16).reshape(4, half, channels)
        ext_ref[part * 4 : part * 4 + 4, 8 : 8 + half, :] = normed.reshape(4, half, channels).astype(BF16)
        for side, at in ((0, 0), (1, half - 8)):
            for pair in range(2):
                first = pair * 2 * half + at
                both_rows = jnp.concatenate(
                    [normed[first : first + 8], normed[first + half : first + half + 8]], axis=0
                )
                sside_ref[side, part * 2 + pair] = both_rows.astype(BF16)

    def rim(first, count, side):
        return sside_ref.at[side, pl.ds(first, count)]

    def gap(first, count, side):
        return side_ref.at[side, pl.ds(first, count)]

    finish(0)
    halo_first = halo(
        16,
        (
            ((0, -1), rim(0, 2, 0), gap(3, 2, 1)),
            ((0, 1), rim(0, 2, 1), gap(3, 2, 0)),
            ((-1, -1), rim(0, 2, 0), gap(9, 2, 1)),
            ((-1, 1), rim(0, 2, 1), gap(9, 2, 0)),
            ((-1, 0), own_ref.at[pl.ds(0, 4)], vert_ref.at[1, pl.ds(0, 4)]),
        ),
    )
    halo_start(halo_first)
    finish(2)
    halo_second = halo(
        21,
        (
            ((0, -1), rim(4, 2, 0), gap(7, 2, 1)),
            ((0, 1), rim(4, 2, 1), gap(7, 2, 0)),
            ((1, -1), rim(4, 2, 0), gap(1, 2, 1)),
            ((1, 1), rim(4, 2, 1), gap(1, 2, 0)),
            ((1, 0), own_ref.at[pl.ds(8, 4)], vert_ref.at[0, pl.ds(2, 4)]),
        ),
    )
    halo_start(halo_second)
    finish(1)
    halo_third = halo(
        26,
        (
            ((0, -1), rim(2, 2, 0), gap(5, 2, 1)),
            ((0, 1), rim(2, 2, 1), gap(5, 2, 0)),
            ((-1, -1), rim(2, 1, 0), gap(11, 1, 1)),
            ((-1, 1), rim(2, 1, 1), gap(11, 1, 0)),
            ((1, -1), rim(3, 1, 0), gap(0, 1, 1)),
            ((1, 1), rim(3, 1, 1), gap(0, 1, 0)),
            ((-1, 0), own_ref.at[pl.ds(4, 2)], vert_ref.at[1, pl.ds(4, 2)]),
            ((1, 0), own_ref.at[pl.ds(6, 2)], vert_ref.at[0, pl.ds(0, 2)]),
        ),
    )
    halo_start(halo_third)
    halo_norm = halo_first + halo_second + halo_third
    halo_side = halo_first[:2] + halo_second[:2] + halo_third[:2]
    halo_far = halo_first[2:] + halo_second[2:] + halo_third[2:]

    @pl.loop(0, out_rows // 4)
    def _(part):
        own = own_ref[pl.ds(part * 4, 4)].reshape(block, channels)
        query = dot(own, wqkv_ref[:, :channels]).astype(BF16) * 0.125
        query_ref[pl.ds(part * 4, 4)] = query.astype(BF16).reshape(4, half, channels)

    half_ch = channels // 2
    lane_head = iota((64, half_ch), 1) // (channels // HEADS)
    same_half = iota((128, 128), 0) // 64 == iota((128, 128), 1) // 64

    def keys_values(x):
        keys = dot(x, wqkv_ref[:, channels : 2 * channels]).astype(BF16)
        return keys, dot_t(turned_ref[...], x).astype(BF16)

    def queries(down, c0, lanes):
        wide = query_ref[down * 4 : down * 4 + 4, pl.ds(c0, 16), lanes].reshape(64, half_ch)
        return jnp.concatenate(
            [jnp.where(lane_head == h, wide, jnp.zeros((), BF16)) for h in range(4)], axis=0
        )

    def attend_near(across):
        c0 = pl.multiple_of(across * 16, 16)
        keys, values = keys_values(ext_ref[:, pl.ds(c0, 32), :].reshape(32 * out_rows, channels))
        for down in range(out_rows // 4):
            spot = down * (half // 16) + across
            for g in range(2):
                lanes = slice(g * half_ch, (g + 1) * half_ch)
                scores = dot_t(keys[:, lanes], queries(down, c0, lanes)) + bias_ref[down, :, lanes]
                peak = jnp.max(scores, axis=0, keepdims=True)
                weight = jnp.exp(scores - peak)
                stat_ref[spot, 0:1, lanes] = peak
                stat_ref[spot, 1:2, lanes] = jnp.sum(weight, axis=0, keepdims=True)
                mixed = dot(values[lanes], weight.astype(BF16))
                for p in range(2):
                    cut = slice(p * 128, p * 128 + 128)
                    held_ref[spot, g * half_ch + p * 128 : g * half_ch + p * 128 + 128, :] = mixed[cut, cut]

    @pl.loop(1, half // 16 - 1)
    def _(across):
        attend_near(across)

    halo_arrive(halo_side)
    for i, at in ((0, 0), (1, 8 + half)):
        x = side_ref[i, 3 : 3 + out_rows // 2].astype(F32).reshape(out_rows, 8, channels)
        ext_ref[:, at : at + 8, :] = x.astype(BF16)

    @pl.loop(0, 2)
    def _(end):
        attend_near(end * (half // 16 - 1))

    halo_arrive(halo_far)
    for i in range(2):
        seg = slice(0, 3) if i == 0 else slice(3 + out_rows // 2, 6 + out_rows // 2)
        far_ref[i, :, 8 : 8 + half, :] = vert_ref[i].astype(F32).astype(BF16)
        for j, at in ((0, 0), (1, 8 + half)):
            x = side_ref[j, seg].astype(F32).reshape(6, 8, channels)
            far_ref[i, :, at : at + 8, :] = x.astype(BF16)

    @pl.loop(0, half // 16)
    def _(across):
        c0 = pl.multiple_of(across * 16, 16)
        above = far_ref[0, :, pl.ds(c0, 32), :].reshape(192, channels)
        below = far_ref[1, :, pl.ds(c0, 32), :].reshape(192, channels)
        keys, values = keys_values(jnp.concatenate([above[128:], below[:64], above, below], axis=0))
        for down, seg in ((0, slice(128, 320)), (1, slice(0, 128)), (2, slice(256, 512))):
            spot = down * (half // 16) + across
            count = seg.stop - seg.start
            parts = []
            for g in range(2):
                lanes = slice(g * half_ch, (g + 1) * half_ch)
                scores = dot_t(keys[seg, lanes], queries(down, c0, lanes)) + rim_ref[down, :count, lanes]
                old_peak, old_norm = stat_ref[spot, 0:1, lanes], stat_ref[spot, 1:2, lanes]
                peak = jnp.maximum(old_peak, jnp.max(scores, axis=0, keepdims=True))
                weight = jnp.exp(scores - peak)
                fade = jnp.exp(old_peak - peak)
                inverse = 1.0 / (old_norm * fade + jnp.sum(weight, axis=0, keepdims=True))
                fade = fade * inverse
                mixed = dot(values[lanes, seg], weight.astype(BF16))
                for p in range(2):
                    cut = slice(p * 128, p * 128 + 128)
                    held = held_ref[spot, g * half_ch + p * 128 : g * half_ch + p * 128 + 128, :]
                    total = held * fade[:, cut] + mixed[cut, cut] * inverse[:, cut]
                    parts.append(jnp.where(same_half, total, 0.0).T.astype(BF16))
            lifted = dot(jnp.concatenate(parts, axis=1), wout_ref[...])
            base = coarse_ref[down * 4 : down * 4 + 4, pl.ds(c0, 16), :].astype(F32)
            result = base + (lifted[:64] + lifted[64:]).reshape(4, 16, channels)
            out_ref[down * 4 : down * 4 + 4, pl.ds(c0, 16), :] = result.astype(BF16)

    for copies in (halo_back, halo_obs, halo_norm):
        halo_sent(copies)


def body(
    obs_feat, obs_dest, obs_cell, obs_sub, background, w_in, dens_vec,
    conv_w, conv_b, norm_gain, w_qkv, rel_bias, w_out,
):
    owners = lax.axis_size("lat") * lax.axis_size("lon")
    rows, cols, channels = background.shape
    obs, width = obs_feat.shape
    half, out_rows, both = cols // 2, rows // 2, 2 * width
    strip = jnp.pad(rel_bias, ((0, 0), (0, 7), (0, 19)), constant_values=NEG).reshape(HEADS, 640)
    vmem = pl.BlockSpec(memory_space=pltpu.VMEM)
    hbm = pl.BlockSpec(memory_space=pl.ANY)
    scratch = [
        ((rows, cols, channels), BF16),
        ((4, 4 * channels, channels), BF16),
        ((channels, 3 * channels), BF16),
        ((channels, channels), BF16),
        ((owners, 32, width), BF16),
        ((owners, 1, 128), I32),
        ((owners, 32, width), BF16),
        ((owners, 1, 128), I32),
        ((512, obs), BF16),
        ((obs, width), BF16),
        ((1, obs), I32),
        ((2, rows, channels), F32),
        ((2, cols, channels), BF16),
        ((2, rows + 16, channels), F32),
        ((2 * channels // 128, cols + 16, 128), F32),
        ((rows + 2, half, 4 * channels), BF16),
        ((half * out_rows, channels), F32),
        ((4, 4 * both, channels), BF16),
        ((1, owners * 32), I32),
        ((obs, rows // 4 * width + 128), BF16),
        ((512, rows // 4 * width + 128), F32),
        ((2, rows, both), F32),
        ((2 * both // 128, cols + 16, 128), F32),
        ((4, cols, both), BF16),
        ((2, rows + 16, both), F32),
        ((rows + 2, half, 4 * both), BF16),
        ((out_rows, half, channels), BF16),
        ((out_rows, half, channels), BF16),
        ((2, 6, half, channels), BF16),
        ((2, out_rows // 2 + 6, 16, channels), BF16),
        ((2, out_rows // 2, 16, channels), BF16),
        ((out_rows, half, channels), BF16),
        ((out_rows, half + 16, channels), BF16),
        ((out_rows // 4, 384, HEADS * 64), F32),
        ((out_rows // 4, 256, HEADS * 64), F32),
        ((2, 6, half + 16, channels), BF16),
        ((channels, channels), BF16),
        ((out_rows * half // 64, channels, 128), F32),
        ((out_rows * half // 64, 8, channels), F32),
    ]
    sems = [pltpu.SemaphoreType.DMA((n,)) for n in (4, 4, 2, 34, 34)]
    sems.append(pltpu.SemaphoreType.REGULAR)
    return pl.pallas_call(
        main_kernel,
        name="main",
        out_shape=jax.ShapeDtypeStruct((out_rows, half, channels), BF16),
        in_specs=[vmem, vmem, vmem, vmem, hbm, vmem, vmem, hbm, vmem, vmem, hbm, vmem, hbm],
        out_specs=vmem,
        scratch_shapes=[pltpu.VMEM(shape, dtype) for shape, dtype in scratch] + sems,
        compiler_params=pltpu.CompilerParams(
            collective_id=0, has_side_effects=True, vmem_limit_bytes=62 << 20
        ),
    )(
        obs_dest.reshape(1, obs),
        obs_cell.reshape(1, obs),
        obs_sub.reshape(1, obs),
        obs_feat,
        background,
        w_in,
        dens_vec.reshape(1, channels),
        conv_w.reshape(4, 4 * channels, channels),
        conv_b.reshape(1, channels),
        norm_gain.reshape(1, channels),
        w_qkv,
        strip,
        w_out,
    )


def solution(mesh):
    split = P(("lat", "lon"))
    wide = P(("lat", "lon"), None)
    tile = P("lat", "lon", None)
    in_specs = (wide, wide, split, split, tile) + (P(),) * 8
    return jax.shard_map(body, mesh=mesh, in_specs=in_specs, out_specs=tile, check_vma=False)
```

```python
import jax
import jax.numpy as jnp
from jax import lax
from jax.experimental import pallas as pl
from jax.experimental.pallas import tpu as pltpu
from jax.sharding import PartitionSpec as P

HEADS = 8
F32 = jnp.float32
BF16 = jnp.bfloat16
I32 = jnp.int32
NEG = -1e30
MESH = pl.DeviceIdType.MESH
WAYS = ((-1, 0), (1, 0), (0, -1), (0, 1), (-1, -1), (-1, 1), (1, -1), (1, 1))


def iota(shape, dim):
    return lax.broadcasted_iota(I32, shape, dim)


def narrow(x):
    return x.astype(F32).astype(BF16)


def dot(x, y):
    return jnp.dot(x, y, preferred_element_type=F32)


def dot_t(x, y):
    return lax.dot_general(x, y, (((1,), (1,)), ((), ())), preferred_element_type=F32)


def column(row):
    return jnp.broadcast_to(row.astype(F32), (128, 128)).T.astype(BF16)


def one_hot(place_ref, index, value):
    for part in range(place_ref.shape[0] // 256):
        local = index - part * 256
        local = narrow(jnp.where((local >= 0) & (local < 256), local, -1))
        line = narrow(iota((256, index.shape[1]), 0))
        place_ref[part * 256 : part * 256 + 256, :] = jnp.where(
            line == local, value, jnp.zeros((), BF16)
        )


def main_kernel(
    dest_ref, cell_ref, sub_ref, feat_ref, back_hbm, win_ref, dens_ref, conv_hbm, bias_in_ref,
    gain_ref, wqkv_hbm, rel_ref, wout_hbm,
    out_ref,
    back_ref, conv_ref, wqkv_ref, wout_ref,
    sendf_ref, sendm_ref, recvf_ref, recvm_ref, pick_ref, group_ref, local_ref,
    edge_ref, brow_ref, bside_ref, line_ref, taps_ref, acc_ref, comp_ref,
    codes_ref, spread_ref, sums_ref, oedge_ref, oline_ref, orow_ref, oside_ref, otaps_ref,
    own_ref, coarse_ref, vert_ref, side_ref, sside_ref, query_ref, ext_ref, bias_ref, rim_ref,
    far_ref, turned_ref, held_ref, stat_ref, strip_ref,
    load_sem, route_sem, arrive_sem, own_sem, halo_send, halo_recv, meet_sem,
):
    obs, width = feat_ref.shape
    owners = sendf_ref.shape[0]
    slots = owners * 32
    rows, cols, channels = back_ref.shape
    half = cols // 2
    out_rows = rows // 2
    both = 2 * width
    lat_count, lon_count = lax.axis_size("lat"), lax.axis_size("lon")
    lat, lon = lax.axis_index("lat"), lax.axis_index("lon")
    me = lat * lon_count + lon

    loads = [
        pltpu.make_async_copy(src, dst, load_sem.at[i])
        for i, (src, dst) in enumerate(
            ((back_hbm, back_ref), (conv_hbm, conv_ref), (wqkv_hbm, wqkv_ref), (wout_hbm, wout_ref))
        )
    ]
    for load in loads:
        load.start()

    def inside(da):
        return (lat + da >= 0) & (lat + da < lat_count)

    def place(device):
        return device // lon_count, lax.rem(device, lon_count)

    barrier = pltpu.get_barrier_semaphore()
    near = [me ^ j for j in range(1, 16)]
    far = [me ^ (16 * j) for j in range(1, owners // 16)]

    def greet(where):
        pl.semaphore_signal(barrier, inc=1, device_id=where, device_id_type=MESH)

    for da, db in WAYS:
        there = (lat + da, lax.rem(lon + db + lon_count, lon_count))
        if da == 0:
            greet(there)
        else:
            pl.when(inside(da))(lambda: greet(there))
    for device in near + far:
        greet(place(device))

    def halo(base, parts):
        copies = []
        for i, ((da, db), src, dst) in enumerate(parts):
            copies.append(
                (
                    da,
                    pltpu.make_async_remote_copy(
                        src_ref=src,
                        dst_ref=dst,
                        send_sem=halo_send.at[base + i],
                        recv_sem=halo_recv.at[base + i],
                        device_id=(lat + da, lax.rem(lon + db + lon_count, lon_count)),
                        device_id_type=MESH,
                    ),
                )
            )
        return copies

    def halo_start(copies):
        for da, copy in copies:
            pl.when(inside(da))(copy.start)

    def halo_arrive(copies):
        for da, copy in copies:
            pl.when(inside(-da))(copy.wait_recv)

    def halo_sent(copies):
        for da, copy in copies:
            pl.when(inside(da))(copy.wait_send)

    loads[0].wait()
    for row in range(rows):
        tile = back_ref[row, 0:16, :].astype(F32)
        edge_ref[0, row : row + 1, :] = tile[0:1]
        tile = back_ref[row, cols - 16 : cols, :].astype(F32)
        edge_ref[1, row : row + 1, :] = tile[15:16]

    neighbours = 2 + 3 * (inside(-1).astype(I32) + inside(1).astype(I32))
    pl.semaphore_wait(barrier, len(near) + len(far) + neighbours)
    for device in far:
        pl.semaphore_signal(meet_sem, inc=1, device_id=place(device), device_id_type=MESH)

    def fine_parts(first, last, edge, row, side):
        top, bottom = pl.ds(0, 8), pl.ds(rows - 8, 8)
        return (
            ((-1, 0), first, row.at[1]),
            ((1, 0), last, row.at[0]),
            ((0, -1), edge.at[0], side.at[1, pl.ds(8, rows)]),
            ((0, 1), edge.at[1], side.at[0, pl.ds(8, rows)]),
            ((-1, -1), edge.at[0, top], side.at[1, pl.ds(8 + rows, 8)]),
            ((-1, 1), edge.at[1, top], side.at[0, pl.ds(8 + rows, 8)]),
            ((1, -1), edge.at[0, bottom], side.at[1, pl.ds(0, 8)]),
            ((1, 1), edge.at[1, bottom], side.at[0, pl.ds(0, 8)]),
        )

    halo_back = halo(0, fine_parts(back_ref.at[0], back_ref.at[rows - 1], edge_ref, brow_ref, bside_ref))
    halo_start(halo_back)

    step = 256
    upper = (iota((step, step), 0) < iota((step, step), 1)).astype(F32).astype(BF16)
    running = jnp.zeros((owners, 1), F32)
    for at in range(0, obs, step):
        dest = dest_ref[:, at : at + step]
        member = (iota((owners, step), 0) == dest).astype(F32)
        earlier = dot(member.astype(BF16), upper) + running
        rank = jnp.sum(member * earlier, axis=0, keepdims=True)
        running = running + jnp.sum(member, axis=1, keepdims=True)
        local_ref[:, at : at + step] = (dest >> 3) * 32 + rank.astype(I32)
        for more in range(0, step, 128):
            group_ref[at + more : at + more + 128, :] = column(dest[:, more : more + 128] & 7)
    one_hot(pick_ref, local_ref[...], jnp.ones((), BF16))

    dest, cell, sub = dest_ref[...], cell_ref[...], sub_ref[...]
    same = iota((8, obs), 0) == (dest & 7)
    meta = jnp.concatenate(
        [jnp.where(same, value, 0) for value in ((cell >> 7) + 1, cell & 127, sub, dest * 0)], axis=0
    )
    meta = dot_t(narrow(meta), pick_ref[...])
    code = (meta[0:8] * 128.0 + meta[8:16]).astype(I32) * 256 + meta[16:24].astype(I32)
    spread_by = lax.rem(lat, 4)
    mine = iota((8, 128), 1) // 32 == spread_by
    for c in range(4):
        chunk = code[:, c * 128 : c * 128 + 128]
        turned = [chunk] + [pltpu.roll(chunk, 32 * k, 1) for k in range(1, 4)]
        for j in range(4):
            near = lax.rem(spread_by - j + 4, 4)
            placed = jnp.where(
                near < 2,
                jnp.where(near == 0, turned[0], turned[1]),
                jnp.where(near == 2, turned[2], turned[3]),
            )
            placed = jnp.where(mine, placed, 0)
            for g in range(8):
                sendm_ref[g * 16 + c * 4 + j] = placed[g : g + 1]

    pl.semaphore_wait(meet_sem, len(far))

    kind = lax.rem(lat + lon, 4)
    home = kind * 32 + lat

    @pl.loop(0, owners // 32)
    def _(turn):
        part = lax.rem(turn + kind, 4)
        group = group_ref[...]
        feat = feat_ref[...]
        wide = jnp.concatenate(
            [
                jnp.where(
                    group == jnp.full((1, 1), 2 * part + i, I32).astype(F32).astype(BF16),
                    feat,
                    jnp.zeros((), BF16),
                )
                for i in range(2)
            ],
            axis=1,
        )
        packed = dot(pick_ref[...], wide).astype(BF16)
        for i in range(2):
            sendf_ref[pl.ds((part * 2 + i) * 16, 16)] = packed[:, i * width : (i + 1) * width].reshape(
                16, 32, width
            )

        @pl.loop(0, 32)
        def _(k):
            turned = lax.rem(k * 5 + me, 32)
            group = part * 2 + lax.rem(turned, 2)
            peer = (turned // 2) * 8 + group

            @pl.when(peer != me)
            def _():
                there = place(peer)
                slot = group * 16 + turned // 2
                for i, (src, dst) in enumerate(((sendf_ref, recvf_ref), (sendm_ref, recvm_ref))):
                    pltpu.make_async_remote_copy(
                        src_ref=src.at[slot],
                        dst_ref=dst.at[home],
                        send_sem=route_sem.at[i],
                        recv_sem=arrive_sem.at[2 * turn + i],
                        device_id=there,
                        device_id_type=MESH,
                    ).start()

    own_copies = [
        pltpu.make_async_copy(src.at[lax.rem(me, 8) * 16 + me // 8], dst.at[home], own_sem.at[i])
        for i, (src, dst) in enumerate(((sendf_ref, recvf_ref), (sendm_ref, recvm_ref)))
    ]
    for copy in own_copies:
        copy.start()

    @pl.when(lat == 0)
    def _():
        brow_ref[0] = jnp.zeros((cols, channels), BF16)
        bside_ref[:, 0:8, :] = jnp.zeros((2, 8, channels), F32)
        orow_ref[0] = jnp.zeros((cols, both), BF16)
        oside_ref[:, 0:8, :] = jnp.zeros((2, 8, both), F32)
        vert_ref[0] = jnp.zeros((6, half, channels), BF16)
        side_ref[:, 0:3] = jnp.zeros((2, 3, 16, channels), BF16)

    @pl.when(lat == lat_count - 1)
    def _():
        brow_ref[1] = jnp.zeros((cols, channels), BF16)
        bside_ref[:, 8 + rows :, :] = jnp.zeros((2, 8, channels), F32)
        orow_ref[1] = jnp.zeros((cols, both), BF16)
        oside_ref[:, 8 + rows :, :] = jnp.zeros((2, 8, both), F32)
        vert_ref[1] = jnp.zeros((6, half, channels), BF16)
        side_ref[:, 9:12] = jnp.zeros((2, 3, 16, channels), BF16)

    halo_arrive(halo_back)

    def lay(taps, buffer, slot, at, line, left, right):
        size = line.shape[1]
        for c in range(size // 128):
            lanes = slice(c * 128, (c + 1) * 128)
            spot = slot * (size // 128) + c
            buffer[spot, 8 : 8 + cols, :] = line[:, lanes].astype(F32)
            if left is not None:
                buffer[spot, 7:8, :] = left[:, lanes]
                buffer[spot, 8 + cols : 9 + cols, :] = right[:, lanes]
            for tap in range(4):
                part = buffer[spot, pl.ds(7 + tap, half, stride=2), :]
                base = tap * size + c * 128
                taps[at, :, base : base + 128] = part.astype(BF16)

    for i, at in ((0, 0), (1, rows + 1)):
        lay(
            taps_ref, line_ref, i, at, brow_ref[i],
            bside_ref[0, at + 7 : at + 8, :], bside_ref[1, at + 7 : at + 8, :],
        )

    @pl.loop(0, rows // 2)
    def _(pair):
        for i in range(2):
            row = pair * 2 + i
            lay(
                taps_ref, line_ref, i, row + 1, back_ref[row],
                bside_ref[0, pl.ds(row + 8, 1), :], bside_ref[1, pl.ds(row + 8, 1), :],
            )

    loads[1].wait()
    block = 4 * half

    def window(taps, part, tap):
        return taps[pl.ds(part * 4 + tap // 2, 4), tap % 2].reshape(block, taps.shape[3])

    taps4 = taps_ref.reshape(rows // 2 + 1, 2, half, 4 * channels)
    otaps4 = otaps_ref.reshape(rows // 2 + 1, 2, half, 4 * both)

    @pl.loop(0, out_rows // 4)
    def _(part):
        total = jnp.broadcast_to(bias_in_ref[...], (block, channels))
        for tap in range(4):
            total = total + dot(window(taps4, part, tap), conv_ref[tap])
        acc_ref[pl.ds(pl.multiple_of(part * block, block), block), :] = total

    dens = jnp.broadcast_to(dens_ref[...], (16, channels))
    dens_hi = dens.astype(BF16)
    dens_lo = (dens - dens_hi.astype(F32)).astype(BF16)
    line16 = iota((16, channels), 0)
    tail = jnp.where(
        line16 == 0, dens_hi.astype(F32), jnp.where(line16 == 1, dens_lo.astype(F32), 0.0)
    ).astype(BF16)
    lift = jnp.concatenate([win_ref[...], tail], axis=0)

    @pl.loop(0, 4)
    def _(tap):
        for s in range(4):
            made = dot(lift, conv_ref[tap, s * channels : (s + 1) * channels, :])
            base = s * both
            comp_ref[tap, base : base + width, :] = made[:width].astype(BF16)
            whole = made[width : width + 1] + made[width + 1 : width + 2]
            upper_part = whole.astype(BF16).astype(F32)
            rest = jnp.where(
                line16 < 2, upper_part, jnp.where(line16 == 2, whole - upper_part, 0.0)
            ).astype(BF16)
            comp_ref[tap, base + width : base + width + 16, :] = rest
            comp_ref[tap, base + width + 16 : base + both, :] = jnp.zeros(
                (width - 16, channels), BF16
            )

    loads[2].wait()
    loads[3].wait()
    turned_ref[...] = wqkv_ref[:, 2 * channels :].astype(F32).T.astype(BF16)

    chunk = spread_ref.shape[0]
    lane = narrow(iota((128, 128), 1))
    sums_ref[...] = jnp.zeros(sums_ref.shape, F32)

    @pl.loop(0, 4)
    def _(turn):
        senders = lax.rem(lax.rem(me, 8) // 2 - turn + 4, 4)
        first = senders * 32

        def arrive(count):
            some = pl.ds(0, count)
            for i, (src, dst) in enumerate(((sendf_ref, recvf_ref), (sendm_ref, recvm_ref))):
                pltpu.make_async_copy(src.at[some], dst.at[some], arrive_sem.at[2 * turn + i]).wait()

        @pl.when(senders == kind)
        def _():
            arrive(31)
            for copy in own_copies:
                copy.wait()

        @pl.when(senders != kind)
        def _():
            arrive(32)

        for group in range(8):
            code = recvm_ref[first + group * 4]
            for other in range(1, 4):
                code = code + recvm_ref[first + group * 4 + other]
            codes_ref[:, group * 128 : group * 128 + 128] = code
        code = codes_ref[...]
        sub = code & 255
        cell = (code >> 8) - 128
        row_off = ((sub >> 4).astype(F32) + 0.5) / 16.0 - 0.5
        col_off = ((sub & 15).astype(F32) + 0.5) / 16.0 - 0.5
        kern = jnp.exp(-(row_off * row_off + col_off * col_off) / (2.0 * 0.35 * 0.35))
        one_hot(pick_ref.at[:, 0:chunk], cell & 511, kern.astype(BF16))
        band = cell >> 9
        for b in range(chunk // 128):
            spot = column(band[:, b * 128 : b * 128 + 128])
            feat = recvf_ref[pl.ds(first + b * 4, 4)].reshape(128, width)
            lines = slice(b * 128, b * 128 + 128)
            for g in range(rows // 4):
                here = jnp.full((1, 1), g, F32).astype(BF16)
                spread_ref[lines, g * width : (g + 1) * width] = jnp.where(
                    spot == here, feat, jnp.zeros((), BF16)
                )
            spread_ref[lines, rows // 4 * width :] = jnp.where(
                spot == lane, jnp.ones((), BF16), jnp.zeros((), BF16)
            )
        sums_ref[...] += dot(pick_ref[:, 0:chunk], spread_ref[...])

    lane_f = iota((cols, width), 1)
    for g in range(rows // 4):
        for r in range(4):
            row = g * 4 + r
            lines = slice(r * cols, (r + 1) * cols)
            density = sums_ref[lines, rows // 4 * width + g : rows // 4 * width + g + 1]
            normed = sums_ref[lines, g * width : (g + 1) * width] / (density + 1.0)
            high = density.astype(BF16).astype(F32)
            marks = jnp.where(
                (lane_f == 0) | (lane_f == 2), high, jnp.where(lane_f == 1, density - high, 0.0)
            )
            line = jnp.concatenate([normed, marks], axis=1)
            oedge_ref[0, row : row + 1, :] = line[0:1]
            oedge_ref[1, row : row + 1, :] = line[cols - 1 : cols]
            if row == 0:
                orow_ref[2] = line.astype(BF16)
            if row == rows - 1:
                orow_ref[3] = line.astype(BF16)
            lay(otaps_ref, oline_ref, row % 2, row + 1, line, None, None)

    halo_obs = halo(8, fine_parts(orow_ref.at[2], orow_ref.at[3], oedge_ref, orow_ref, oside_ref))
    halo_start(halo_obs)

    middle = slice(both, 3 * both)
    for part in (1, 0, 2):
        lines = slice(part * block, (part + 1) * block)
        total = acc_ref[lines, :]
        for tap in range(4):
            if (part, tap) not in ((0, 0), (out_rows // 4 - 1, 3)):
                total = total + dot(window(otaps4, part, tap)[:, middle], comp_ref[tap, middle, :])
        acc_ref[lines, :] = total

    no_up = jnp.where(lat == 0, NEG, 0.0)
    no_down = jnp.where(lat == lat_count - 1, NEG, 0.0)
    strip_ref[...] = jnp.full(strip_ref.shape, NEG, F32)
    for r in range(rel_ref.shape[1]):
        strip_ref[:, r * 32 : r * 32 + rel_ref.shape[2]] = rel_ref[:, r, :]
    lane256 = iota((16, 256), 1)
    for pair in range(HEADS // 2):
        places = slice(pair * 128, pair * 128 + 128)
        for down in range(out_rows // 4):
            inner_part, outer_part = [], []
            for h in (2 * pair, 2 * pair + 1):
                strip = jnp.broadcast_to(strip_ref[h : h + 1, :], (16, 640))
                for r in range(4):

                    def shifted(first_row, lead, size):
                        amount = (2 + 32 * (r + 4 * down - first_row) + lead) % 640
                        return pltpu.roll(strip, amount, 1, stride=1, stride_axis=0)[:, :size]

                    inner_part.append(shifted(6, 0, 384))
                    if down == 0:
                        outer_part.append(shifted(0, 0, 256) + no_up)
                    elif down == 1:
                        outer_part.append(
                            jnp.where(
                                lane256 < 64, shifted(4, 0, 256) + no_up, shifted(18, 64, 256) + no_down
                            )
                        )
                    else:
                        outer_part.append(jnp.where(lane256 < 64, NEG, shifted(18, 64, 256) + no_down))
            bias_ref[down, :, places] = jnp.concatenate(inner_part, axis=0).T
            rim_ref[down, :, places] = jnp.concatenate(outer_part, axis=0).T

    halo_arrive(halo_obs)
    for i, at in ((0, 0), (1, rows + 1)):
        lay(otaps_ref, oline_ref, i, at, orow_ref[i], None, None)
    first_line = iota((16, both), 0) == 0
    last_line = iota((16, both), 0) == 15
    for at in range(rows + 2):
        old = otaps_ref[at, 0:16, 0:both].astype(F32)
        otaps_ref[at, 0:16, 0:both] = jnp.where(
            first_line, oside_ref[0, at + 7 : at + 8, :], old
        ).astype(BF16)
        old = otaps_ref[at, half - 16 : half, 3 * both :].astype(F32)
        otaps_ref[at, half - 16 : half, 3 * both :] = jnp.where(
            last_line, oside_ref[1, at + 7 : at + 8, :], old
        ).astype(BF16)


    outer = (slice(0, both), slice(3 * both, 4 * both))

    def finish(part):
        lines = slice(part * block, (part + 1) * block)
        total = acc_ref[lines, :]
        for tap in range(4):
            view = window(otaps4, part, tap)
            if (part, tap) in ((0, 0), (out_rows // 4 - 1, 3)):
                total = total + dot(view, comp_ref[tap])
            else:
                for lanes in outer:
                    total = total + dot(view[:, lanes], comp_ref[tap, lanes, :])
        inner = 0.7978845608028654 * (total + 0.044715 * total * total * total)
        coarse = (0.5 * total * (1.0 + jnp.tanh(inner))).astype(BF16)
        coarse_ref[part * 4 : part * 4 + 4] = coarse.reshape(4, half, channels)
        value = coarse.astype(F32)
        scale = lax.rsqrt(jnp.mean(value * value, axis=1, keepdims=True) + 1e-05)
        normed = value * scale * gain_ref[...]
        own_ref[part * 4 : part * 4 + 4] = normed.astype(BF16).reshape(4, half, channels)
        ext_ref[part * 4 : part * 4 + 4, 8 : 8 + half, :] = normed.reshape(4, half, channels).astype(BF16)
        for side, at in ((0, 0), (1, half - 8)):
            for pair in range(2):
                first = pair * 2 * half + at
                both_rows = jnp.concatenate(
                    [normed[first : first + 8], normed[first + half : first + half + 8]], axis=0
                )
                sside_ref[side, part * 2 + pair] = both_rows.astype(BF16)

    def rim(first, count, side):
        return sside_ref.at[side, pl.ds(first, count)]

    def gap(first, count, side):
        return side_ref.at[side, pl.ds(first, count)]

    finish(0)
    halo_first = halo(
        16,
        (
            ((0, -1), rim(0, 2, 0), gap(3, 2, 1)),
            ((0, 1), rim(0, 2, 1), gap(3, 2, 0)),
            ((-1, 0), own_ref.at[pl.ds(0, 4)], vert_ref.at[1, pl.ds(0, 4)]),
        ),
    )
    halo_start(halo_first)
    finish(2)
    halo_second = halo(
        21,
        (
            ((0, -1), rim(4, 2, 0), gap(7, 2, 1)),
            ((0, 1), rim(4, 2, 1), gap(7, 2, 0)),
            ((1, 0), own_ref.at[pl.ds(8, 4)], vert_ref.at[0, pl.ds(2, 4)]),
        ),
    )
    halo_start(halo_second)
    finish(1)
    halo_third = halo(
        26,
        (
            ((0, -1), rim(2, 2, 0), gap(5, 2, 1)),
            ((0, 1), rim(2, 2, 1), gap(5, 2, 0)),
            ((-1, 0), own_ref.at[pl.ds(4, 2)], vert_ref.at[1, pl.ds(4, 2)]),
            ((1, 0), own_ref.at[pl.ds(6, 2)], vert_ref.at[0, pl.ds(0, 2)]),
        ),
    )
    halo_start(halo_third)
    halo_norm = halo_first + halo_second + halo_third
    halo_side = halo_first[:2] + halo_second[:2] + halo_third[:2]
    halo_far = halo_first[2:] + halo_second[2:] + halo_third[2:]

    @pl.loop(0, out_rows // 4)
    def _(part):
        own = own_ref[pl.ds(part * 4, 4)].reshape(block, channels)
        query = dot(own, wqkv_ref[:, :channels]).astype(BF16) * 0.125
        query_ref[pl.ds(part * 4, 4)] = query.astype(BF16).reshape(4, half, channels)

    half_ch = channels // 2
    lane_head = iota((64, half_ch), 1) // (channels // HEADS)
    same_half = iota((128, 128), 0) // 64 == iota((128, 128), 1) // 64

    def keys_values(x):
        keys = dot(x, wqkv_ref[:, channels : 2 * channels]).astype(BF16)
        return keys, dot_t(turned_ref[...], x).astype(BF16)

    def queries(down, c0, lanes):
        wide = query_ref[down * 4 : down * 4 + 4, pl.ds(c0, 16), lanes].reshape(64, half_ch)
        return jnp.concatenate(
            [jnp.where(lane_head == h, wide, jnp.zeros((), BF16)) for h in range(4)], axis=0
        )

    def attend_near(across):
        c0 = pl.multiple_of(across * 16, 16)
        keys, values = keys_values(ext_ref[:, pl.ds(c0, 32), :].reshape(32 * out_rows, channels))
        for down in range(out_rows // 4):
            spot = down * (half // 16) + across
            for g in range(2):
                lanes = slice(g * half_ch, (g + 1) * half_ch)
                scores = dot_t(keys[:, lanes], queries(down, c0, lanes)) + bias_ref[down, :, lanes]
                peak = jnp.max(scores, axis=0, keepdims=True)
                weight = jnp.exp(scores - peak)
                stat_ref[spot, 0:1, lanes] = peak
                stat_ref[spot, 1:2, lanes] = jnp.sum(weight, axis=0, keepdims=True)
                mixed = dot(values[lanes], weight.astype(BF16))
                for p in range(2):
                    cut = slice(p * 128, p * 128 + 128)
                    held_ref[spot, g * half_ch + p * 128 : g * half_ch + p * 128 + 128, :] = mixed[cut, cut]

    @pl.loop(1, half // 16 - 1)
    def _(across):
        attend_near(across)

    halo_arrive(halo_side)
    halo_corner = halo(
        34,
        [
            ((way, 0), side_ref.at[i, pl.ds(start, 3)], side_ref.at[i, pl.ds(stop, 3)])
            for i in range(2)
            for way, start, stop in ((-1, 3, 9), (1, 6, 0))
        ],
    )
    halo_start(halo_corner)
    for i, at in ((0, 0), (1, 8 + half)):
        x = side_ref[i, 3 : 3 + out_rows // 2].astype(F32).reshape(out_rows, 8, channels)
        ext_ref[:, at : at + 8, :] = x.astype(BF16)

    @pl.loop(0, 2)
    def _(end):
        attend_near(end * (half // 16 - 1))

    halo_arrive(halo_far + halo_corner)
    for i in range(2):
        seg = slice(0, 3) if i == 0 else slice(3 + out_rows // 2, 6 + out_rows // 2)
        far_ref[i, :, 8 : 8 + half, :] = vert_ref[i].astype(F32).astype(BF16)
        for j, at in ((0, 0), (1, 8 + half)):
            x = side_ref[j, seg].astype(F32).reshape(6, 8, channels)
            far_ref[i, :, at : at + 8, :] = x.astype(BF16)

    @pl.loop(0, half // 16)
    def _(across):
        c0 = pl.multiple_of(across * 16, 16)
        above = far_ref[0, :, pl.ds(c0, 32), :].reshape(192, channels)
        below = far_ref[1, :, pl.ds(c0, 32), :].reshape(192, channels)
        keys, values = keys_values(jnp.concatenate([above[128:], below[:64], above, below], axis=0))
        for down, seg in ((0, slice(128, 320)), (1, slice(0, 128)), (2, slice(256, 512))):
            spot = down * (half // 16) + across
            count = seg.stop - seg.start
            parts = []
            for g in range(2):
                lanes = slice(g * half_ch, (g + 1) * half_ch)
                scores = dot_t(keys[seg, lanes], queries(down, c0, lanes)) + rim_ref[down, :count, lanes]
                old_peak, old_norm = stat_ref[spot, 0:1, lanes], stat_ref[spot, 1:2, lanes]
                peak = jnp.maximum(old_peak, jnp.max(scores, axis=0, keepdims=True))
                weight = jnp.exp(scores - peak)
                fade = jnp.exp(old_peak - peak)
                inverse = 1.0 / (old_norm * fade + jnp.sum(weight, axis=0, keepdims=True))
                fade = fade * inverse
                mixed = dot(values[lanes, seg], weight.astype(BF16))
                for p in range(2):
                    cut = slice(p * 128, p * 128 + 128)
                    held = held_ref[spot, g * half_ch + p * 128 : g * half_ch + p * 128 + 128, :]
                    total = held * fade[:, cut] + mixed[cut, cut] * inverse[:, cut]
                    parts.append(jnp.where(same_half, total, 0.0).T.astype(BF16))
            lifted = dot(jnp.concatenate(parts, axis=1), wout_ref[...])
            base = coarse_ref[down * 4 : down * 4 + 4, pl.ds(c0, 16), :].astype(F32)
            result = base + (lifted[:64] + lifted[64:]).reshape(4, 16, channels)
            out_ref[down * 4 : down * 4 + 4, pl.ds(c0, 16), :] = result.astype(BF16)

    rest = pl.ds(0, owners - 1)
    for i, (src, dst) in enumerate(((sendf_ref, recvf_ref), (sendm_ref, recvm_ref))):
        pltpu.make_async_copy(src.at[rest], dst.at[rest], route_sem.at[i]).wait()
    for copies in (halo_back, halo_obs, halo_norm, halo_corner):
        halo_sent(copies)


def body(
    obs_feat, obs_dest, obs_cell, obs_sub, background, w_in, dens_vec,
    conv_w, conv_b, norm_gain, w_qkv, rel_bias, w_out,
):
    owners = lax.axis_size("lat") * lax.axis_size("lon")
    rows, cols, channels = background.shape
    obs, width = obs_feat.shape
    half, out_rows, both = cols // 2, rows // 2, 2 * width
    vmem = pl.BlockSpec(memory_space=pltpu.VMEM)
    hbm = pl.BlockSpec(memory_space=pl.ANY)
    scratch = [
        ((rows, cols, channels), BF16),
        ((4, 4 * channels, channels), BF16),
        ((channels, 3 * channels), BF16),
        ((channels, channels), BF16),
        ((owners, 32, width), BF16),
        ((owners, 1, 128), I32),
        ((owners, 32, width), BF16),
        ((owners, 1, 128), I32),
        ((512, obs), BF16),
        ((obs, width), BF16),
        ((1, obs), I32),
        ((2, rows, channels), F32),
        ((2, cols, channels), BF16),
        ((2, rows + 16, channels), F32),
        ((2 * channels // 128, cols + 16, 128), F32),
        ((rows + 2, half, 4 * channels), BF16),
        ((half * out_rows, channels), F32),
        ((4, 4 * both, channels), BF16),
        ((1, owners * 8), I32),
        ((owners * 8, rows // 4 * width + 128), BF16),
        ((512, rows // 4 * width + 128), F32),
        ((2, rows, both), F32),
        ((2 * both // 128, cols + 16, 128), F32),
        ((4, cols, both), BF16),
        ((2, rows + 16, both), F32),
        ((rows + 2, half, 4 * both), BF16),
        ((out_rows, half, channels), BF16),
        ((out_rows, half, channels), BF16),
        ((2, 6, half, channels), BF16),
        ((2, out_rows // 2 + 6, 16, channels), BF16),
        ((2, out_rows // 2, 16, channels), BF16),
        ((out_rows, half, channels), BF16),
        ((out_rows, half + 16, channels), BF16),
        ((out_rows // 4, 384, HEADS * 64), F32),
        ((out_rows // 4, 256, HEADS * 64), F32),
        ((2, 6, half + 16, channels), BF16),
        ((channels, channels), BF16),
        ((out_rows * half // 64, channels, 128), F32),
        ((out_rows * half // 64, 8, channels), F32),
        ((HEADS, 640), F32),
    ]
    sems = [pltpu.SemaphoreType.DMA((n,)) for n in (4, 2, 8, 2, 38, 38)]
    sems.append(pltpu.SemaphoreType.REGULAR)
    return pl.pallas_call(
        main_kernel,
        name="main",
        out_shape=jax.ShapeDtypeStruct((out_rows, half, channels), BF16),
        in_specs=[vmem, vmem, vmem, vmem, hbm, vmem, vmem, hbm, vmem, vmem, hbm, vmem, hbm],
        out_specs=vmem,
        scratch_shapes=[pltpu.VMEM(shape, dtype) for shape, dtype in scratch] + sems,
        compiler_params=pltpu.CompilerParams(
            collective_id=0, has_side_effects=True, vmem_limit_bytes=62 << 20
        ),
    )(
        obs_dest.reshape(1, obs),
        obs_cell.reshape(1, obs),
        obs_sub.reshape(1, obs),
        obs_feat,
        background,
        w_in,
        dens_vec.reshape(1, channels),
        conv_w.reshape(4, 4 * channels, channels),
        conv_b.reshape(1, channels),
        norm_gain.reshape(1, channels),
        w_qkv,
        rel_bias,
        w_out,
    )


def solution(mesh):
    split = P(("lat", "lon"))
    wide = P(("lat", "lon"), None)
    tile = P("lat", "lon", None)
    in_specs = (wide, wide, split, split, tile) + (P(),) * 8
    return jax.shard_map(body, mesh=mesh, in_specs=in_specs, out_specs=tile, check_vma=False)
```

```python
import jax
import jax.numpy as jnp
from jax import lax
from jax.experimental import pallas as pl
from jax.experimental.pallas import tpu as pltpu
from jax.sharding import PartitionSpec as P

HEADS = 8
F32 = jnp.float32
BF16 = jnp.bfloat16
I32 = jnp.int32
NEG = -1e30
LOG2E = 1.4426950408889634
MESH = pl.DeviceIdType.MESH
WAYS = ((-1, 0), (1, 0), (0, -1), (0, 1), (-1, -1), (-1, 1), (1, -1), (1, 1))


def iota(shape, dim):
    return lax.broadcasted_iota(I32, shape, dim)


def narrow(x):
    return x.astype(F32).astype(BF16)


def dot(x, y):
    return jnp.dot(x, y, preferred_element_type=F32)


def dot_t(x, y):
    return lax.dot_general(x, y, (((1,), (1,)), ((), ())), preferred_element_type=F32)


def column(row):
    return jnp.broadcast_to(row.astype(F32), (128, 128)).T.astype(BF16)


def one_hot(place_ref, index, value):
    for part in range(place_ref.shape[0] // 256):
        local = index - part * 256
        local = narrow(jnp.where((local >= 0) & (local < 256), local, -1))
        line = narrow(iota((256, index.shape[1]), 0))
        place_ref[part * 256 : part * 256 + 256, :] = jnp.where(
            line == local, value, jnp.zeros((), BF16)
        )


def main_kernel(
    dest_ref, cell_ref, sub_ref, feat_hbm, back_hbm, win_hbm, dens_ref, conv_hbm, bias_in_ref,
    gain_ref, wqkv_hbm, rel_ref, wout_hbm,
    out_hbm,
    feat_ref, win_ref, out_ref, back_ref, conv_ref, wqkv_ref, wout_ref,
    sendf_ref, sendm_ref, recvf_ref, recvm_ref, pick_ref, group_ref, local_ref,
    edge_ref, brow_ref, bside_ref, line_ref, taps_ref, acc_ref, comp_ref,
    codes_ref, spread_ref, sums_ref, oedge_ref, oline_ref, orow_ref, oside_ref, otaps_ref,
    own_ref, coarse_ref, vert_ref, side_ref, sside_ref, query_ref, ext_ref, bias_ref, rim_ref,
    far_ref, turned_ref, held_ref, stat_ref, strip_ref, keys_ref, values_ref,
    load_sem, route_sem, arrive_sem, own_sem, out_sem, halo_send, halo_recv, meet_sem,
):
    obs, width = feat_ref.shape
    owners = sendf_ref.shape[0]
    slots = owners * 32
    rows, cols, channels = back_ref.shape
    half = cols // 2
    out_rows = rows // 2
    both = 2 * width
    lat_count, lon_count = lax.axis_size("lat"), lax.axis_size("lon")
    lat, lon = lax.axis_index("lat"), lax.axis_index("lon")
    me = lat * lon_count + lon

    loads = [
        pltpu.make_async_copy(src, dst, load_sem.at[i])
        for i, (src, dst) in enumerate(
            (
                (back_hbm, back_ref),
                (conv_hbm, conv_ref),
                (wqkv_hbm, wqkv_ref),
                (wout_hbm, wout_ref),
                (feat_hbm, feat_ref),
                (win_hbm, win_ref),
            )
        )
    ]
    for i in (0, 4, 5, 1, 2, 3):
        loads[i].start()

    def inside(da):
        return (lat + da >= 0) & (lat + da < lat_count)

    def place(device):
        return device // lon_count, lax.rem(device, lon_count)

    barrier = pltpu.get_barrier_semaphore()
    near = [me ^ j for j in range(1, 16)]
    far = [me ^ (16 * j) for j in range(1, owners // 16)]

    def greet(where):
        pl.semaphore_signal(barrier, inc=1, device_id=where, device_id_type=MESH)

    for da, db in WAYS:
        there = (lat + da, lax.rem(lon + db + lon_count, lon_count))
        if da == 0:
            greet(there)
        else:
            pl.when(inside(da))(lambda: greet(there))
    for device in near + far:
        greet(place(device))

    def halo(base, parts):
        copies = []
        for i, ((da, db), src, dst) in enumerate(parts):
            copies.append(
                (
                    da,
                    pltpu.make_async_remote_copy(
                        src_ref=src,
                        dst_ref=dst,
                        send_sem=halo_send.at[base + i],
                        recv_sem=halo_recv.at[base + i],
                        device_id=(lat + da, lax.rem(lon + db + lon_count, lon_count)),
                        device_id_type=MESH,
                    ),
                )
            )
        return copies

    def halo_start(copies):
        for da, copy in copies:
            pl.when(inside(da))(copy.start)

    def halo_arrive(copies):
        for da, copy in copies:
            pl.when(inside(-da))(copy.wait_recv)

    def halo_sent(copies):
        for da, copy in copies:
            pl.when(inside(da))(copy.wait_send)

    loads[0].wait()
    @pl.loop(0, rows)
    def _(row):
        edge_ref[0, pl.ds(row, 1), :] = back_ref[row, 0:16, :].astype(F32)[0:1]
        edge_ref[1, pl.ds(row, 1), :] = back_ref[row, cols - 16 : cols, :].astype(F32)[15:16]

    neighbours = 2 + 3 * (inside(-1).astype(I32) + inside(1).astype(I32))
    pl.semaphore_wait(barrier, len(near) + len(far) + neighbours)
    for device in far:
        pl.semaphore_signal(meet_sem, inc=1, device_id=place(device), device_id_type=MESH)

    def fine_parts(first, last, edge, row, side):
        top, bottom = pl.ds(0, 8), pl.ds(rows - 8, 8)
        return (
            ((-1, 0), first, row.at[1]),
            ((1, 0), last, row.at[0]),
            ((0, -1), edge.at[0], side.at[1, pl.ds(8, rows)]),
            ((0, 1), edge.at[1], side.at[0, pl.ds(8, rows)]),
            ((-1, -1), edge.at[0, top], side.at[1, pl.ds(8 + rows, 8)]),
            ((-1, 1), edge.at[1, top], side.at[0, pl.ds(8 + rows, 8)]),
            ((1, -1), edge.at[0, bottom], side.at[1, pl.ds(0, 8)]),
            ((1, 1), edge.at[1, bottom], side.at[0, pl.ds(0, 8)]),
        )

    halo_back = halo(0, fine_parts(back_ref.at[0], back_ref.at[rows - 1], edge_ref, brow_ref, bside_ref))
    halo_start(halo_back)

    step = 256
    upper = (iota((step, step), 0) < iota((step, step), 1)).astype(F32).astype(BF16)
    running = jnp.zeros((owners, 1), F32)
    for at in range(0, obs, step):
        dest = dest_ref[:, at : at + step]
        member = (iota((owners, step), 0) == dest).astype(F32)
        earlier = dot(member.astype(BF16), upper) + running
        rank = jnp.sum(member * earlier, axis=0, keepdims=True)
        running = running + jnp.sum(member, axis=1, keepdims=True)
        local_ref[:, at : at + step] = (dest >> 3) * 32 + rank.astype(I32)
        for more in range(0, step, 128):
            group_ref[at + more : at + more + 128, :] = column(dest[:, more : more + 128] & 7)
    one_hot(pick_ref, local_ref[...], jnp.ones((), BF16))

    dest, cell, sub = dest_ref[...], cell_ref[...], sub_ref[...]
    same = iota((8, obs), 0) == (dest & 7)
    meta = jnp.concatenate(
        [jnp.where(same, value, 0) for value in ((cell >> 7) + 1, cell & 127, sub, dest * 0)], axis=0
    )
    meta = dot_t(narrow(meta), pick_ref[...])
    code = (meta[0:8] * 128.0 + meta[8:16]).astype(I32) * 256 + meta[16:24].astype(I32)
    spread_by = lax.rem(lat, 4)
    mine = iota((8, 128), 1) // 32 == spread_by
    for c in range(4):
        chunk = code[:, c * 128 : c * 128 + 128]
        turned = [chunk] + [pltpu.roll(chunk, 32 * k, 1) for k in range(1, 4)]
        for j in range(4):
            near = lax.rem(spread_by - j + 4, 4)
            placed = jnp.where(
                near < 2,
                jnp.where(near == 0, turned[0], turned[1]),
                jnp.where(near == 2, turned[2], turned[3]),
            )
            placed = jnp.where(mine, placed, 0)
            for g in range(8):
                sendm_ref[g * 16 + c * 4 + j] = placed[g : g + 1]

    pl.semaphore_wait(meet_sem, len(far))

    kind = lax.rem(lat + lon, 4)
    home = kind * 32 + lat

    loads[4].wait()

    @pl.loop(0, owners // 32)
    def _(turn):
        part = lax.rem(turn + kind, 4)
        group = group_ref[...]
        feat = feat_ref[...]
        wide = jnp.concatenate(
            [
                jnp.where(
                    group == jnp.full((1, 1), 2 * part + i, I32).astype(F32).astype(BF16),
                    feat,
                    jnp.zeros((), BF16),
                )
                for i in range(2)
            ],
            axis=1,
        )
        packed = dot(pick_ref[...], wide).astype(BF16)
        for i in range(2):
            sendf_ref[pl.ds((part * 2 + i) * 16, 16)] = packed[:, i * width : (i + 1) * width].reshape(
                16, 32, width
            )

        @pl.loop(0, 32)
        def _(k):
            turned = lax.rem(k * 5 + me, 32)
            group = part * 2 + lax.rem(turned, 2)
            peer = (turned // 2) * 8 + group

            @pl.when(peer != me)
            def _():
                there = place(peer)
                slot = group * 16 + turned // 2
                for i, (src, dst) in enumerate(((sendf_ref, recvf_ref), (sendm_ref, recvm_ref))):
                    pltpu.make_async_remote_copy(
                        src_ref=src.at[slot],
                        dst_ref=dst.at[home],
                        send_sem=route_sem.at[i],
                        recv_sem=arrive_sem.at[2 * turn + i],
                        device_id=there,
                        device_id_type=MESH,
                    ).start()

    own_copies = [
        pltpu.make_async_copy(src.at[lax.rem(me, 8) * 16 + me // 8], dst.at[home], own_sem.at[i])
        for i, (src, dst) in enumerate(((sendf_ref, recvf_ref), (sendm_ref, recvm_ref)))
    ]
    for copy in own_copies:
        copy.start()

    @pl.when(lat == 0)
    def _():
        brow_ref[0] = jnp.zeros((cols, channels), BF16)
        bside_ref[:, 0:8, :] = jnp.zeros((2, 8, channels), F32)
        orow_ref[0] = jnp.zeros((cols, both), BF16)
        oside_ref[:, 0:8, :] = jnp.zeros((2, 8, both), F32)
        vert_ref[0] = jnp.zeros((6, half, channels), BF16)
        side_ref[:, 0:3] = jnp.zeros((2, 3, 16, channels), BF16)

    @pl.when(lat == lat_count - 1)
    def _():
        brow_ref[1] = jnp.zeros((cols, channels), BF16)
        bside_ref[:, 8 + rows :, :] = jnp.zeros((2, 8, channels), F32)
        orow_ref[1] = jnp.zeros((cols, both), BF16)
        oside_ref[:, 8 + rows :, :] = jnp.zeros((2, 8, both), F32)
        vert_ref[1] = jnp.zeros((6, half, channels), BF16)
        side_ref[:, 9:12] = jnp.zeros((2, 3, 16, channels), BF16)

    halo_arrive(halo_back)

    def lay(taps, buffer, slot, at, line, left, right):
        size = line.shape[1]
        for c in range(size // 128):
            lanes = slice(c * 128, (c + 1) * 128)
            spot = slot * (size // 128) + c
            buffer[spot, 8 : 8 + cols, :] = line[:, lanes].astype(F32)
            if left is not None:
                buffer[spot, 7:8, :] = left[:, lanes]
                buffer[spot, 8 + cols : 9 + cols, :] = right[:, lanes]
            for tap in range(4):
                part = buffer[spot, pl.ds(7 + tap, half, stride=2), :]
                base = tap * size + c * 128
                taps[at, :, base : base + 128] = part.astype(BF16)

    for i, at in ((0, 0), (1, rows + 1)):
        lay(
            taps_ref, line_ref, i, at, brow_ref[i],
            bside_ref[0, at + 7 : at + 8, :], bside_ref[1, at + 7 : at + 8, :],
        )

    @pl.loop(0, rows // 2)
    def _(pair):
        for i in range(2):
            row = pair * 2 + i
            lay(
                taps_ref, line_ref, i, row + 1, back_ref[row],
                bside_ref[0, pl.ds(row + 8, 1), :], bside_ref[1, pl.ds(row + 8, 1), :],
            )

    loads[1].wait()
    block = 4 * half

    def window(taps, part, tap):
        return taps[pl.ds(part * 4 + tap // 2, 4), tap % 2].reshape(block, taps.shape[3])

    taps4 = taps_ref.reshape(rows // 2 + 1, 2, half, 4 * channels)
    otaps4 = otaps_ref.reshape(rows // 2 + 1, 2, half, 4 * both)

    @pl.loop(0, out_rows // 4)
    def _(part):
        total = jnp.broadcast_to(bias_in_ref[...], (block, channels))
        for tap in range(4):
            total = total + dot(window(taps4, part, tap), conv_ref[tap])
        acc_ref[pl.ds(pl.multiple_of(part * block, block), block), :] = total

    dens = jnp.broadcast_to(dens_ref[...], (16, channels))
    dens_hi = dens.astype(BF16)
    dens_lo = (dens - dens_hi.astype(F32)).astype(BF16)
    line16 = iota((16, channels), 0)
    tail = jnp.where(
        line16 == 0, dens_hi.astype(F32), jnp.where(line16 == 1, dens_lo.astype(F32), 0.0)
    ).astype(BF16)
    loads[5].wait()
    lift = jnp.concatenate([win_ref[...], tail], axis=0)

    @pl.loop(0, 4)
    def _(tap):
        for s in range(4):
            made = dot(lift, conv_ref[tap, s * channels : (s + 1) * channels, :])
            base = s * both
            comp_ref[tap, base : base + width, :] = made[:width].astype(BF16)
            whole = made[width : width + 1] + made[width + 1 : width + 2]
            upper_part = whole.astype(BF16).astype(F32)
            rest = jnp.where(
                line16 < 2, upper_part, jnp.where(line16 == 2, whole - upper_part, 0.0)
            ).astype(BF16)
            comp_ref[tap, base + width : base + width + 16, :] = rest
            comp_ref[tap, base + width + 16 : base + both, :] = jnp.zeros(
                (width - 16, channels), BF16
            )

    loads[2].wait()
    loads[3].wait()
    turned_ref[...] = wqkv_ref[:, 2 * channels :].astype(F32).T.astype(BF16)

    chunk = spread_ref.shape[0]
    lane = narrow(iota((128, 128), 1))
    sums_ref[...] = jnp.zeros(sums_ref.shape, F32)

    @pl.loop(0, 4)
    def _(turn):
        senders = lax.rem(lax.rem(me, 8) // 2 - turn + 4, 4)
        first = senders * 32

        def arrive(count):
            some = pl.ds(0, count)
            for i, (src, dst) in enumerate(((sendf_ref, recvf_ref), (sendm_ref, recvm_ref))):
                pltpu.make_async_copy(src.at[some], dst.at[some], arrive_sem.at[2 * turn + i]).wait()

        @pl.when(senders == kind)
        def _():
            arrive(31)
            for copy in own_copies:
                copy.wait()

        @pl.when(senders != kind)
        def _():
            arrive(32)

        for group in range(8):
            code = recvm_ref[first + group * 4]
            for other in range(1, 4):
                code = code + recvm_ref[first + group * 4 + other]
            codes_ref[:, group * 128 : group * 128 + 128] = code
        code = codes_ref[...]
        sub = code & 255
        cell = (code >> 8) - 128
        row_off = ((sub >> 4).astype(F32) + 0.5) / 16.0 - 0.5
        col_off = ((sub & 15).astype(F32) + 0.5) / 16.0 - 0.5
        kern = jnp.exp(-(row_off * row_off + col_off * col_off) / (2.0 * 0.35 * 0.35))
        one_hot(pick_ref.at[:, 0:chunk], cell & 511, kern.astype(BF16))
        band = cell >> 9
        for b in range(chunk // 128):
            spot = column(band[:, b * 128 : b * 128 + 128])
            feat = recvf_ref[pl.ds(first + b * 4, 4)].reshape(128, width)
            lines = slice(b * 128, b * 128 + 128)
            for g in range(rows // 4):
                here = jnp.full((1, 1), g, F32).astype(BF16)
                spread_ref[lines, g * width : (g + 1) * width] = jnp.where(
                    spot == here, feat, jnp.zeros((), BF16)
                )
            spread_ref[lines, rows // 4 * width :] = jnp.where(
                spot == lane, jnp.ones((), BF16), jnp.zeros((), BF16)
            )
        sums_ref[...] += dot(pick_ref[:, 0:chunk], spread_ref[...])

    lane_f = iota((cols, width), 1)
    for g in range(rows // 4):
        for r in range(4):
            row = g * 4 + r
            lines = slice(r * cols, (r + 1) * cols)
            density = sums_ref[lines, rows // 4 * width + g : rows // 4 * width + g + 1]
            normed = sums_ref[lines, g * width : (g + 1) * width] / (density + 1.0)
            high = density.astype(BF16).astype(F32)
            marks = jnp.where(
                (lane_f == 0) | (lane_f == 2), high, jnp.where(lane_f == 1, density - high, 0.0)
            )
            line = jnp.concatenate([normed, marks], axis=1)
            oedge_ref[0, row : row + 1, :] = line[0:1]
            oedge_ref[1, row : row + 1, :] = line[cols - 1 : cols]
            if row == 0:
                orow_ref[2] = line.astype(BF16)
            if row == rows - 1:
                orow_ref[3] = line.astype(BF16)
            lay(otaps_ref, oline_ref, row % 2, row + 1, line, None, None)

    halo_obs = halo(8, fine_parts(orow_ref.at[2], orow_ref.at[3], oedge_ref, orow_ref, oside_ref))
    halo_start(halo_obs)

    middle = slice(both, 3 * both)
    for part in (1, 0, 2):
        lines = slice(part * block, (part + 1) * block)
        total = acc_ref[lines, :]
        for tap in range(4):
            if (part, tap) not in ((0, 0), (out_rows // 4 - 1, 3)):
                total = total + dot(window(otaps4, part, tap)[:, middle], comp_ref[tap, middle, :])
        acc_ref[lines, :] = total

    no_up = jnp.where(lat == 0, NEG, 0.0)
    no_down = jnp.where(lat == lat_count - 1, NEG, 0.0)
    strip_ref[...] = jnp.full(strip_ref.shape, NEG, F32)
    for r in range(rel_ref.shape[0]):
        strip_ref[:, r * 32 : r * 32 + rel_ref.shape[2]] = rel_ref[r] * LOG2E
    lane256 = iota((16, 256), 1)

    @pl.loop(0, HEADS // 2)
    def _(pair):
        places = pl.ds(pl.multiple_of(pair * 128, 128), 128)
        for down in range(out_rows // 4):
            inner_part, outer_part = [], []
            for i in range(2):
                strip = jnp.broadcast_to(strip_ref[pl.ds(2 * pair + i, 1), :], (16, 640))
                for r in range(4):

                    def shifted(first_row, lead, size):
                        amount = (2 + 32 * (r + 4 * down - first_row) + lead) % 640
                        return pltpu.roll(strip, amount, 1, stride=1, stride_axis=0)[:, :size]

                    inner_part.append(shifted(6, 0, 384))
                    if down == 0:
                        found = jnp.where(lane256 < 192, shifted(0, 0, 256) + no_up, NEG)
                    elif down == 1:
                        found = jnp.where(
                            lane256 < 64,
                            shifted(4, 0, 256) + no_up,
                            jnp.where(lane256 < 128, shifted(18, 64, 256) + no_down, NEG),
                        )
                    else:
                        found = jnp.where(lane256 < 64, NEG, shifted(18, 64, 256) + no_down)
                    outer_part.append(found)
            bias_ref[down, :, places] = jnp.concatenate(inner_part, axis=0).T
            rim_ref[down, :, places] = jnp.concatenate(outer_part, axis=0).T

    halo_arrive(halo_obs)
    for i, at in ((0, 0), (1, rows + 1)):
        lay(otaps_ref, oline_ref, i, at, orow_ref[i], None, None)
    first_line = iota((16, both), 0) == 0
    last_line = iota((16, both), 0) == 15
    @pl.loop(0, rows + 2)
    def _(at):
        old = otaps_ref[at, 0:16, 0:both].astype(F32)
        otaps_ref[at, 0:16, 0:both] = jnp.where(
            first_line, oside_ref[0, pl.ds(at + 7, 1), :], old
        ).astype(BF16)
        old = otaps_ref[at, half - 16 : half, 3 * both :].astype(F32)
        otaps_ref[at, half - 16 : half, 3 * both :] = jnp.where(
            last_line, oside_ref[1, pl.ds(at + 7, 1), :], old
        ).astype(BF16)

    outer = (slice(0, both), slice(3 * both, 4 * both))

    def finish(part):
        lines = slice(part * block, (part + 1) * block)
        total = acc_ref[lines, :]
        for tap in range(4):
            view = window(otaps4, part, tap)
            if (part, tap) in ((0, 0), (out_rows // 4 - 1, 3)):
                total = total + dot(view, comp_ref[tap])
            else:
                for lanes in outer:
                    total = total + dot(view[:, lanes], comp_ref[tap, lanes, :])
        inner = 0.7978845608028654 * (total + 0.044715 * total * total * total)
        coarse = (0.5 * total * (1.0 + jnp.tanh(inner))).astype(BF16)
        coarse_ref[part * 4 : part * 4 + 4] = coarse.reshape(4, half, channels)
        value = coarse.astype(F32)
        scale = lax.rsqrt(jnp.mean(value * value, axis=1, keepdims=True) + 1e-05)
        normed = value * scale * gain_ref[...]
        own_ref[part * 4 : part * 4 + 4] = normed.astype(BF16).reshape(4, half, channels)
        ext_ref[part * 4 : part * 4 + 4, 8 : 8 + half, :] = normed.reshape(4, half, channels).astype(BF16)
        for side, at in ((0, 0), (1, half - 8)):
            for pair in range(2):
                first = pair * 2 * half + at
                both_rows = jnp.concatenate(
                    [normed[first : first + 8], normed[first + half : first + half + 8]], axis=0
                )
                sside_ref[side, part * 2 + pair] = both_rows.astype(BF16)

    def rim(first, count, side):
        return sside_ref.at[side, pl.ds(first, count)]

    def gap(first, count, side):
        return side_ref.at[side, pl.ds(first, count)]

    finish(0)
    halo_first = halo(
        16,
        (
            ((0, -1), rim(0, 2, 0), gap(3, 2, 1)),
            ((0, 1), rim(0, 2, 1), gap(3, 2, 0)),
            ((-1, 0), own_ref.at[pl.ds(0, 4)], vert_ref.at[1, pl.ds(0, 4)]),
        ),
    )
    halo_start(halo_first)
    finish(2)
    halo_second = halo(
        21,
        (
            ((0, -1), rim(4, 2, 0), gap(7, 2, 1)),
            ((0, 1), rim(4, 2, 1), gap(7, 2, 0)),
            ((1, 0), own_ref.at[pl.ds(8, 4)], vert_ref.at[0, pl.ds(2, 4)]),
        ),
    )
    halo_start(halo_second)
    finish(1)
    halo_third = halo(
        26,
        (
            ((0, -1), rim(2, 2, 0), gap(5, 2, 1)),
            ((0, 1), rim(2, 2, 1), gap(5, 2, 0)),
            ((-1, 0), own_ref.at[pl.ds(4, 2)], vert_ref.at[1, pl.ds(4, 2)]),
            ((1, 0), own_ref.at[pl.ds(6, 2)], vert_ref.at[0, pl.ds(0, 2)]),
        ),
    )
    halo_start(halo_third)
    halo_norm = halo_first + halo_second + halo_third
    halo_side = halo_first[:2] + halo_second[:2] + halo_third[:2]
    halo_far = halo_first[2:] + halo_second[2:] + halo_third[2:]

    @pl.loop(0, out_rows // 4)
    def _(part):
        own = own_ref[pl.ds(part * 4, 4)].reshape(block, channels)
        query = dot(own, wqkv_ref[:, :channels]) * (0.125 * LOG2E)
        query_ref[pl.ds(part * 4, 4)] = query.astype(BF16).reshape(4, half, channels)

    half_ch = channels // 2
    lane_head = iota((64, half_ch), 1) // (channels // HEADS)
    same_half = iota((128, 128), 0) // 64 == iota((128, 128), 1) // 64

    def keys_values(x):
        keys = dot(x, wqkv_ref[:, channels : 2 * channels]).astype(BF16)
        return keys, dot_t(turned_ref[...], x).astype(BF16)

    def queries(down, c0, lanes):
        wide = query_ref[pl.ds(down * 4, 4), pl.ds(c0, 16), lanes].reshape(64, half_ch)
        return jnp.concatenate(
            [jnp.where(lane_head == h, wide, jnp.zeros((), BF16)) for h in range(4)], axis=0
        )

    corners = [
        ((way, 0), side_ref.at[i, pl.ds(start, 3)], side_ref.at[i, pl.ds(stop, 3)])
        for i in range(2)
        for way, start, stop in ((-1, 3, 9), (1, 6, 0))
    ]

    tall = 32 * out_rows

    @pl.loop(0, half // 16)
    def _(turn):
        across = lax.rem(turn + 1, half // 16)

        @pl.when(turn == half // 16 - 2)
        def _():
            halo_arrive(halo_side)
            halo_start(halo(34, corners))
            for i, at in ((0, 0), (1, 8 + half)):
                x = side_ref[i, 3 : 3 + out_rows // 2].astype(F32).reshape(out_rows, 8, channels)
                ext_ref[:, at : at + 8, :] = x.astype(BF16)

        c0 = pl.multiple_of(across * 16, 16)
        keys, values = keys_values(ext_ref[:, pl.ds(c0, 32), :].reshape(tall, channels))
        keys_ref[0:tall, :] = keys
        values_ref[:, 0:tall] = values

        @pl.loop(0, out_rows // 4)
        def _(down):
            spot = down * (half // 16) + across
            for g in range(2):
                lanes = slice(g * half_ch, (g + 1) * half_ch)
                scores = dot_t(keys_ref[0:tall, lanes], queries(down, c0, lanes)) + bias_ref[down, :, lanes]
                peak = jnp.max(scores, axis=0, keepdims=True)
                weight = jnp.exp2(scores - peak)
                stat_ref[spot, 0:1, lanes] = peak
                stat_ref[spot, 1:2, lanes] = jnp.sum(weight, axis=0, keepdims=True)
                mixed = dot(values_ref[lanes, 0:tall], weight.astype(BF16))
                for p in range(2):
                    cut = slice(p * 128, p * 128 + 128)
                    held_ref[spot, g * half_ch + p * 128 : g * half_ch + p * 128 + 128, :] = mixed[cut, cut]

    halo_corner = halo(34, corners)

    def out_copy(across):
        some = pl.ds(pl.multiple_of(across * 16, 16), 16)
        return pltpu.make_async_copy(out_ref.at[:, some], out_hbm.at[:, some], out_sem.at[across])

    halo_arrive(halo_far + halo_corner)
    for i in range(2):
        seg = slice(0, 3) if i == 0 else slice(3 + out_rows // 2, 6 + out_rows // 2)
        far_ref[i, :, 8 : 8 + half, :] = vert_ref[i].astype(F32).astype(BF16)
        for j, at in ((0, 0), (1, 8 + half)):
            x = side_ref[j, seg].astype(F32).reshape(6, 8, channels)
            far_ref[i, :, at : at + 8, :] = x.astype(BF16)

    @pl.loop(0, half // 16)
    def _(across):
        c0 = pl.multiple_of(across * 16, 16)
        above = far_ref[0, :, pl.ds(c0, 32), :].reshape(192, channels)
        below = far_ref[1, :, pl.ds(c0, 32), :].reshape(192, channels)
        keys, values = keys_values(jnp.concatenate([above[128:], below[:64], above, below], axis=0))
        keys_ref[...] = keys
        values_ref[...] = values

        @pl.loop(0, out_rows // 4)
        def _(down):
            seg = pl.ds(pl.multiple_of(lax.rem(2 * down + 1, 3) * 128, 128), 256)
            spot = down * (half // 16) + across
            parts = []
            for g in range(2):
                lanes = slice(g * half_ch, (g + 1) * half_ch)
                scores = dot_t(keys_ref[seg, lanes], queries(down, c0, lanes)) + rim_ref[down, :, lanes]
                old_peak, old_norm = stat_ref[spot, 0:1, lanes], stat_ref[spot, 1:2, lanes]
                peak = jnp.maximum(old_peak, jnp.max(scores, axis=0, keepdims=True))
                weight = jnp.exp2(scores - peak)
                fade = jnp.exp2(old_peak - peak)
                inverse = 1.0 / (old_norm * fade + jnp.sum(weight, axis=0, keepdims=True))
                fade = fade * inverse
                mixed = dot(values_ref[lanes, seg], weight.astype(BF16))
                for p in range(2):
                    cut = slice(p * 128, p * 128 + 128)
                    held = held_ref[spot, g * half_ch + p * 128 : g * half_ch + p * 128 + 128, :]
                    total = held * fade[:, cut] + mixed[cut, cut] * inverse[:, cut]
                    parts.append(jnp.where(same_half, total, 0.0).T.astype(BF16))
            lifted = dot(jnp.concatenate(parts, axis=1), wout_ref[...])
            base = coarse_ref[pl.ds(down * 4, 4), pl.ds(c0, 16), :].astype(F32)
            result = base + (lifted[:64] + lifted[64:]).reshape(4, 16, channels)
            out_ref[pl.ds(down * 4, 4), pl.ds(c0, 16), :] = result.astype(BF16)

        out_copy(across).start()

    @pl.loop(0, half // 16)
    def _(across):
        out_copy(across).wait()

    rest = pl.ds(0, owners - 1)
    for i, (src, dst) in enumerate(((sendf_ref, recvf_ref), (sendm_ref, recvm_ref))):
        pltpu.make_async_copy(src.at[rest], dst.at[rest], route_sem.at[i]).wait()
    for copies in (halo_back, halo_obs, halo_norm, halo_corner):
        halo_sent(copies)


def body(
    obs_feat, obs_dest, obs_cell, obs_sub, background, w_in, dens_vec,
    conv_w, conv_b, norm_gain, w_qkv, rel_bias, w_out,
):
    owners = lax.axis_size("lat") * lax.axis_size("lon")
    rows, cols, channels = background.shape
    obs, width = obs_feat.shape
    half, out_rows, both = cols // 2, rows // 2, 2 * width
    vmem = pl.BlockSpec(memory_space=pltpu.VMEM)
    hbm = pl.BlockSpec(memory_space=pl.ANY)
    scratch = [
        ((obs, width), BF16),
        ((width, channels), BF16),
        ((out_rows, half, channels), BF16),
        ((rows, cols, channels), BF16),
        ((4, 4 * channels, channels), BF16),
        ((channels, 3 * channels), BF16),
        ((channels, channels), BF16),
        ((owners, 32, width), BF16),
        ((owners, 1, 128), I32),
        ((owners, 32, width), BF16),
        ((owners, 1, 128), I32),
        ((512, obs), BF16),
        ((obs, width), BF16),
        ((1, obs), I32),
        ((2, rows, channels), F32),
        ((2, cols, channels), BF16),
        ((2, rows + 16, channels), F32),
        ((2 * channels // 128, cols + 16, 128), F32),
        ((rows + 2, half, 4 * channels), BF16),
        ((half * out_rows, channels), F32),
        ((4, 4 * both, channels), BF16),
        ((1, owners * 8), I32),
        ((owners * 8, rows // 4 * width + 128), BF16),
        ((512, rows // 4 * width + 128), F32),
        ((2, rows, both), F32),
        ((2 * both // 128, cols + 16, 128), F32),
        ((4, cols, both), BF16),
        ((2, rows + 16, both), F32),
        ((rows + 2, half, 4 * both), BF16),
        ((out_rows, half, channels), BF16),
        ((out_rows, half, channels), BF16),
        ((2, 6, half, channels), BF16),
        ((2, out_rows // 2 + 6, 16, channels), BF16),
        ((2, out_rows // 2, 16, channels), BF16),
        ((out_rows, half, channels), BF16),
        ((out_rows, half + 16, channels), BF16),
        ((out_rows // 4, 384, HEADS * 64), F32),
        ((out_rows // 4, 256, HEADS * 64), F32),
        ((2, 6, half + 16, channels), BF16),
        ((channels, channels), BF16),
        ((out_rows * half // 64, channels, 128), F32),
        ((out_rows * half // 64, 8, channels), F32),
        ((HEADS, 640), F32),
        ((512, channels), BF16),
        ((channels, 512), BF16),
    ]
    sems = [pltpu.SemaphoreType.DMA((n,)) for n in (6, 2, 8, 2, half // 16, 38, 38)]
    sems.append(pltpu.SemaphoreType.REGULAR)
    return pl.pallas_call(
        main_kernel,
        name="main",
        out_shape=jax.ShapeDtypeStruct((out_rows, half, channels), BF16),
        in_specs=[vmem, vmem, vmem, hbm, hbm, hbm, vmem, hbm, vmem, vmem, hbm, vmem, hbm],
        out_specs=hbm,
        scratch_shapes=[pltpu.VMEM(shape, dtype) for shape, dtype in scratch] + sems,
        compiler_params=pltpu.CompilerParams(
            collective_id=0, has_side_effects=True, vmem_limit_bytes=62 << 20
        ),
    )(
        obs_dest.reshape(1, obs),
        obs_cell.reshape(1, obs),
        obs_sub.reshape(1, obs),
        obs_feat,
        background,
        w_in,
        dens_vec.reshape(1, channels),
        conv_w.reshape(4, 4 * channels, channels),
        conv_b.reshape(1, channels),
        norm_gain.reshape(1, channels),
        w_qkv,
        jnp.transpose(rel_bias, (1, 0, 2)),
        w_out,
    )


def solution(mesh):
    split = P(("lat", "lon"))
    wide = P(("lat", "lon"), None)
    tile = P("lat", "lon", None)
    in_specs = (wide, wide, split, split, tile) + (P(),) * 8
    return jax.shard_map(body, mesh=mesh, in_specs=in_specs, out_specs=tile, check_vma=False)
```

```python
import jax
import jax.numpy as jnp
from jax import lax
from jax.experimental import pallas as pl
from jax.experimental.pallas import tpu as pltpu
from jax.sharding import PartitionSpec as P

HEADS = 8
F32 = jnp.float32
BF16 = jnp.bfloat16
I32 = jnp.int32
NEG = -1e30
LOG2E = 1.4426950408889634
MESH = pl.DeviceIdType.MESH
WAYS = ((-1, 0), (1, 0), (0, -1), (0, 1), (-1, -1), (-1, 1), (1, -1), (1, 1))


def iota(shape, dim):
    return lax.broadcasted_iota(I32, shape, dim)


def narrow(x):
    return x.astype(F32).astype(BF16)


def dot(x, y):
    return jnp.dot(x, y, preferred_element_type=F32)


def dot_t(x, y):
    return lax.dot_general(x, y, (((1,), (1,)), ((), ())), preferred_element_type=F32)


def column(row):
    return jnp.broadcast_to(row.astype(F32), (128, 128)).T.astype(BF16)


def one_hot(place_ref, index, value):
    for part in range(place_ref.shape[0] // 256):
        local = index - part * 256
        local = narrow(jnp.where((local >= 0) & (local < 256), local, -1))
        line = narrow(iota((256, index.shape[1]), 0))
        place_ref[part * 256 : part * 256 + 256, :] = jnp.where(
            line == local, value, jnp.zeros((), BF16)
        )


def main_kernel(
    dest_ref, cell_ref, sub_ref, feat_hbm, back_hbm, win_hbm, dens_ref, conv_hbm, bias_in_ref,
    gain_ref, wqkv_hbm, rel_ref, wout_hbm,
    out_hbm,
    feat_ref, win_ref, out_ref, back_ref, conv_ref, wqkv_ref, wout_ref,
    sendf_ref, sendm_ref, recvf_ref, recvm_ref, pick_ref, group_ref, local_ref,
    edge_ref, brow_ref, bside_ref, line_ref, taps_ref, acc_ref, comp_ref,
    codes_ref, spread_ref, sums_ref, oedge_ref, oline_ref, orow_ref, oside_ref, otaps_ref,
    own_ref, coarse_ref, vert_ref, side_ref, sside_ref, query_ref, ext_ref, bias_ref, rim_ref,
    far_ref, turned_ref, held_ref, stat_ref, strip_ref,
    load_sem, route_sem, arrive_sem, own_sem, out_sem, halo_send, halo_recv, meet_sem,
):
    obs, width = feat_ref.shape
    owners = sendf_ref.shape[0]
    slots = owners * 32
    rows, cols, channels = back_ref.shape
    half = cols // 2
    out_rows = rows // 2
    both = 2 * width
    lat_count, lon_count = lax.axis_size("lat"), lax.axis_size("lon")
    lat, lon = lax.axis_index("lat"), lax.axis_index("lon")
    me = lat * lon_count + lon

    loads = [
        pltpu.make_async_copy(src, dst, load_sem.at[i])
        for i, (src, dst) in enumerate(
            (
                (back_hbm, back_ref),
                (conv_hbm, conv_ref),
                (wqkv_hbm, wqkv_ref),
                (wout_hbm, wout_ref),
                (feat_hbm, feat_ref),
                (win_hbm, win_ref),
            )
        )
    ]
    for i in (0, 4, 5, 1, 2, 3):
        loads[i].start()

    def inside(da):
        return (lat + da >= 0) & (lat + da < lat_count)

    def place(device):
        return device // lon_count, lax.rem(device, lon_count)

    barrier = pltpu.get_barrier_semaphore()
    near = [me ^ j for j in range(1, 16)]
    far = [me ^ (16 * j) for j in range(1, owners // 16)]

    def greet(where):
        pl.semaphore_signal(barrier, inc=1, device_id=where, device_id_type=MESH)

    for da, db in WAYS:
        there = (lat + da, lax.rem(lon + db + lon_count, lon_count))
        if da == 0:
            greet(there)
        else:
            pl.when(inside(da))(lambda: greet(there))
    for device in near + far:
        greet(place(device))

    def halo(base, parts):
        copies = []
        for i, ((da, db), src, dst) in enumerate(parts):
            copies.append(
                (
                    da,
                    pltpu.make_async_remote_copy(
                        src_ref=src,
                        dst_ref=dst,
                        send_sem=halo_send.at[base + i],
                        recv_sem=halo_recv.at[base + i],
                        device_id=(lat + da, lax.rem(lon + db + lon_count, lon_count)),
                        device_id_type=MESH,
                    ),
                )
            )
        return copies

    def halo_start(copies):
        for da, copy in copies:
            pl.when(inside(da))(copy.start)

    def halo_arrive(copies):
        for da, copy in copies:
            pl.when(inside(-da))(copy.wait_recv)

    def halo_sent(copies):
        for da, copy in copies:
            pl.when(inside(da))(copy.wait_send)

    loads[0].wait()
    for row in range(rows):
        tile = back_ref[row, 0:16, :].astype(F32)
        edge_ref[0, row : row + 1, :] = tile[0:1]
        tile = back_ref[row, cols - 16 : cols, :].astype(F32)
        edge_ref[1, row : row + 1, :] = tile[15:16]

    neighbours = 2 + 3 * (inside(-1).astype(I32) + inside(1).astype(I32))
    pl.semaphore_wait(barrier, len(near) + len(far) + neighbours)
    for device in far:
        pl.semaphore_signal(meet_sem, inc=1, device_id=place(device), device_id_type=MESH)

    def fine_parts(first, last, edge, row, side):
        top, bottom = pl.ds(0, 8), pl.ds(rows - 8, 8)
        return (
            ((-1, 0), first, row.at[1]),
            ((1, 0), last, row.at[0]),
            ((0, -1), edge.at[0], side.at[1, pl.ds(8, rows)]),
            ((0, 1), edge.at[1], side.at[0, pl.ds(8, rows)]),
            ((-1, -1), edge.at[0, top], side.at[1, pl.ds(8 + rows, 8)]),
            ((-1, 1), edge.at[1, top], side.at[0, pl.ds(8 + rows, 8)]),
            ((1, -1), edge.at[0, bottom], side.at[1, pl.ds(0, 8)]),
            ((1, 1), edge.at[1, bottom], side.at[0, pl.ds(0, 8)]),
        )

    halo_back = halo(0, fine_parts(back_ref.at[0], back_ref.at[rows - 1], edge_ref, brow_ref, bside_ref))
    halo_start(halo_back)

    step = 256
    upper = (iota((step, step), 0) < iota((step, step), 1)).astype(F32).astype(BF16)
    running = jnp.zeros((owners, 1), F32)
    for at in range(0, obs, step):
        dest = dest_ref[:, at : at + step]
        member = (iota((owners, step), 0) == dest).astype(F32)
        earlier = dot(member.astype(BF16), upper) + running
        rank = jnp.sum(member * earlier, axis=0, keepdims=True)
        running = running + jnp.sum(member, axis=1, keepdims=True)
        local_ref[:, at : at + step] = (dest >> 3) * 32 + rank.astype(I32)
        for more in range(0, step, 128):
            group_ref[at + more : at + more + 128, :] = column(dest[:, more : more + 128] & 7)
    one_hot(pick_ref, local_ref[...], jnp.ones((), BF16))

    dest, cell, sub = dest_ref[...], cell_ref[...], sub_ref[...]
    same = iota((8, obs), 0) == (dest & 7)
    meta = jnp.concatenate(
        [jnp.where(same, value, 0) for value in ((cell >> 7) + 1, cell & 127, sub, dest * 0)], axis=0
    )
    meta = dot_t(narrow(meta), pick_ref[...])
    code = (meta[0:8] * 128.0 + meta[8:16]).astype(I32) * 256 + meta[16:24].astype(I32)
    spread_by = lax.rem(lat, 4)
    mine = iota((8, 128), 1) // 32 == spread_by
    for c in range(4):
        chunk = code[:, c * 128 : c * 128 + 128]
        turned = [chunk] + [pltpu.roll(chunk, 32 * k, 1) for k in range(1, 4)]
        for j in range(4):
            near = lax.rem(spread_by - j + 4, 4)
            placed = jnp.where(
                near < 2,
                jnp.where(near == 0, turned[0], turned[1]),
                jnp.where(near == 2, turned[2], turned[3]),
            )
            placed = jnp.where(mine, placed, 0)
            for g in range(8):
                sendm_ref[g * 16 + c * 4 + j] = placed[g : g + 1]

    pl.semaphore_wait(meet_sem, len(far))

    kind = lax.rem(lat + lon, 4)
    home = kind * 32 + lat

    loads[4].wait()

    @pl.loop(0, owners // 32)
    def _(turn):
        part = lax.rem(turn + kind, 4)
        group = group_ref[...]
        feat = feat_ref[...]
        wide = jnp.concatenate(
            [
                jnp.where(
                    group == jnp.full((1, 1), 2 * part + i, I32).astype(F32).astype(BF16),
                    feat,
                    jnp.zeros((), BF16),
                )
                for i in range(2)
            ],
            axis=1,
        )
        packed = dot(pick_ref[...], wide).astype(BF16)
        for i in range(2):
            sendf_ref[pl.ds((part * 2 + i) * 16, 16)] = packed[:, i * width : (i + 1) * width].reshape(
                16, 32, width
            )

        @pl.loop(0, 32)
        def _(k):
            turned = lax.rem(k * 5 + me, 32)
            group = part * 2 + lax.rem(turned, 2)
            peer = (turned // 2) * 8 + group

            @pl.when(peer != me)
            def _():
                there = place(peer)
                slot = group * 16 + turned // 2
                for i, (src, dst) in enumerate(((sendf_ref, recvf_ref), (sendm_ref, recvm_ref))):
                    pltpu.make_async_remote_copy(
                        src_ref=src.at[slot],
                        dst_ref=dst.at[home],
                        send_sem=route_sem.at[i],
                        recv_sem=arrive_sem.at[2 * turn + i],
                        device_id=there,
                        device_id_type=MESH,
                    ).start()

    own_copies = [
        pltpu.make_async_copy(src.at[lax.rem(me, 8) * 16 + me // 8], dst.at[home], own_sem.at[i])
        for i, (src, dst) in enumerate(((sendf_ref, recvf_ref), (sendm_ref, recvm_ref)))
    ]
    for copy in own_copies:
        copy.start()

    @pl.when(lat == 0)
    def _():
        brow_ref[0] = jnp.zeros((cols, channels), BF16)
        bside_ref[:, 0:8, :] = jnp.zeros((2, 8, channels), F32)
        orow_ref[0] = jnp.zeros((cols, both), BF16)
        oside_ref[:, 0:8, :] = jnp.zeros((2, 8, both), F32)
        vert_ref[0] = jnp.zeros((6, half, channels), BF16)
        side_ref[:, 0:3] = jnp.zeros((2, 3, 16, channels), BF16)

    @pl.when(lat == lat_count - 1)
    def _():
        brow_ref[1] = jnp.zeros((cols, channels), BF16)
        bside_ref[:, 8 + rows :, :] = jnp.zeros((2, 8, channels), F32)
        orow_ref[1] = jnp.zeros((cols, both), BF16)
        oside_ref[:, 8 + rows :, :] = jnp.zeros((2, 8, both), F32)
        vert_ref[1] = jnp.zeros((6, half, channels), BF16)
        side_ref[:, 9:12] = jnp.zeros((2, 3, 16, channels), BF16)

    halo_arrive(halo_back)

    def lay(taps, buffer, slot, at, line, left, right):
        size = line.shape[1]
        for c in range(size // 128):
            lanes = slice(c * 128, (c + 1) * 128)
            spot = slot * (size // 128) + c
            buffer[spot, 8 : 8 + cols, :] = line[:, lanes].astype(F32)
            if left is not None:
                buffer[spot, 7:8, :] = left[:, lanes]
                buffer[spot, 8 + cols : 9 + cols, :] = right[:, lanes]
            for tap in range(4):
                part = buffer[spot, pl.ds(7 + tap, half, stride=2), :]
                base = tap * size + c * 128
                taps[at, :, base : base + 128] = part.astype(BF16)

    for i, at in ((0, 0), (1, rows + 1)):
        lay(
            taps_ref, line_ref, i, at, brow_ref[i],
            bside_ref[0, at + 7 : at + 8, :], bside_ref[1, at + 7 : at + 8, :],
        )

    @pl.loop(0, rows // 2)
    def _(pair):
        for i in range(2):
            row = pair * 2 + i
            lay(
                taps_ref, line_ref, i, row + 1, back_ref[row],
                bside_ref[0, pl.ds(row + 8, 1), :], bside_ref[1, pl.ds(row + 8, 1), :],
            )

    loads[1].wait()
    block = 4 * half

    def window(taps, part, tap):
        return taps[pl.ds(part * 4 + tap // 2, 4), tap % 2].reshape(block, taps.shape[3])

    taps4 = taps_ref.reshape(rows // 2 + 1, 2, half, 4 * channels)
    otaps4 = otaps_ref.reshape(rows // 2 + 1, 2, half, 4 * both)

    @pl.loop(0, out_rows // 4)
    def _(part):
        total = jnp.broadcast_to(bias_in_ref[...], (block, channels))
        for tap in range(4):
            total = total + dot(window(taps4, part, tap), conv_ref[tap])
        acc_ref[pl.ds(pl.multiple_of(part * block, block), block), :] = total

    dens = jnp.broadcast_to(dens_ref[...], (16, channels))
    dens_hi = dens.astype(BF16)
    dens_lo = (dens - dens_hi.astype(F32)).astype(BF16)
    line16 = iota((16, channels), 0)
    tail = jnp.where(
        line16 == 0, dens_hi.astype(F32), jnp.where(line16 == 1, dens_lo.astype(F32), 0.0)
    ).astype(BF16)
    loads[5].wait()
    lift = jnp.concatenate([win_ref[...], tail], axis=0)

    @pl.loop(0, 4)
    def _(tap):
        for s in range(4):
            made = dot(lift, conv_ref[tap, s * channels : (s + 1) * channels, :])
            base = s * both
            comp_ref[tap, base : base + width, :] = made[:width].astype(BF16)
            whole = made[width : width + 1] + made[width + 1 : width + 2]
            upper_part = whole.astype(BF16).astype(F32)
            rest = jnp.where(
                line16 < 2, upper_part, jnp.where(line16 == 2, whole - upper_part, 0.0)
            ).astype(BF16)
            comp_ref[tap, base + width : base + width + 16, :] = rest
            comp_ref[tap, base + width + 16 : base + both, :] = jnp.zeros(
                (width - 16, channels), BF16
            )

    loads[2].wait()
    loads[3].wait()
    turned_ref[...] = wqkv_ref[:, 2 * channels :].astype(F32).T.astype(BF16)

    chunk = spread_ref.shape[0]
    lane = narrow(iota((128, 128), 1))
    sums_ref[...] = jnp.zeros(sums_ref.shape, F32)

    @pl.loop(0, 4)
    def _(turn):
        senders = lax.rem(lax.rem(me, 8) // 2 - turn + 4, 4)
        first = senders * 32

        def arrive(count):
            some = pl.ds(0, count)
            for i, (src, dst) in enumerate(((sendf_ref, recvf_ref), (sendm_ref, recvm_ref))):
                pltpu.make_async_copy(src.at[some], dst.at[some], arrive_sem.at[2 * turn + i]).wait()

        @pl.when(senders == kind)
        def _():
            arrive(31)
            for copy in own_copies:
                copy.wait()

        @pl.when(senders != kind)
        def _():
            arrive(32)

        for group in range(8):
            code = recvm_ref[first + group * 4]
            for other in range(1, 4):
                code = code + recvm_ref[first + group * 4 + other]
            codes_ref[:, group * 128 : group * 128 + 128] = code
        code = codes_ref[...]
        sub = code & 255
        cell = (code >> 8) - 128
        row_off = ((sub >> 4).astype(F32) + 0.5) / 16.0 - 0.5
        col_off = ((sub & 15).astype(F32) + 0.5) / 16.0 - 0.5
        kern = jnp.exp(-(row_off * row_off + col_off * col_off) / (2.0 * 0.35 * 0.35))
        one_hot(pick_ref.at[:, 0:chunk], cell & 511, kern.astype(BF16))
        band = cell >> 9
        for b in range(chunk // 128):
            spot = column(band[:, b * 128 : b * 128 + 128])
            feat = recvf_ref[pl.ds(first + b * 4, 4)].reshape(128, width)
            lines = slice(b * 128, b * 128 + 128)
            for g in range(rows // 4):
                here = jnp.full((1, 1), g, F32).astype(BF16)
                spread_ref[lines, g * width : (g + 1) * width] = jnp.where(
                    spot == here, feat, jnp.zeros((), BF16)
                )
            spread_ref[lines, rows // 4 * width :] = jnp.where(
                spot == lane, jnp.ones((), BF16), jnp.zeros((), BF16)
            )
        sums_ref[...] += dot(pick_ref[:, 0:chunk], spread_ref[...])

    lane_f = iota((cols, width), 1)
    for g in range(rows // 4):
        for r in range(4):
            row = g * 4 + r
            lines = slice(r * cols, (r + 1) * cols)
            density = sums_ref[lines, rows // 4 * width + g : rows // 4 * width + g + 1]
            normed = sums_ref[lines, g * width : (g + 1) * width] / (density + 1.0)
            high = density.astype(BF16).astype(F32)
            marks = jnp.where(
                (lane_f == 0) | (lane_f == 2), high, jnp.where(lane_f == 1, density - high, 0.0)
            )
            line = jnp.concatenate([normed, marks], axis=1)
            oedge_ref[0, row : row + 1, :] = line[0:1]
            oedge_ref[1, row : row + 1, :] = line[cols - 1 : cols]
            if row == 0:
                orow_ref[2] = line.astype(BF16)
            if row == rows - 1:
                orow_ref[3] = line.astype(BF16)
            lay(otaps_ref, oline_ref, row % 2, row + 1, line, None, None)

    halo_obs = halo(8, fine_parts(orow_ref.at[2], orow_ref.at[3], oedge_ref, orow_ref, oside_ref))
    halo_start(halo_obs)

    middle = slice(both, 3 * both)
    for part in (1, 0, 2):
        lines = slice(part * block, (part + 1) * block)
        total = acc_ref[lines, :]
        for tap in range(4):
            if (part, tap) not in ((0, 0), (out_rows // 4 - 1, 3)):
                total = total + dot(window(otaps4, part, tap)[:, middle], comp_ref[tap, middle, :])
        acc_ref[lines, :] = total

    no_up = jnp.where(lat == 0, NEG, 0.0)
    no_down = jnp.where(lat == lat_count - 1, NEG, 0.0)
    strip_ref[...] = jnp.full(strip_ref.shape, NEG, F32)
    for r in range(rel_ref.shape[0]):
        strip_ref[:, r * 32 : r * 32 + rel_ref.shape[2]] = rel_ref[r] * LOG2E
    lane256 = iota((16, 256), 1)
    for pair in range(HEADS // 2):
        places = slice(pair * 128, pair * 128 + 128)
        for down in range(out_rows // 4):
            inner_part, outer_part = [], []
            for h in (2 * pair, 2 * pair + 1):
                strip = jnp.broadcast_to(strip_ref[h : h + 1, :], (16, 640))
                for r in range(4):

                    def shifted(first_row, lead, size):
                        amount = (2 + 32 * (r + 4 * down - first_row) + lead) % 640
                        return pltpu.roll(strip, amount, 1, stride=1, stride_axis=0)[:, :size]

                    inner_part.append(shifted(6, 0, 384))
                    if down == 0:
                        outer_part.append(shifted(0, 0, 256) + no_up)
                    elif down == 1:
                        outer_part.append(
                            jnp.where(
                                lane256 < 64, shifted(4, 0, 256) + no_up, shifted(18, 64, 256) + no_down
                            )
                        )
                    else:
                        outer_part.append(jnp.where(lane256 < 64, NEG, shifted(18, 64, 256) + no_down))
            bias_ref[down, :, places] = jnp.concatenate(inner_part, axis=0).T
            rim_ref[down, :, places] = jnp.concatenate(outer_part, axis=0).T

    halo_arrive(halo_obs)
    for i, at in ((0, 0), (1, rows + 1)):
        lay(otaps_ref, oline_ref, i, at, orow_ref[i], None, None)
    first_line = iota((16, both), 0) == 0
    last_line = iota((16, both), 0) == 15
    for at in range(rows + 2):
        old = otaps_ref[at, 0:16, 0:both].astype(F32)
        otaps_ref[at, 0:16, 0:both] = jnp.where(
            first_line, oside_ref[0, at + 7 : at + 8, :], old
        ).astype(BF16)
        old = otaps_ref[at, half - 16 : half, 3 * both :].astype(F32)
        otaps_ref[at, half - 16 : half, 3 * both :] = jnp.where(
            last_line, oside_ref[1, at + 7 : at + 8, :], old
        ).astype(BF16)


    outer = (slice(0, both), slice(3 * both, 4 * both))

    def finish(part):
        lines = slice(part * block, (part + 1) * block)
        total = acc_ref[lines, :]
        for tap in range(4):
            view = window(otaps4, part, tap)
            if (part, tap) in ((0, 0), (out_rows // 4 - 1, 3)):
                total = total + dot(view, comp_ref[tap])
            else:
                for lanes in outer:
                    total = total + dot(view[:, lanes], comp_ref[tap, lanes, :])
        inner = 0.7978845608028654 * (total + 0.044715 * total * total * total)
        coarse = (0.5 * total * (1.0 + jnp.tanh(inner))).astype(BF16)
        coarse_ref[part * 4 : part * 4 + 4] = coarse.reshape(4, half, channels)
        value = coarse.astype(F32)
        scale = lax.rsqrt(jnp.mean(value * value, axis=1, keepdims=True) + 1e-05)
        normed = value * scale * gain_ref[...]
        own_ref[part * 4 : part * 4 + 4] = normed.astype(BF16).reshape(4, half, channels)
        ext_ref[part * 4 : part * 4 + 4, 8 : 8 + half, :] = normed.reshape(4, half, channels).astype(BF16)
        for side, at in ((0, 0), (1, half - 8)):
            for pair in range(2):
                first = pair * 2 * half + at
                both_rows = jnp.concatenate(
                    [normed[first : first + 8], normed[first + half : first + half + 8]], axis=0
                )
                sside_ref[side, part * 2 + pair] = both_rows.astype(BF16)

    def rim(first, count, side):
        return sside_ref.at[side, pl.ds(first, count)]

    def gap(first, count, side):
        return side_ref.at[side, pl.ds(first, count)]

    finish(0)
    halo_first = halo(
        16,
        (
            ((0, -1), rim(0, 2, 0), gap(3, 2, 1)),
            ((0, 1), rim(0, 2, 1), gap(3, 2, 0)),
            ((-1, 0), own_ref.at[pl.ds(0, 4)], vert_ref.at[1, pl.ds(0, 4)]),
        ),
    )
    halo_start(halo_first)
    finish(2)
    halo_second = halo(
        21,
        (
            ((0, -1), rim(4, 2, 0), gap(7, 2, 1)),
            ((0, 1), rim(4, 2, 1), gap(7, 2, 0)),
            ((1, 0), own_ref.at[pl.ds(8, 4)], vert_ref.at[0, pl.ds(2, 4)]),
        ),
    )
    halo_start(halo_second)
    finish(1)
    halo_third = halo(
        26,
        (
            ((0, -1), rim(2, 2, 0), gap(5, 2, 1)),
            ((0, 1), rim(2, 2, 1), gap(5, 2, 0)),
            ((-1, 0), own_ref.at[pl.ds(4, 2)], vert_ref.at[1, pl.ds(4, 2)]),
            ((1, 0), own_ref.at[pl.ds(6, 2)], vert_ref.at[0, pl.ds(0, 2)]),
        ),
    )
    halo_start(halo_third)
    halo_norm = halo_first + halo_second + halo_third
    halo_side = halo_first[:2] + halo_second[:2] + halo_third[:2]
    halo_far = halo_first[2:] + halo_second[2:] + halo_third[2:]

    @pl.loop(0, out_rows // 4)
    def _(part):
        own = own_ref[pl.ds(part * 4, 4)].reshape(block, channels)
        query = dot(own, wqkv_ref[:, :channels]) * (0.125 * LOG2E)
        query_ref[pl.ds(part * 4, 4)] = query.astype(BF16).reshape(4, half, channels)

    half_ch = channels // 2
    lane_head = iota((64, half_ch), 1) // (channels // HEADS)
    same_half = iota((128, 128), 0) // 64 == iota((128, 128), 1) // 64

    def keys_values(x):
        keys = dot(x, wqkv_ref[:, channels : 2 * channels]).astype(BF16)
        return keys, dot_t(turned_ref[...], x).astype(BF16)

    def queries(down, c0, lanes):
        wide = query_ref[down * 4 : down * 4 + 4, pl.ds(c0, 16), lanes].reshape(64, half_ch)
        return jnp.concatenate(
            [jnp.where(lane_head == h, wide, jnp.zeros((), BF16)) for h in range(4)], axis=0
        )

    def attend_near(across):
        c0 = pl.multiple_of(across * 16, 16)
        keys, values = keys_values(ext_ref[:, pl.ds(c0, 32), :].reshape(32 * out_rows, channels))
        for down in range(out_rows // 4):
            spot = down * (half // 16) + across
            for g in range(2):
                lanes = slice(g * half_ch, (g + 1) * half_ch)
                scores = dot_t(keys[:, lanes], queries(down, c0, lanes)) + bias_ref[down, :, lanes]
                peak = jnp.max(scores, axis=0, keepdims=True)
                weight = jnp.exp2(scores - peak)
                stat_ref[spot, 0:1, lanes] = peak
                stat_ref[spot, 1:2, lanes] = jnp.sum(weight, axis=0, keepdims=True)
                mixed = dot(values[lanes], weight.astype(BF16))
                for p in range(2):
                    cut = slice(p * 128, p * 128 + 128)
                    held_ref[spot, g * half_ch + p * 128 : g * half_ch + p * 128 + 128, :] = mixed[cut, cut]

    @pl.loop(1, half // 16 - 1)
    def _(across):
        attend_near(across)

    halo_arrive(halo_side)
    halo_corner = halo(
        34,
        [
            ((way, 0), side_ref.at[i, pl.ds(start, 3)], side_ref.at[i, pl.ds(stop, 3)])
            for i in range(2)
            for way, start, stop in ((-1, 3, 9), (1, 6, 0))
        ],
    )
    halo_start(halo_corner)
    for i, at in ((0, 0), (1, 8 + half)):
        x = side_ref[i, 3 : 3 + out_rows // 2].astype(F32).reshape(out_rows, 8, channels)
        ext_ref[:, at : at + 8, :] = x.astype(BF16)

    @pl.loop(0, 2)
    def _(end):
        attend_near(end * (half // 16 - 1))

    def out_copy(across):
        some = pl.ds(pl.multiple_of(across * 16, 16), 16)
        return pltpu.make_async_copy(out_ref.at[:, some], out_hbm.at[:, some], out_sem.at[across])

    halo_arrive(halo_far + halo_corner)
    for i in range(2):
        seg = slice(0, 3) if i == 0 else slice(3 + out_rows // 2, 6 + out_rows // 2)
        far_ref[i, :, 8 : 8 + half, :] = vert_ref[i].astype(F32).astype(BF16)
        for j, at in ((0, 0), (1, 8 + half)):
            x = side_ref[j, seg].astype(F32).reshape(6, 8, channels)
            far_ref[i, :, at : at + 8, :] = x.astype(BF16)

    @pl.loop(0, half // 16)
    def _(across):
        c0 = pl.multiple_of(across * 16, 16)
        above = far_ref[0, :, pl.ds(c0, 32), :].reshape(192, channels)
        below = far_ref[1, :, pl.ds(c0, 32), :].reshape(192, channels)
        keys, values = keys_values(jnp.concatenate([above[128:], below[:64], above, below], axis=0))
        for down, seg in ((0, slice(128, 320)), (1, slice(0, 128)), (2, slice(256, 512))):
            spot = down * (half // 16) + across
            count = seg.stop - seg.start
            parts = []
            for g in range(2):
                lanes = slice(g * half_ch, (g + 1) * half_ch)
                scores = dot_t(keys[seg, lanes], queries(down, c0, lanes)) + rim_ref[down, :count, lanes]
                old_peak, old_norm = stat_ref[spot, 0:1, lanes], stat_ref[spot, 1:2, lanes]
                peak = jnp.maximum(old_peak, jnp.max(scores, axis=0, keepdims=True))
                weight = jnp.exp2(scores - peak)
                fade = jnp.exp2(old_peak - peak)
                inverse = 1.0 / (old_norm * fade + jnp.sum(weight, axis=0, keepdims=True))
                fade = fade * inverse
                mixed = dot(values[lanes, seg], weight.astype(BF16))
                for p in range(2):
                    cut = slice(p * 128, p * 128 + 128)
                    held = held_ref[spot, g * half_ch + p * 128 : g * half_ch + p * 128 + 128, :]
                    total = held * fade[:, cut] + mixed[cut, cut] * inverse[:, cut]
                    parts.append(jnp.where(same_half, total, 0.0).T.astype(BF16))
            lifted = dot(jnp.concatenate(parts, axis=1), wout_ref[...])
            base = coarse_ref[down * 4 : down * 4 + 4, pl.ds(c0, 16), :].astype(F32)
            result = base + (lifted[:64] + lifted[64:]).reshape(4, 16, channels)
            out_ref[down * 4 : down * 4 + 4, pl.ds(c0, 16), :] = result.astype(BF16)
        out_copy(across).start()

    @pl.loop(0, half // 16)
    def _(across):
        out_copy(across).wait()

    rest = pl.ds(0, owners - 1)
    for i, (src, dst) in enumerate(((sendf_ref, recvf_ref), (sendm_ref, recvm_ref))):
        pltpu.make_async_copy(src.at[rest], dst.at[rest], route_sem.at[i]).wait()
    for copies in (halo_back, halo_obs, halo_norm, halo_corner):
        halo_sent(copies)


def body(
    obs_feat, obs_dest, obs_cell, obs_sub, background, w_in, dens_vec,
    conv_w, conv_b, norm_gain, w_qkv, rel_bias, w_out,
):
    owners = lax.axis_size("lat") * lax.axis_size("lon")
    rows, cols, channels = background.shape
    obs, width = obs_feat.shape
    half, out_rows, both = cols // 2, rows // 2, 2 * width
    vmem = pl.BlockSpec(memory_space=pltpu.VMEM)
    hbm = pl.BlockSpec(memory_space=pl.ANY)
    scratch = [
        ((obs, width), BF16),
        ((width, channels), BF16),
        ((out_rows, half, channels), BF16),
        ((rows, cols, channels), BF16),
        ((4, 4 * channels, channels), BF16),
        ((channels, 3 * channels), BF16),
        ((channels, channels), BF16),
        ((owners, 32, width), BF16),
        ((owners, 1, 128), I32),
        ((owners, 32, width), BF16),
        ((owners, 1, 128), I32),
        ((512, obs), BF16),
        ((obs, width), BF16),
        ((1, obs), I32),
        ((2, rows, channels), F32),
        ((2, cols, channels), BF16),
        ((2, rows + 16, channels), F32),
        ((2 * channels // 128, cols + 16, 128), F32),
        ((rows + 2, half, 4 * channels), BF16),
        ((half * out_rows, channels), F32),
        ((4, 4 * both, channels), BF16),
        ((1, owners * 8), I32),
        ((owners * 8, rows // 4 * width + 128), BF16),
        ((512, rows // 4 * width + 128), F32),
        ((2, rows, both), F32),
        ((2 * both // 128, cols + 16, 128), F32),
        ((4, cols, both), BF16),
        ((2, rows + 16, both), F32),
        ((rows + 2, half, 4 * both), BF16),
        ((out_rows, half, channels), BF16),
        ((out_rows, half, channels), BF16),
        ((2, 6, half, channels), BF16),
        ((2, out_rows // 2 + 6, 16, channels), BF16),
        ((2, out_rows // 2, 16, channels), BF16),
        ((out_rows, half, channels), BF16),
        ((out_rows, half + 16, channels), BF16),
        ((out_rows // 4, 384, HEADS * 64), F32),
        ((out_rows // 4, 256, HEADS * 64), F32),
        ((2, 6, half + 16, channels), BF16),
        ((channels, channels), BF16),
        ((out_rows * half // 64, channels, 128), F32),
        ((out_rows * half // 64, 8, channels), F32),
        ((HEADS, 640), F32),
    ]
    sems = [pltpu.SemaphoreType.DMA((n,)) for n in (6, 2, 8, 2, half // 16, 38, 38)]
    sems.append(pltpu.SemaphoreType.REGULAR)
    return pl.pallas_call(
        main_kernel,
        name="main",
        out_shape=jax.ShapeDtypeStruct((out_rows, half, channels), BF16),
        in_specs=[vmem, vmem, vmem, hbm, hbm, hbm, vmem, hbm, vmem, vmem, hbm, vmem, hbm],
        out_specs=hbm,
        scratch_shapes=[pltpu.VMEM(shape, dtype) for shape, dtype in scratch] + sems,
        compiler_params=pltpu.CompilerParams(
            collective_id=0, has_side_effects=True, vmem_limit_bytes=62 << 20
        ),
    )(
        obs_dest.reshape(1, obs),
        obs_cell.reshape(1, obs),
        obs_sub.reshape(1, obs),
        obs_feat,
        background,
        w_in,
        dens_vec.reshape(1, channels),
        conv_w.reshape(4, 4 * channels, channels),
        conv_b.reshape(1, channels),
        norm_gain.reshape(1, channels),
        w_qkv,
        jnp.transpose(rel_bias, (1, 0, 2)),
        w_out,
    )


def solution(mesh):
    split = P(("lat", "lon"))
    wide = P(("lat", "lon"), None)
    tile = P("lat", "lon", None)
    in_specs = (wide, wide, split, split, tile) + (P(),) * 8
    return jax.shard_map(body, mesh=mesh, in_specs=in_specs, out_specs=tile, check_vma=False)
```
